32 devices in a mesh: dp: 8 (over z, x), seq: 4 (over y, core).
Axes of the slice: x: 2, y: 2, z: 4, core: 2. Of those that a mesh axis runs over, the one named last changes fastest.
Arguments:
- tokens: bfloat16 [4, 32, 256, 512], P(None, 'dp', 'seq'), may hold values from -6 to 6
- cotangent: bfloat16 [4, 32, 256, 512], P(None, 'dp', 'seq'), may hold values from -6 to 6
- lengths: int32 [4, 32], P(None, 'dp'), may hold values from 64 to 250, as said below
- attn_w: float32 [512, 2048], P('dp'), may hold values from -1.06066017 to 1.06066017
- attn_m: float32 [512, 2048], P('dp'), may hold values from -0.0009765625 to 0.0009765625
- attn_v: float32 [512, 2048], P('dp'), may hold values from 1.5868744e-10 to 2.538999e-09
- mlp_w: float32 [2, 512, 2048], P(None, 'dp'), may hold values from -0.25 to 0.25
- mlp_m: float32 [2, 512, 2048], P(None, 'dp'), may hold values from -0.0009765625 to 0.0009765625
- mlp_v: float32 [2, 512, 2048], P(None, 'dp'), may hold values from 1.5868744e-10 to 2.538999e-09
- vec_w: float32 [10, 512], P(None, 'dp'), may hold values from -1 to 3.2
- vec_m: float32 [10, 512], P(None, 'dp'), may hold values from -0.0009765625 to 0.0009765625
- vec_v: float32 [10, 512], P(None, 'dp'), may hold values from 1.5868744e-10 to 2.538999e-09
Outputs:
- output: bfloat16 [4, 32, 256, 512], P(None, 'dp', 'seq')
- input_grad: bfloat16 [4, 32, 256, 512], P(None, 'dp', 'seq')
- attn_w_new: float32 [512, 2048], P('dp')
- attn_m_new: float32 [512, 2048], P('dp')
- attn_v_new: float32 [512, 2048], P('dp')
- mlp_w_new: float32 [2, 512, 2048], P(None, 'dp')
- mlp_m_new: float32 [2, 512, 2048], P(None, 'dp')
- mlp_v_new: float32 [2, 512, 2048], P(None, 'dp')
- vec_w_new: float32 [10, 512], P(None, 'dp')
- vec_m_new: float32 [10, 512], P(None, 'dp')
- vec_v_new: float32 [10, 512], P(None, 'dp')
- grad_norm: float32 [], replicated
The draws below stay inside these ranges and needn't reach their ends.
Inputs may be any that keep to these rules, and one draw needn't show every extreme that they name: `lengths`: each length is 64, 128 or 250; among the 4 rows of one index of dp in each micro-batch at least one has 250.
All inputs are finite; a program needn't handle non-finite values.
Results may differ from the reference program's by a relative error of at most 0.018.
The reference program's roundings to bfloat16 on the way count: a program that leaves them out, or rounds other values in their place, can miss the bound.
Values may be sent and summed in bfloat16 or wider, within the bound.
No kernel may reach another device: no remote copies, remote signals or barrier semaphores. Data moves between devices by JAX's collectives and lax.ppermute only.
A program may use at most 128 MiB of HBM per device.

```python
import math
import jax
import jax.numpy as jnp
from jax import lax

D = 512
HEADS = 8
FF = 2048
SLOTS = 256
LONGEST = 250
MB = 4
ROWS = 4
ADAM_STEP = 10
ROWS_ALL = 32
VROWS = 10
PARAMS = 3150848


def draw_lengths(key, part):
    key = jax.random.fold_in(key, 11)
    pick_key, long_key = jax.random.split(key)
    picks = jax.random.randint(pick_key, (MB, ROWS_ALL), 0, 3)
    base = jnp.where(picks == 0, SLOTS // 4, jnp.where(picks == 1, SLOTS // 2, LONGEST)).astype(jnp.int32)
    forced = jax.random.randint(long_key, (MB, ROWS_ALL // ROWS), 0, ROWS)
    place = jnp.arange(ROWS_ALL, dtype=jnp.int32) % ROWS
    chosen = place[None, :] == jnp.repeat(forced, ROWS, axis=1)
    return jnp.where(chosen, LONGEST, base).astype(jnp.int32)


def draw_attn_w(key, part):
    key = jax.random.fold_in(key, 12)
    base = jnp.clip(jax.random.normal(key, (D, 4 * D), jnp.float32), -6.0, 6.0)
    column = jnp.arange(4 * D)
    column_scale = jnp.where(column < 3 * D, 1.0, 4.0) / math.sqrt(D)
    return (base * column_scale[None, :]).astype(jnp.float32)


def draw_vec_w(key, part):
    key = jax.random.fold_in(key, 13)
    rough_key, shift_key = jax.random.split(key)
    place = jnp.arange(D, dtype=jnp.float32) / (D - 1)
    rise = 0.5 * 3.0 ** place
    shifts = jnp.clip(0.3 * jax.random.normal(shift_key, (VROWS - 2, D), jnp.float32), -1.0, 1.0)
    rough = jax.random.uniform(rough_key, (2, D), jnp.float32, 0.8, 1.25)
    gains = rise[None, :] * rough
    return jnp.concatenate([gains[0:1], shifts[0:1], gains[1:2], shifts[1:]], axis=0).astype(jnp.float32)


def level_of(rng, extent, cuts, low, high):
    loudness = 1.0
    for dim, parts in cuts:
        steps = jax.random.uniform(jax.random.fold_in(jax.random.fold_in(rng, 6), dim), (parts,), jnp.float32, low / len(cuts), high / len(cuts))
        loudness = loudness * jnp.repeat(jnp.exp(steps), extent[dim] // parts).reshape((-1,) + (1,) * (len(extent) - 1 - dim))
    return loudness


def scatter_about(rng, shape, width, limit, cuts=(), kind=jnp.bfloat16):
    values = jax.random.normal(rng, shape, jnp.float32) * width
    if len(cuts) > 0:
        values = level_of(rng, shape, cuts, -0.22, 0.18) * values
    return jnp.clip(values, min=-limit, max=limit).astype(kind)


def setup_inputs(seed: int = 0) -> dict:
    key_of = jax.random.split(jax.random.key(seed), 13)
    tokens = scatter_about(key_of[0], (MB, ROWS_ALL, SLOTS, D), 1.0, 6.0, ((1, 8), (2, 4)))
    cotangent = scatter_about(key_of[1], (MB, ROWS_ALL, SLOTS, D), 1.0, 6.0, ((1, 8), (2, 4)))
    lengths = draw_lengths(jax.random.fold_in(key_of[12], 71), 0)
    attn_w = draw_attn_w(jax.random.fold_in(key_of[12], 71), 0)
    attn_m = scatter_about(key_of[4], (D, 4 * D), (0.11 / PARAMS ** 0.5), 0.0009765625, ((0, 8),), jnp.float32)
    attn_v = jnp.clip(jnp.exp(math.log(2.5389990110369354e-09) - 2.7725887 * jax.random.uniform(key_of[5], (D, 4 * D), jnp.float32) ** level_of(key_of[5], (D, 4 * D), ((0, 8),), -0.2, 0.2)), 1.5868743818980846e-10, 2.5389990110369354e-09)
    mlp_w = scatter_about(key_of[6], (2, D, FF), D ** -0.5, 0.25, ((1, 8),), jnp.float32)
    mlp_m = scatter_about(key_of[7], (2, D, FF), (0.11 / PARAMS ** 0.5), 0.0009765625, ((1, 8),), jnp.float32)
    mlp_v = jnp.clip(jnp.exp(math.log(2.5389990110369354e-09) - 2.7725887 * jax.random.uniform(key_of[8], (2, D, FF), jnp.float32) ** level_of(key_of[8], (2, D, FF), ((1, 8),), -0.2, 0.2)), 1.5868743818980846e-10, 2.5389990110369354e-09)
    vec_w = draw_vec_w(jax.random.fold_in(key_of[12], 71), 0)
    vec_m = scatter_about(key_of[10], (VROWS, D), (0.11 / PARAMS ** 0.5), 0.0009765625, ((1, 8),), jnp.float32)
    vec_v = jnp.clip(jnp.exp(math.log(2.5389990110369354e-09) - 2.7725887 * jax.random.uniform(key_of[11], (VROWS, D), jnp.float32) ** level_of(key_of[11], (VROWS, D), ((1, 8),), -0.2, 0.2)), 1.5868743818980846e-10, 2.5389990110369354e-09)
    return {"tokens": tokens, "cotangent": cotangent, "lengths": lengths, "attn_w": attn_w, "attn_m": attn_m, "attn_v": attn_v, "mlp_w": mlp_w, "mlp_m": mlp_m, "mlp_v": mlp_v, "vec_w": vec_w, "vec_m": vec_m, "vec_v": vec_v}


@jax.custom_vjp
def low(v):
    return lax.optimization_barrier(v.astype(jnp.bfloat16)).astype(jnp.float32)

@jax.custom_vjp
def low_back(v):
    return v

def low_keep(v):
    return (low(v), None)

def low_pass(kept, grad):
    return (grad,)

def back_keep(v):
    return (v, None)

def back_low(kept, grad):
    return (low(grad),)
low.defvjp(low_keep, low_pass)
low_back.defvjp(back_keep, back_low)
CLIP_NORM = 1.0
BETA_ONE = 0.9
BETA_TWO = 0.999
LEARN_RATE = 0.08
VEC_RATE = 0.4
WEIGHT_DECAY = 0.01
ADAM_EPS = 1e-08
NORM_EPS = 1e-05

def layer_norm(values, gain, shift):
    center = values - lax.optimization_barrier(jnp.mean(values, axis=-1, keepdims=True))
    spread = lax.optimization_barrier(jnp.mean(center * center, axis=-1, keepdims=True))
    return center * lax.rsqrt(spread + NORM_EPS) * gain + shift

def matmul_high(form, left, right):
    return jnp.einsum(form, left, right, precision=lax.Precision.HIGHEST)

def forward(x_float, attn_now, mlp_now, vec_now, length_piece):
    attn_low = low(attn_now)
    mlp_low = low(mlp_now)
    vec_low = low(vec_now)
    row_count, slot_count, model_width = x_float.shape
    head_size = model_width // HEADS
    w_qkv = attn_low[:, :3 * model_width]
    w_out = attn_low[:, 3 * model_width:]
    h_one = low(layer_norm(x_float, vec_low[0], vec_low[1]))
    qkv = low(low_back(matmul_high('rpd,de->rpe', h_one, w_qkv)))
    qkv = qkv.reshape(row_count, slot_count, 3, HEADS, head_size)
    queries = qkv[:, :, 0]
    keys_h = qkv[:, :, 1]
    values_h = qkv[:, :, 2]
    scores = low_back(matmul_high('rqhc,rkhc->rhqk', queries, keys_h) * (1.0 / math.sqrt(head_size)))
    valid = jnp.arange(slot_count)[None, :] < length_piece[:, None]
    scores = jnp.where(valid[:, None, None, :], scores, -1e+30)
    probs = low(jax.nn.softmax(scores, axis=-1))
    attended = matmul_high('rhqk,rkhc->rqhc', probs, values_h).reshape(row_count, slot_count, model_width)
    attended = low(low_back(attended))
    x_one = x_float + low_back(matmul_high('rpd,de->rpe', attended, w_out) + vec_low[4])
    h_two = low(layer_norm(x_one, vec_low[2], vec_low[3]))
    up_pre = low_back(matmul_high('rpd,df->rpf', h_two, mlp_low[0]) + vec_low[6:].reshape(-1))
    act = low(jax.nn.gelu(up_pre, approximate=False))
    return x_one + low_back(matmul_high('rpf,df->rpd', act, mlp_low[1]) + vec_low[5])

def adam_update(weight, moment, second, grad, decay, rate):
    moment_new = BETA_ONE * moment + (1.0 - BETA_ONE) * grad
    second_new = BETA_TWO * second + (1.0 - BETA_TWO) * grad * grad
    first_hat = moment_new / (1.0 - BETA_ONE ** ADAM_STEP)
    second_hat = second_new / (1.0 - BETA_TWO ** ADAM_STEP)
    weight_new = weight - rate * (first_hat / (jnp.sqrt(second_hat) + ADAM_EPS) + decay * weight)
    return (weight_new, moment_new, second_new)

def reference(tokens, cotangent, lengths, attn_w, attn_m, attn_v, mlp_w, mlp_m, mlp_v, vec_w, vec_m, vec_v):
    model_width = tokens.shape[-1]
    slot_count = tokens.shape[2]
    group_rows = 16
    token_groups = tokens.reshape(-1, group_rows, slot_count, model_width)
    cot_groups = cotangent.reshape(-1, group_rows, slot_count, model_width)
    length_groups = lengths.reshape(-1, group_rows)

    def advance(totals, pieces):
        token_piece, cot_piece, length_piece = pieces

        def layer_of(x_float, attn_now, mlp_now, vec_now):
            return forward(x_float, attn_now, mlp_now, vec_now, length_piece)
        result, pullback = jax.vjp(layer_of, token_piece.astype(jnp.float32), attn_w, mlp_w, vec_w)
        grad_x, grad_attn, grad_mlp, grad_vec = pullback(cot_piece.astype(jnp.float32))
        totals = (totals[0] + grad_attn, totals[1] + grad_mlp, totals[2] + grad_vec)
        return (totals, (result.astype(jnp.bfloat16), grad_x.astype(jnp.bfloat16)))
    start_totals = (jnp.zeros_like(attn_w), jnp.zeros_like(mlp_w), jnp.zeros_like(vec_w))
    sums, (results, grads_x) = lax.scan(advance, start_totals, (token_groups, cot_groups, length_groups))
    attn_grad, mlp_grad, vec_grad = sums
    square_total = jnp.sum(attn_grad * attn_grad) + jnp.sum(mlp_grad * mlp_grad) + jnp.sum(vec_grad * vec_grad)
    grad_norm = jnp.sqrt(square_total)
    clip_factor = CLIP_NORM / jnp.maximum(grad_norm, CLIP_NORM)
    attn_new = adam_update(attn_w, attn_m, attn_v, attn_grad * clip_factor, WEIGHT_DECAY, LEARN_RATE)
    mlp_new = adam_update(mlp_w, mlp_m, mlp_v, mlp_grad * clip_factor, WEIGHT_DECAY, LEARN_RATE)
    vec_new = adam_update(vec_w, vec_m, vec_v, vec_grad * clip_factor, 0.0, VEC_RATE)
    return (results.reshape(tokens.shape), grads_x.reshape(tokens.shape), attn_new[0], attn_new[1], attn_new[2], mlp_new[0], mlp_new[1], mlp_new[2], vec_new[0], vec_new[1], vec_new[2], grad_norm)
```

```python
import math

import jax
import jax.numpy as jnp
from jax import lax
from jax.sharding import PartitionSpec as P

HEADS = 8
ADAM_STEP = 10


CLIP_NORM = 1.0
BETA_ONE = 0.9
BETA_TWO = 0.999
LEARN_RATE = 0.08
VEC_RATE = 0.4
WEIGHT_DECAY = 0.01
ADAM_EPS = 1e-08
NORM_EPS = 1e-05


def layer_norm(values, gain, shift):
    center = values - jnp.mean(values, axis=-1, keepdims=True)
    spread = jnp.mean(center * center, axis=-1, keepdims=True)
    return center * lax.rsqrt(spread + NORM_EPS) * gain + shift


def exact_gelu(values):
    return jax.nn.gelu(values, approximate=False)


def adam_update(weight, moment, second, grad, decay, rate):
    moment_new = BETA_ONE * moment + (1.0 - BETA_ONE) * grad
    second_new = BETA_TWO * second + (1.0 - BETA_TWO) * grad * grad
    first_hat = moment_new / (1.0 - BETA_ONE**ADAM_STEP)
    second_hat = second_new / (1.0 - BETA_TWO**ADAM_STEP)
    weight_new = weight - rate * (first_hat / (jnp.sqrt(second_hat) + ADAM_EPS) + decay * weight)
    return (weight_new, moment_new, second_new)


def same_value(value):
    return value


def layer_pass(
    slot_ids, x_float, grad_y_low, row_lengths, params, spread_qkv, gather_attn, spread_grad, gather_grad
):
    (
        w_qkv,
        w_out,
        w_up,
        w_down,
        gain_one,
        shift_one,
        gain_two,
        shift_two,
        bias_out,
        bias_down,
        bias_up,
    ) = params
    row_count, part_slots, model_width = x_float.shape
    head_size = model_width // HEADS
    score_scale = 1.0 / math.sqrt(head_size)
    h_one_f, norm_one_pull = jax.vjp(layer_norm, x_float, gain_one, shift_one)
    h_one = h_one_f.astype(jnp.bfloat16)
    qkv_local = jnp.einsum("rpd,de->rpe", h_one, w_qkv, preferred_element_type=jnp.float32).astype(
        jnp.bfloat16
    )
    qkv_local = qkv_local.reshape(row_count, part_slots, 3, model_width)
    qkv_heads = spread_qkv(qkv_local)
    slot_count = qkv_heads.shape[1]
    local_width = qkv_heads.shape[3]
    heads_dev = local_width // head_size
    queries = qkv_heads[:, :, 0].reshape(row_count, slot_count, heads_dev, head_size)
    keys_h = qkv_heads[:, :, 1].reshape(row_count, slot_count, heads_dev, head_size)
    values_h = qkv_heads[:, :, 2].reshape(row_count, slot_count, heads_dev, head_size)
    valid = slot_ids[None, :] < row_lengths[:, None]
    key_mask = valid[:, None, None, :]
    scores = (
        jnp.einsum("rqhc,rkhc->rhqk", queries, keys_h, preferred_element_type=jnp.float32)
        * score_scale
    )
    scores = jnp.where(key_mask, scores, -1e30)
    row_max = jnp.max(scores, axis=-1, keepdims=True)
    shifted = jnp.exp(scores - row_max)
    log_total = row_max + jnp.log(jnp.sum(shifted, axis=-1, keepdims=True))
    probs_low = jnp.exp(scores - log_total).astype(jnp.bfloat16)
    attended = jnp.einsum(
        "rhqk,rkhc->rqhc", probs_low, values_h, preferred_element_type=jnp.float32
    )
    attended = attended.astype(jnp.bfloat16).reshape(row_count, slot_count, local_width)
    features = gather_attn(attended)
    x_one = (
        x_float
        + jnp.einsum("rpd,de->rpe", features, w_out, preferred_element_type=jnp.float32)
        + bias_out
    )
    h_two_f, norm_two_pull = jax.vjp(layer_norm, x_one, gain_two, shift_two)
    h_two = h_two_f.astype(jnp.bfloat16)
    up_pre = jnp.einsum("rpd,df->rpf", h_two, w_up, preferred_element_type=jnp.float32) + bias_up
    act_f, gelu_pull = jax.vjp(exact_gelu, up_pre)
    act = act_f.astype(jnp.bfloat16)
    result = (
        x_one
        + jnp.einsum("rpf,df->rpd", act, w_down, preferred_element_type=jnp.float32)
        + bias_down
    )
    grad_y = grad_y_low.astype(jnp.float32)
    grad_wdown = jnp.einsum("rpd,rpf->df", grad_y_low, act, preferred_element_type=jnp.float32)
    bdown_term = jnp.sum(grad_y, axis=(0, 1))
    grad_act = jnp.einsum("rpd,df->rpf", grad_y_low, w_down, preferred_element_type=jnp.float32)
    grad_up_pre = gelu_pull(grad_act)[0].astype(jnp.bfloat16)
    grad_wup = jnp.einsum("rpd,rpf->df", h_two, grad_up_pre, preferred_element_type=jnp.float32)
    grad_bup = jnp.sum(grad_up_pre.astype(jnp.float32), axis=(0, 1))
    grad_h_two = jnp.einsum("rpf,df->rpd", grad_up_pre, w_up, preferred_element_type=jnp.float32)
    grad_x_one, grad_g_two, grad_s_two = norm_two_pull(grad_h_two)
    grad_x_one = grad_x_one + grad_y
    grad_attn_out = grad_x_one.astype(jnp.bfloat16)
    grad_wout = jnp.einsum(
        "rpd,rpe->de", features, grad_attn_out, preferred_element_type=jnp.float32
    )
    bout_term = jnp.sum(grad_attn_out.astype(jnp.float32), axis=(0, 1))
    grad_feat = jnp.einsum(
        "rpe,de->rpd", grad_attn_out, w_out, preferred_element_type=jnp.float32
    ).astype(jnp.bfloat16)
    grad_heads = spread_grad(grad_feat)
    grad_heads = grad_heads.reshape(row_count, slot_count, heads_dev, head_size)
    again_scores = (
        jnp.einsum("rqhc,rkhc->rhqk", queries, keys_h, preferred_element_type=jnp.float32)
        * score_scale
    )
    again_scores = jnp.where(key_mask, again_scores, -1e30)
    probs_again = jnp.exp(again_scores - log_total)
    grad_probs = jnp.einsum(
        "rqhc,rkhc->rhqk", grad_heads, values_h, preferred_element_type=jnp.float32
    )
    inner = jnp.sum(probs_again * grad_probs, axis=-1, keepdims=True)
    grad_scores = (probs_again * (grad_probs - inner)).astype(jnp.bfloat16)
    grad_queries = (
        jnp.einsum("rhqk,rkhc->rqhc", grad_scores, keys_h, preferred_element_type=jnp.float32)
        * score_scale
    )
    grad_keys = (
        jnp.einsum("rhqk,rqhc->rkhc", grad_scores, queries, preferred_element_type=jnp.float32)
        * score_scale
    )
    grad_values = jnp.einsum(
        "rhqk,rqhc->rkhc",
        probs_again.astype(jnp.bfloat16),
        grad_heads,
        preferred_element_type=jnp.float32,
    )
    grad_qkv_heads = jnp.stack([grad_queries, grad_keys, grad_values], axis=2)
    grad_qkv_heads = grad_qkv_heads.reshape(row_count, slot_count, 3, local_width).astype(
        jnp.bfloat16
    )
    grad_qkv_local = gather_grad(grad_qkv_heads)
    grad_qkv_local = grad_qkv_local.reshape(row_count, part_slots, 3 * model_width)
    grad_wqkv = jnp.einsum("rpd,rpe->de", h_one, grad_qkv_local, preferred_element_type=jnp.float32)
    grad_h_one = jnp.einsum(
        "rpe,de->rpd", grad_qkv_local, w_qkv, preferred_element_type=jnp.float32
    )
    grad_x_ln, grad_g_one, grad_s_one = norm_one_pull(grad_h_one)
    input_piece = (grad_x_ln + grad_x_one).astype(jnp.bfloat16)
    small_terms = jnp.stack([grad_g_one, grad_s_one, grad_g_two, grad_s_two, bout_term, bdown_term])
    return (
        result.astype(jnp.bfloat16),
        input_piece,
        (grad_wqkv, grad_wout, grad_wup, grad_wdown, small_terms, grad_bup),
    )


def swap(value, axis):
    return lax.ppermute(value, axis, [(0, 1), (1, 0)])


def ordered(own, other, index, axis):
    first = jnp.where(index == 0, own, other)
    second = jnp.where(index == 0, other, own)
    return jnp.stack([first, second], axis)


def from_seq(pieces, axes):
    perm = [(j, j) for j in range(4)]
    out = []
    for k in range(4):
        if k == 0:
            out.append(pieces[0])
        else:
            out.append(lax.ppermute(pieces[k], axes, [(j, j ^ k) for j in range(4)]))
    return out


def gather_rows(shard, lo, core):
    hi_count = lax.axis_size("hi")
    rows, cols = shard.shape
    half = lax.dynamic_slice_in_dim(shard, core * (rows // 2), rows // 2, 0)
    spread = jnp.broadcast_to(half[None], (hi_count, rows // 2, cols))
    own = lax.all_to_all(spread, "hi", 0, 0)
    other = swap(own, "lo")
    own_far = swap(own, "core")
    other_far = swap(other, "core")
    near = ordered(own, other, lo, 1)
    far = ordered(own_far, other_far, lo, 1)
    whole = ordered(near, far, core, 2)
    return whole.reshape(hi_count * 2 * rows, cols)


def reduce_rows(total, y, core):
    hi_count = lax.axis_size("hi")
    width, cols = total.shape
    rows = width // (2 * hi_count)
    half = cols // 2
    quarter = half // 2
    keep = lax.dynamic_slice_in_dim(total, core * half, half, 1)
    send = lax.dynamic_slice_in_dim(total, (1 - core) * half, half, 1)
    got = swap(send.astype(jnp.bfloat16), "core")
    part = (keep + got.astype(jnp.float32)).astype(jnp.bfloat16)
    part = part.reshape(hi_count, 2, rows, 2, quarter).transpose(1, 3, 0, 2, 4)
    part = part.reshape(4, hi_count, rows, quarter)
    part = lax.all_to_all(part, ("lo", "y"), 0, 0)
    part = jnp.sum(part.astype(jnp.float32), axis=0).astype(jnp.bfloat16)
    part = lax.all_to_all(part, "hi", 0, 0)
    part = jnp.sum(part.astype(jnp.float32), axis=0).astype(jnp.bfloat16)
    other = swap(part, "y")
    mine = ordered(part, other, y, 1).reshape(rows, half)
    far = swap(mine, "core")
    whole = ordered(mine, far, core, 1).reshape(rows, cols)
    return whole.astype(jnp.float32)


def on_device(
    tokens, cotangent, lengths, attn_w, attn_m, attn_v, mlp_w, mlp_m, mlp_v, vec_w, vec_m, vec_v
):
    lo = lax.axis_index("lo")
    y = lax.axis_index("y")
    core = lax.axis_index("core")
    me = y * 2 + core
    seq_axes = ("y", "core")
    model_width = tokens.shape[-1]
    vec_low = vec_w.astype(jnp.bfloat16)
    attn_low = attn_w.astype(jnp.bfloat16)
    mlp_low = mlp_w.astype(jnp.bfloat16)
    micro_count, row_count, part_slots, _ = tokens.shape
    flat_count = micro_count * row_count
    seq_count = 4
    per_device = flat_count // seq_count
    flat_tokens = tokens.reshape(seq_count, per_device, part_slots, model_width)
    flat_cot = cotangent.reshape(seq_count, per_device, part_slots, model_width)

    def pick(stack, k):
        return lax.dynamic_index_in_dim(stack, me ^ k, 0, keepdims=False)

    moved_tokens = from_seq([pick(flat_tokens, k) for k in range(4)], seq_axes)
    w_qkv = gather_rows(attn_low[:, : 3 * model_width], lo, core)
    vec_all = lax.all_gather(vec_low, ("hi", "lo"), axis=1, tiled=True)
    w_out = gather_rows(attn_low[:, 3 * model_width :], lo, core)
    moved_cot = from_seq([pick(flat_cot, k) for k in range(4)], seq_axes)
    w_up = gather_rows(mlp_low[0], lo, core)
    w_down = gather_rows(mlp_low[1], lo, core)
    vec_float = vec_all.astype(jnp.float32)
    params = (
        w_qkv,
        w_out,
        w_up,
        w_down,
        vec_float[0],
        vec_float[1],
        vec_float[2],
        vec_float[3],
        vec_float[4],
        vec_float[5],
        vec_float[6:].reshape(-1),
    )
    row_lengths = lax.dynamic_slice_in_dim(lengths.reshape(-1), me * per_device, per_device)
    slot_ids = jnp.concatenate(
        [(me ^ k) * part_slots + jnp.arange(part_slots, dtype=jnp.int32) for k in range(4)]
    )
    x_float = jnp.concatenate(moved_tokens, axis=1).astype(jnp.float32)
    result, input_piece, totals = layer_pass(
        slot_ids,
        x_float,
        jnp.concatenate(moved_cot, axis=1),
        row_lengths,
        params,
        same_value,
        same_value,
        same_value,
        same_value,
    )

    def send_back(value):
        parts = [value[:, k * part_slots : (k + 1) * part_slots] for k in range(4)]
        parts = from_seq(parts, seq_axes)
        pairs = [ordered(parts[0], parts[1], core, 0), ordered(parts[2], parts[3], core, 0)]
        return ordered(pairs[0], pairs[1], y, 0).reshape(tokens.shape)

    output = send_back(result)
    input_grad = send_back(input_piece)
    grad_wqkv, grad_wout, grad_wup, grad_wdown, grad_small, grad_bup = totals
    vec_total = jnp.concatenate([grad_small, grad_bup.reshape(-1, model_width)], axis=0)
    vec_rows = vec_total.shape[0]
    vec_cols = vec_w.shape[1]
    down_sum = reduce_rows(grad_wdown, y, core)
    up_sum = reduce_rows(grad_wup, y, core)
    attn_sum = reduce_rows(jnp.concatenate([grad_wqkv, grad_wout], axis=1), y, core)
    vec_flat = jnp.pad(vec_total.reshape(vec_rows, -1, vec_cols).transpose(1, 0, 2), ((0, 0), (0, 6), (0, 0)))
    vec_sum = reduce_rows(vec_flat.reshape(-1, vec_cols * 2), y, core)
    vec_sum = vec_sum.reshape(16, vec_cols)[:vec_rows]
    square = jnp.sum(attn_sum * attn_sum) + jnp.sum(up_sum * up_sum)
    square = square + jnp.sum(down_sum * down_sum) + jnp.sum(vec_sum * vec_sum)
    dp_count = lax.axis_size(("hi", "lo"))
    squares = lax.all_to_all(jnp.full((dp_count, 8, 128), square), ("hi", "lo"), 0, 0)
    grad_norm = jnp.sqrt(jnp.sum(squares[:, 0, 0]))
    clip_factor = CLIP_NORM / jnp.maximum(grad_norm, CLIP_NORM)
    mlp_sum = jnp.stack([up_sum, down_sum])
    attn_new = adam_update(
        attn_w, attn_m, attn_v, attn_sum * clip_factor, WEIGHT_DECAY, LEARN_RATE
    )
    mlp_new = adam_update(mlp_w, mlp_m, mlp_v, mlp_sum * clip_factor, WEIGHT_DECAY, LEARN_RATE)
    vec_new = adam_update(vec_w, vec_m, vec_v, vec_sum * clip_factor, 0.0, VEC_RATE)
    return (output, input_grad, *attn_new, *mlp_new, *vec_new, grad_norm)


def solution(mesh):
    dp_count = mesh.shape["dp"]
    seq_count = mesh.shape["seq"]
    fine = jax.sharding.Mesh(
        mesh.devices.reshape(dp_count // 2, 2, seq_count // 2, 2), ("hi", "lo", "y", "core")
    )
    dp = ("hi", "lo")
    seq = ("y", "core")
    acts = P(None, dp, seq, None)
    attn = P(dp, None)
    mlp = P(None, dp, None)
    vec = P(None, dp)
    return jax.shard_map(
        on_device,
        mesh=fine,
        in_specs=(acts, acts, P(None, dp), attn, attn, attn, mlp, mlp, mlp, vec, vec, vec),
        out_specs=(acts, acts, attn, attn, attn, mlp, mlp, mlp, vec, vec, vec, P()),
        check_vma=False,
    )
```

```python
import functools
import math

import jax
import jax.numpy as jnp
from jax import lax
from jax.experimental import pallas as pl
from jax.experimental.pallas import tpu as pltpu
from jax.sharding import PartitionSpec as P

HEADS = 8
ADAM_STEP = 10
CLIP_NORM = 1.0
BETA_ONE = 0.9
BETA_TWO = 0.999
LEARN_RATE = 0.08
VEC_RATE = 0.4
WEIGHT_DECAY = 0.01
ADAM_EPS = 1e-08
NORM_EPS = 1e-05
VMEM_BYTES = 60 * 1024 * 1024

TAIL_SCALE = 0.4 / math.sqrt(2.0)
TAIL = (
    0.2256758631446491,
    0.22566953041000726,
    0.2078437638365498,
    0.16853459369628254,
    0.1414582080030511,
    -0.005661972621845868,
    0.1691478544806666,
    -0.18293913558029784,
    0.05027141967490775,
)
F32 = jnp.float32
BF16 = jnp.bfloat16
ANY = pl.BlockSpec(memory_space=pl.ANY)
SMEM = pl.BlockSpec(memory_space=pltpu.SMEM)


def nt_dot(left, right):
    return lax.dot_general(left, right, (((1,), (1,)), ((), ())), preferred_element_type=F32)


def nn_dot(left, right):
    return jnp.dot(left, right, preferred_element_type=F32)


def centered(values):
    center = values - jnp.mean(values, axis=-1, keepdims=True)
    spread = jnp.mean(center * center, axis=-1, keepdims=True)
    scale = lax.rsqrt(spread + NORM_EPS)
    return center * scale, scale


def norm_back(unit, scale, grad):
    mean_grad = jnp.mean(grad, axis=-1, keepdims=True)
    mean_both = jnp.mean(grad * unit, axis=-1, keepdims=True)
    return scale * (grad - mean_grad - unit * mean_both)


def gelu_and_slope(up):
    size = jnp.abs(up)
    t = 1.0 / (1.0 + TAIL_SCALE * size)
    poly = jnp.full_like(t, TAIL[-1])
    for coef in TAIL[-2::-1]:
        poly = poly * t + coef
    bell = jnp.exp(-0.5 * up * up)
    tail = 0.5 * (t * poly) * bell
    share = jnp.where(up >= 0, 1.0 - tail, tail)
    return up * share, share + up * (bell * (1.0 / math.sqrt(2.0 * math.pi)))


def placements(pieces, jobs, place, sems):
    lo = place[0]
    core = place[1]
    copies = []
    for i, piece in enumerate(pieces):
        lo_at = lo if i % 2 == 0 else 1 - lo
        core_at = core if i < 2 else 1 - core
        hi_count, rows, _ = piece.shape
        for h in range(hi_count):
            row = pl.multiple_of(((h * 2 + lo_at) * 2 + core_at) * rows, rows)
            for column, width, target in jobs:
                copies.append(
                    pltpu.make_async_copy(
                        piece.at[h, :, pl.ds(column, width)],
                        target.at[pl.ds(row, rows), :],
                        sems.at[len(copies)],
                    )
                )
    return copies


def dp_placements(pieces, target, place, sems):
    copies = []
    for i, piece in enumerate(pieces):
        core_at = place[1] if i == 0 else 1 - place[1]
        dp_count, rows, _ = piece.shape
        for d in range(dp_count):
            row = pl.multiple_of((d * 2 + core_at) * rows, rows)
            copies.append(
                pltpu.make_async_copy(
                    piece.at[d], target.at[pl.ds(row, rows), :], sems.at[len(copies)]
                )
            )
    return copies


def head_masks(width):
    lane = lax.broadcasted_iota(jnp.int32, (1, width), 1)
    first = jnp.where(lane < width // 2, 1.0, 0.0)
    return first.astype(BF16), (1.0 - first).astype(BF16)


def fill_bias(place, lengths, row, bias):
    part = bias.shape[0] // 4
    for k in range(4):
        base = (place[2] ^ k) * part
        slot = lax.broadcasted_iota(jnp.int32, (part, bias.shape[1]), 0) + base
        bias[k * part : (k + 1) * part, :] = jnp.where(slot < lengths[row], 0.0, -1e30)


def qkv_body(place, x0, x1, x2, x3, p0, p1, p2, p3, vec, h_out, qkv_out, w_qkv, sems):
    row = pl.program_id(0)
    width = vec.shape[1]
    copies = placements((p0, p1, p2, p3), [(0, 3 * width, w_qkv)], place, sems)

    @pl.when(row == 0)
    def _():
        for copy in copies:
            copy.start()

    x = jnp.concatenate([ref[0] for ref in (x0, x1, x2, x3)], axis=0).astype(F32)
    unit, _ = centered(x)
    h = (unit * vec[0:1] + vec[1:2]).astype(BF16)
    h_out[...] = h

    @pl.when(row == 0)
    def _():
        for copy in copies:
            copy.wait()

    q = nn_dot(h, w_qkv[:, :width]).astype(BF16)
    qkv_out[:, :width] = q * jnp.asarray(1.0 / math.sqrt(width // HEADS), BF16)
    qkv_out[:, width:] = nn_dot(h, w_qkv[:, width:]).astype(BF16)


def attend_body(place, lengths, qkv, attn_out, lse_out, bias):
    row = pl.program_id(0)
    width = attn_out.shape[1]
    pair = 2 * (width // HEADS)
    fill_bias(place, lengths, row, bias)
    masks = head_masks(pair)
    for p in range(HEADS // 2):
        at = p * pair
        qp = qkv[:, at : at + pair]
        kp = qkv[:, width + at : width + at + pair]
        v_turned = qkv[:, 2 * width + at : 2 * width + at + pair].T
        outs = []
        for i in range(2):
            scores = nt_dot(kp, qp * masks[i]) + bias[...]
            top = jnp.max(scores, axis=0, keepdims=True)
            grown = jnp.exp(scores - top)
            total = jnp.sum(grown, axis=0, keepdims=True)
            lse_out[0, 2 * p + i : 2 * p + i + 1, :] = top + jnp.log(total)
            probs = (grown * (1.0 / total)).astype(BF16)
            outs.append(nn_dot(v_turned[i * (pair // 2) : (i + 1) * (pair // 2)], probs))
        attn_out[:, at : at + pair] = jnp.concatenate(outs, axis=0).T.astype(BF16)


def up_body(
    place, x0, x1, x2, x3, attn, p0, p1, p2, p3, vec,
    x_one_out, h_out, act_out, slope_out, w_out, w_up, sems,
):
    row = pl.program_id(0)
    width = vec.shape[1]
    hidden = w_up.shape[1]
    jobs = [(0, width, w_out), (width, hidden, w_up)]
    copies = placements((p0, p1, p2, p3), jobs, place, sems)

    @pl.when(row == 0)
    def _():
        for copy in copies:
            copy.start()
        for copy in copies:
            copy.wait()

    x = jnp.concatenate([ref[0] for ref in (x0, x1, x2, x3)], axis=0).astype(F32)
    x_one = x + (nn_dot(attn[...], w_out[...]) + vec[4:5])
    x_one_out[...] = x_one
    unit, _ = centered(x_one)
    h = (unit * vec[2:3] + vec[3:4]).astype(BF16)
    h_out[...] = h
    for j in range(hidden // width):
        columns = slice(j * width, (j + 1) * width)
        up = nn_dot(h, w_up[:, columns]) + vec[6 + j : 7 + j]
        act, slope = gelu_and_slope(up)
        act_out[:, columns] = act.astype(BF16)
        slope_out[:, columns] = slope.astype(BF16)


def write_parts(parts, half, y, column, value, dims):
    hi_count, lo_count, rows = dims
    quarter = value.shape[1]
    value = value.astype(BF16)
    for h in range(hi_count):
        for lo in range(lo_count):
            at = (h * lo_count + lo) * rows
            parts[half, lo, y, h, :, column : column + quarter] = value[at : at + rows]


def send_parts(parts, keep, send, core, sems):
    copies = [
        pltpu.make_async_copy(parts.at[core], keep, sems.at[0]),
        pltpu.make_async_copy(parts.at[1 - core], send, sems.at[1]),
    ]
    for copy in copies:
        copy.start()
    for copy in copies:
        copy.wait()


def down_grad_body(dims, place, act, d0, d1, d2, d3, keep, send, dy_turned, parts, sems):
    part = d0.shape[1]
    for r in range(d0.shape[0]):
        for k, ref in enumerate((d0, d1, d2, d3)):
            at = (r * 4 + k) * part
            if k % 2 == 0:
                both = jnp.concatenate([ref[r], (d1, d3)[k // 2][r]], axis=0)
                dy_turned[:, at : at + 2 * part] = both.T
    quarter = act.shape[1] // 4
    for half in range(2):
        for y in range(2):
            at = (half * 2 + y) * quarter
            value = nn_dot(dy_turned[...], act[:, at : at + quarter])
            write_parts(parts, half, y, 0, value, dims)
    send_parts(parts, keep, send, place[3], sems)


def down_body(
    place, x_one, act, slope, d0, d1, d2, d3,
    b0, b1, b2, b3, c0, c1, vec,
    o0, o1, o2, o3, dx_out, dattn_out, dup_out, dao_out, vec_out,
    w_out, w_up, w_down, up_sems, down_sems,
):
    row = pl.program_id(0)
    width = vec.shape[1]
    hidden = w_up.shape[1]
    slots = x_one.shape[0]
    up_copies = placements((b0, b1, b2, b3), [(0, width, w_out), (width, hidden, w_up)], place, up_sems)
    down_copies = dp_placements((c0, c1), w_down, place, down_sems)

    @pl.when(row == 0)
    def _():
        vec_out[...] = jnp.zeros_like(vec_out)
        for copy in down_copies + up_copies:
            copy.start()
        for copy in down_copies + up_copies:
            copy.wait()

    dy = jnp.concatenate([ref[0] for ref in (d0, d1, d2, d3)], axis=0)
    dy_float = dy.astype(F32)
    result = (x_one[...] + (nt_dot(act[...], w_down[...]) + vec[5:6])).astype(BF16)
    part = slots // 4
    for k, out in enumerate((o0, o1, o2, o3)):
        out[0] = result[k * part : (k + 1) * part]
    for j in range(hidden // width):
        columns = slice(j * width, (j + 1) * width)
        dact = nn_dot(dy, w_down[:, columns])
        dup = (slope[:, columns].astype(F32) * dact).astype(BF16)
        dup_out[:, columns] = dup
        vec_out[6 + j : 7 + j] += jnp.sum(dup.astype(F32), axis=0, keepdims=True)
    dh = nt_dot(dup_out[...], w_up[...])
    unit, scale = centered(x_one[...])
    vec_out[2:3] += jnp.sum(dh * unit, axis=0, keepdims=True)
    vec_out[3:4] += jnp.sum(dh, axis=0, keepdims=True)
    dx = dy_float + norm_back(unit, scale, dh * vec[2:3])
    dx_out[...] = dx
    dao = dx.astype(BF16)
    dao_out[...] = dao
    vec_out[4:5] += jnp.sum(dao.astype(F32), axis=0, keepdims=True)
    vec_out[5:6] += jnp.sum(dy_float, axis=0, keepdims=True)
    dattn_out[...] = nt_dot(dao, w_out[...]).astype(BF16)


def up_grad_body(dims, place, h_two, dup, attn, dao, keep, send, turned, parts, sems):
    turned[...] = h_two[...].T
    quarter = dup.shape[1] // 4
    small = dao.shape[1] // 4
    for half in range(2):
        for y in range(2):
            at = (half * 2 + y) * quarter
            value = nn_dot(turned[...], dup[:, at : at + quarter])
            write_parts(parts, half, y, 0, value, dims)
    turned[...] = attn[...].T
    for half in range(2):
        for y in range(2):
            at = (half * 2 + y) * small
            value = nn_dot(turned[...], dao[:, at : at + small])
            write_parts(parts, half, y, quarter, value, dims)
    send_parts(parts, keep, send, place[3], sems)


def scores_back_body(place, lengths, qkv, lse, dattn, dqkv, bias):
    row = pl.program_id(0) + place[4]
    width = dattn.shape[1]
    pair = 2 * (width // HEADS)
    score_scale = 1.0 / math.sqrt(width // HEADS)
    fill_bias(place, lengths, row, bias)
    masks = head_masks(pair)
    for p in range(HEADS // 2):
        at = p * pair
        qp = qkv[:, at : at + pair]
        kp = qkv[:, width + at : width + at + pair]
        vp = qkv[:, 2 * width + at : 2 * width + at + pair]
        gp = dattn[:, at : at + pair]
        k_turned = kp.T
        probs_list, ds_list, dq_list, q_list, g_list = [], [], [], [], []
        for i in range(2):
            qh = qp * masks[i]
            gh = gp * masks[i]
            scores = nt_dot(kp, qh) + bias[...]
            probs = jnp.exp(scores - lse[0, 2 * p + i : 2 * p + i + 1, :])
            dprobs = nt_dot(vp, gh)
            inner = jnp.sum(probs * dprobs, axis=0, keepdims=True)
            ds = (probs * (dprobs - inner)).astype(BF16)
            dq_list.append(nn_dot(k_turned[i * (pair // 2) : (i + 1) * (pair // 2)], ds))
            probs_list.append(probs.astype(BF16))
            ds_list.append(ds)
            q_list.append(qh)
            g_list.append(gh)
        dq = jnp.concatenate(dq_list, axis=0).T * score_scale
        dk = nn_dot(jnp.concatenate(ds_list, axis=1), jnp.concatenate(q_list, axis=0))
        dv = nn_dot(jnp.concatenate(probs_list, axis=1), jnp.concatenate(g_list, axis=0))
        dqkv[:, at : at + pair] = dq.astype(BF16)
        dqkv[:, width + at : width + at + pair] = dk.astype(BF16)
        dqkv[:, 2 * width + at : 2 * width + at + pair] = dv.astype(BF16)


def qkv_grad_body(dims, place, h_one, g0, g1, keep, send, turned, parts, sems):
    turned[...] = h_one[...].T
    count = g0.shape[0]
    quarter = g0.shape[1] // 4
    for half in range(2):
        for y in range(2):
            at = (half * 2 + y) * quarter
            value = nn_dot(turned[:, :count], g0[:, at : at + quarter])
            value = value + nn_dot(turned[:, count:], g1[:, at : at + quarter])
            write_parts(parts, half, y, 0, value, dims)
    send_parts(parts, keep, send, place[3], sems)


def input_body(
    place, g0, g1, x0, x1, x2, x3, dx, p0, p1, p2, p3, vec, o0, o1, o2, o3, vec_out, w_qkv, sems
):
    row = pl.program_id(0)
    width = vec.shape[1]
    slots = dx.shape[0]
    copies = placements((p0, p1, p2, p3), [(0, 3 * width, w_qkv)], place, sems)

    @pl.when(row == 0)
    def _():
        vec_out[...] = jnp.zeros_like(vec_out)
        for copy in copies:
            copy.start()
        for copy in copies:
            copy.wait()

    first = row < pl.num_programs(0) // 2
    dqkv = jnp.where(first, g0[...], g1[...])
    dh = nt_dot(dqkv, w_qkv[...])
    x = jnp.concatenate([ref[0] for ref in (x0, x1, x2, x3)], axis=0).astype(F32)
    unit, scale = centered(x)
    vec_out[0:1] += jnp.sum(dh * unit, axis=0, keepdims=True)
    vec_out[1:2] += jnp.sum(dh, axis=0, keepdims=True)
    grad = (dx[...] + norm_back(unit, scale, dh * vec[0:1])).astype(BF16)
    part = slots // 4
    for k, out in enumerate((o0, o1, o2, o3)):
        out[0] = grad[k * part : (k + 1) * part]


def shape_of(dims, dtype):
    return jax.ShapeDtypeStruct(dims, dtype)


def rows_spec(rows, cols):
    return pl.BlockSpec((rows, cols), lambda r: (r, 0))


def whole_spec(shape):
    return pl.BlockSpec(shape, lambda r: (0,) * len(shape))


def call(body, grid, in_specs, out_specs, out_shape, scratch, cost, name):
    return pl.pallas_call(
        body,
        grid=(grid,),
        in_specs=in_specs,
        out_specs=out_specs,
        out_shape=out_shape,
        scratch_shapes=scratch,
        compiler_params=pltpu.CompilerParams(
            vmem_limit_bytes=VMEM_BYTES, dimension_semantics=("arbitrary",)
        ),
        cost_estimate=pl.CostEstimate(
            flops=int(cost * 1e9), bytes_accessed=int(cost * 2e6), transcendentals=0
        ),
        name=name,
    )


def swap(value, axis):
    return lax.ppermute(value, axis, [(0, 1), (1, 0)])


def ordered(own, other, index, axis):
    first = jnp.where(index == 0, own, other)
    second = jnp.where(index == 0, other, own)
    return jnp.stack([first, second], axis)


def from_seq(pieces):
    moved = [pieces[0]]
    for k in range(1, 4):
        moved.append(lax.ppermute(pieces[k], ("y", "core"), [(j, j ^ k) for j in range(4)]))
    return moved


def spread_hi(half):
    hi_count = lax.axis_size("hi")
    spread = jnp.broadcast_to(half[None], (hi_count, *half.shape))
    return lax.all_to_all(spread, "hi", 0, 0)


def share(own):
    other = swap(own, "lo")
    return [own, other, swap(own, "core"), swap(other, "core")]


def settle(pieces, lo, core, groups=4):
    near = ordered(pieces[0], pieces[1], lo, 1)
    far = ordered(pieces[2], pieces[3], lo, 1)
    whole = ordered(near, far, core, 2)
    cols = whole.shape[-1]
    whole = whole.reshape(groups, 2, 2, -1, cols)
    return [whole[:, 0, 0], whole[:, 1, 0], whole[:, 0, 1], whole[:, 1, 1]]


def add_pair(keep, got):
    return (keep.astype(F32) + got.astype(F32)).astype(BF16)


def spread_plane(part):
    part = part.reshape(4, *part.shape[2:])
    return lax.all_to_all(part, ("lo", "y"), 0, 0)


def total(part):
    return jnp.sum(part.astype(F32), axis=0).astype(BF16)


def to_all(mine):
    side = swap(mine, "y")
    return [mine, side, swap(mine, "core"), swap(side, "core")]


def after(value, *others):
    return lax.optimization_barrier((value, *others))[0]


def in_columns(pieces, y, core):
    near = ordered(pieces[0], pieces[1], y, 1)
    far = ordered(pieces[2], pieces[3], y, 1)
    both = ordered(near, far, core, 1)
    return both.reshape(both.shape[0], -1).astype(F32)


def adam_update(weight, moment, second, grad, decay, rate):
    moment_new = BETA_ONE * moment + (1.0 - BETA_ONE) * grad
    second_new = BETA_TWO * second + (1.0 - BETA_TWO) * grad * grad
    first_hat = moment_new / (1.0 - BETA_ONE**ADAM_STEP)
    second_hat = second_new / (1.0 - BETA_TWO**ADAM_STEP)
    weight_new = weight - rate * (first_hat / (jnp.sqrt(second_hat) + ADAM_EPS) + decay * weight)
    return (weight_new, moment_new, second_new)


def on_device(
    tokens, cotangent, lengths, attn_w, attn_m, attn_v, mlp_w, mlp_m, mlp_v, vec_w, vec_m, vec_v
):
    lo = lax.axis_index("lo")
    y = lax.axis_index("y")
    core = lax.axis_index("core")
    hi_count = lax.axis_size("hi")
    me = y * 2 + core
    micro_count, row_count, part, width = tokens.shape
    hidden = mlp_w.shape[2]
    shard = attn_w.shape[0]
    slots = 4 * part
    rows = micro_count * row_count // 4
    count = rows * slots
    vec_rows, vec_cols = vec_w.shape
    half_rows = shard // 2
    fits = half_rows % 16 == 0

    flat_tokens = tokens.reshape(4, rows, part, width)
    flat_cot = cotangent.reshape(4, rows, part, width)

    def pick(stack, k):
        return lax.dynamic_index_in_dim(stack, me ^ k, 0, keepdims=False)

    def half_of(value):
        return lax.dynamic_slice_in_dim(value, core * half_rows, half_rows, 0)

    xs = from_seq([pick(flat_tokens, k) for k in range(4)])
    lanes = 128
    ride = jnp.pad(vec_w.reshape(-1), (0, half_rows * lanes - vec_w.size)).reshape(half_rows, lanes)
    first_half = jnp.concatenate([half_of(attn_w[:, : 3 * width]), ride], axis=1).astype(BF16)
    qkv_own = spread_hi(first_half)
    up_half = jnp.concatenate([half_of(attn_w[:, 3 * width :]), half_of(mlp_w[0])], axis=1)
    up_half, down_half, qkv_own = lax.optimization_barrier(
        (up_half.astype(BF16), half_of(mlp_w[1]).astype(BF16), qkv_own)
    )
    qkv_pieces = share(qkv_own)
    up_own = spread_hi(up_half)
    down_own = lax.all_gather(down_half, ("hi", "lo"), axis=0)
    vec_all = ordered(qkv_pieces[0][:, :, 3 * width :], qkv_pieces[1][:, :, 3 * width :], lo, 1)
    vec_all = vec_all.reshape(2 * hi_count, -1)[:, : vec_w.size].reshape(-1, vec_rows, vec_cols)
    vec_all = vec_all.transpose(1, 0, 2).reshape(vec_rows, width)
    vec_float = jnp.pad(vec_all.astype(F32), ((0, 16 - vec_rows), (0, 0)))

    if fits:
        place = jnp.stack([lo, core, me, core, 0 * lo]).astype(jnp.int32)
        dims = (hi_count, 2, shard)
    else:
        qkv_pieces = settle(qkv_pieces, lo, core)
        place = jnp.stack([0 * lo, 0 * lo, me, core, 0 * lo]).astype(jnp.int32)
        dims = (1, 1, width)
    row_lengths = lax.dynamic_slice_in_dim(lengths.reshape(-1), me * rows, rows)

    slot_spec = pl.BlockSpec((1, part, width), lambda r: (r, 0, 0))
    vec_spec = whole_spec((16, width))
    lse_spec = pl.BlockSpec((1, HEADS, slots), lambda r: (r, 0, 0))
    wide = rows_spec(slots, hidden)
    narrow = rows_spec(slots, width)
    triple = rows_spec(slots, 3 * width)
    n_piece = 4 * qkv_pieces[0].shape[0]
    dma = pltpu.SemaphoreType.DMA
    h_one, qkv = call(
        qkv_body,
        rows,
        [SMEM, *[slot_spec] * 4, *[ANY] * 4, vec_spec],
        [narrow, triple],
        [shape_of((count, width), BF16), shape_of((count, 3 * width), BF16)],
        [pltpu.VMEM((width, 3 * width), BF16), dma((n_piece,))],
        7,
        "qkv",
    )(place, *xs, *qkv_pieces, vec_float)

    cot, qkv, up_own = lax.optimization_barrier((flat_cot, qkv, up_own))
    dys = from_seq([pick(cot, k) for k in range(4)])
    up_pieces = share(up_own)
    attn, lse = call(
        attend_body,
        rows,
        [SMEM, SMEM, triple],
        [narrow, lse_spec],
        [shape_of((count, width), BF16), shape_of((rows, HEADS, slots), F32)],
        [pltpu.VMEM((slots, slots), F32)],
        12,
        "attend",
    )(place, row_lengths, qkv)

    if not fits:
        up_pieces = settle(up_pieces, lo, core)
    x_one, h_two, act, slope = call(
        up_body,
        rows,
        [SMEM, *[slot_spec] * 4, narrow, *[ANY] * 4, vec_spec],
        [narrow, narrow, wide, wide],
        [
            shape_of((count, width), F32),
            shape_of((count, width), BF16),
            shape_of((count, hidden), BF16),
            shape_of((count, hidden), BF16),
        ],
        [pltpu.VMEM((width, width), BF16), pltpu.VMEM((width, hidden), BF16), dma((2 * n_piece,))],
        17,
        "up",
    )(place, *xs, attn, *up_pieces, vec_float)

    def parts_shape(quarter):
        return (dims[1], 2, dims[0], dims[2], quarter)

    def grad_call(body, args, quarter, scratch, cost, name):
        shape = parts_shape(quarter)
        return call(
            functools.partial(body, dims),
            1,
            [SMEM, *[whole_spec(a.shape) for a in args]],
            [ANY, ANY],
            [shape_of(shape, BF16)] * 2,
            [scratch, pltpu.VMEM((2, *shape), BF16), dma((2,))],
            cost,
            name,
        )(place, *args)

    def in_dp_order(value):
        if fits:
            return value
        value = value.reshape(2, hi_count, 2, shard, value.shape[-1])
        return value.transpose(2, 0, 1, 3, 4)

    turned = pltpu.VMEM((width, count), BF16)
    down_keep, down_send = grad_call(
        down_grad_body, [act, *dys], hidden // 4, turned, 4, "down_grad"
    )
    down_got = swap(down_send, "core")
    down_far = swap(down_own, "core")
    down_pieces = [down_own, down_far]
    if not fits:
        whole = ordered(down_own, down_far, core, 1).reshape(8, 2, -1, hidden)
        down_pieces = [whole[:, 0], whole[:, 1]]
    n_down = 2 * down_pieces[0].shape[0]
    outs = call(
        down_body,
        rows,
        [SMEM, narrow, wide, wide, *[slot_spec] * 4, *[ANY] * 6, vec_spec],
        [*[slot_spec] * 4, narrow, narrow, wide, narrow, vec_spec],
        [
            *[shape_of((rows, part, width), BF16)] * 4,
            shape_of((count, width), F32),
            shape_of((count, width), BF16),
            shape_of((count, hidden), BF16),
            shape_of((count, width), BF16),
            shape_of((16, width), F32),
        ],
        [
            pltpu.VMEM((width, width), BF16),
            pltpu.VMEM((width, hidden), BF16),
            pltpu.VMEM((width, hidden), BF16),
            dma((2 * n_piece,)),
            dma((n_down,)),
        ],
        18,
        "down",
    )(place, x_one, act, slope, *dys, *up_pieces, *down_pieces, vec_float)
    results, (dx, dattn, dup, dao, vec_mlp) = outs[:4], outs[4:]
    down_part = in_dp_order(add_pair(down_keep, down_got))
    down_part = down_part.reshape(4, *down_part.shape[2:])
    down_part = lax.psum_scatter(down_part, ("lo", "y"), scatter_dimension=0)
    down_mine = lax.psum_scatter(down_part, "hi", scatter_dimension=0)

    up_keep, up_send = grad_call(
        up_grad_body, [h_two, dup, attn, dao], hidden // 4 + width // 4, turned, 6, "up_grad"
    )
    up_got = swap(up_send, "core")

    def scores_back(qkv, half):
        base = half * (rows // 2)
        return call(
            scores_back_body,
            rows // 2,
            [
                SMEM,
                SMEM,
                pl.BlockSpec((slots, 3 * width), lambda r: (r + base, 0)),
                pl.BlockSpec((1, HEADS, slots), lambda r: (r + base, 0, 0)),
                pl.BlockSpec((slots, width), lambda r: (r + base, 0)),
            ],
            triple,
            shape_of((count // 2, 3 * width), BF16),
            [pltpu.VMEM((slots, slots), F32)],
            8,
            "scores_back",
        )(place.at[4].set(base), row_lengths, qkv, lse, dattn)

    grad_first = scores_back(after(qkv, up_send), 0)
    up_part = in_dp_order(add_pair(up_keep, up_got))
    up_part, grad_first = lax.optimization_barrier((up_part, grad_first))
    up_part = spread_plane(up_part)
    grad_last = scores_back(after(qkv, grad_first), 1)
    qkv_keep, qkv_send = grad_call(
        qkv_grad_body, [h_one, grad_first, grad_last], 3 * width // 4, turned, 4, "qkv_grad"
    )
    qkv_got = swap(qkv_send, "core")
    outs = call(
        input_body,
        rows,
        [
            SMEM,
            pl.BlockSpec((slots, 3 * width), lambda r: (jnp.minimum(r, rows // 2 - 1), 0)),
            pl.BlockSpec((slots, 3 * width), lambda r: (jnp.maximum(r - rows // 2, 0), 0)),
            *[slot_spec] * 4,
            narrow,
            *[ANY] * 4,
            vec_spec,
        ],
        [*[slot_spec] * 4, vec_spec],
        [*[shape_of((rows, part, width), BF16)] * 4, shape_of((16, width), F32)],
        [pltpu.VMEM((width, 3 * width), BF16), dma((n_piece,))],
        6,
        "input_grad",
    )(place, grad_first, after(grad_last, qkv_send), *xs, dx, *qkv_pieces, vec_float)
    input_parts, vec_attn = outs[:4], outs[4]

    def send_back(parts):
        parts = from_seq(parts)
        pairs = [ordered(parts[0], parts[1], core, 0), ordered(parts[2], parts[3], core, 0)]
        return ordered(pairs[0], pairs[1], y, 0).reshape(tokens.shape)

    extra_rows = 8
    quarter = 3 * width // 4
    vec_total = (vec_attn + vec_mlp)[:vec_rows].reshape(vec_rows, hi_count, 2, vec_cols)
    vec_total = vec_total.transpose(2, 1, 0, 3).reshape(2, hi_count, -1)
    vec_total = jnp.pad(
        vec_total, ((0, 0), (0, 0), (0, extra_rows * quarter - vec_total.shape[-1]))
    )
    vec_total = vec_total.reshape(2, 1, hi_count, extra_rows, quarter).astype(BF16)
    vec_total = jnp.broadcast_to(vec_total, (2, 2, *vec_total.shape[2:]))
    qkv_part = in_dp_order(add_pair(qkv_keep, qkv_got))
    qkv_part = jnp.concatenate([qkv_part, vec_total], axis=3)
    up_part, qkv_part = lax.optimization_barrier((up_part, qkv_part))
    qkv_part = spread_plane(qkv_part)
    up_mine = total(lax.all_to_all(total(up_part), "hi", 0, 0))
    qkv_mine = total(lax.all_to_all(total(qkv_part), "hi", 0, 0))
    mlp_pieces = to_all(jnp.concatenate([up_mine, down_mine], axis=1))
    qkv_mine, *_ = lax.optimization_barrier((qkv_mine, *mlp_pieces[:1]))
    attn_pieces = to_all(qkv_mine)
    output = send_back(results)
    input_grad = send_back(input_parts)

    vec_sum = attn_pieces[0][shard:].astype(F32) + attn_pieces[2][shard:].astype(F32)
    vec_sum = vec_sum.reshape(-1)[: vec_rows * vec_cols].reshape(vec_rows, vec_cols)
    up_at = hidden // 4
    out_at = up_at + width // 4
    up_sum = in_columns([p[:, :up_at] for p in mlp_pieces], y, core)
    out_sum = in_columns([p[:, up_at:out_at] for p in mlp_pieces], y, core)
    down_sum = in_columns([p[:, out_at:] for p in mlp_pieces], y, core)
    qkv_sum = in_columns([p[:shard] for p in attn_pieces], y, core)
    attn_sum = jnp.concatenate([qkv_sum, out_sum], axis=1)
    mlp_sum = jnp.stack([up_sum, down_sum])
    square = jnp.sum(attn_sum * attn_sum) + jnp.sum(mlp_sum * mlp_sum) + jnp.sum(vec_sum * vec_sum)
    dp_count = 2 * hi_count
    squares = lax.all_to_all(jnp.full((dp_count, 8, 128), square), ("hi", "lo"), 0, 0)
    grad_norm = jnp.sqrt(jnp.sum(squares[:, 0, 0]))
    clip_factor = CLIP_NORM / jnp.maximum(grad_norm, CLIP_NORM)
    attn_new = adam_update(
        attn_w, attn_m, attn_v, attn_sum * clip_factor, WEIGHT_DECAY, LEARN_RATE
    )
    mlp_new = adam_update(mlp_w, mlp_m, mlp_v, mlp_sum * clip_factor, WEIGHT_DECAY, LEARN_RATE)
    vec_new = adam_update(vec_w, vec_m, vec_v, vec_sum * clip_factor, 0.0, VEC_RATE)
    return (output, input_grad, *attn_new, *mlp_new, *vec_new, grad_norm)


def solution(mesh):
    dp_count = mesh.shape["dp"]
    seq_count = mesh.shape["seq"]
    fine = jax.sharding.Mesh(
        mesh.devices.reshape(dp_count // 2, 2, seq_count // 2, 2), ("hi", "lo", "y", "core")
    )
    dp = ("hi", "lo")
    seq = ("y", "core")
    acts = P(None, dp, seq, None)
    attn = P(dp, None)
    mlp = P(None, dp, None)
    vec = P(None, dp)
    return jax.shard_map(
        on_device,
        mesh=fine,
        in_specs=(acts, acts, P(None, dp), attn, attn, attn, mlp, mlp, mlp, vec, vec, vec),
        out_specs=(acts, acts, attn, attn, attn, mlp, mlp, mlp, vec, vec, vec, P()),
        check_vma=False,
    )
```

```python
import functools
import math

import jax
import jax.numpy as jnp
from jax import lax
from jax.experimental import pallas as pl
from jax.experimental.pallas import tpu as pltpu
from jax.sharding import PartitionSpec as P

HEADS = 8
ADAM_STEP = 10
CLIP_NORM = 1.0
BETA_ONE = 0.9
BETA_TWO = 0.999
LEARN_RATE = 0.08
VEC_RATE = 0.4
WEIGHT_DECAY = 0.01
ADAM_EPS = 1e-08
NORM_EPS = 1e-05
VMEM_BYTES = 60 * 1024 * 1024

TAIL_SCALE = 0.4 / math.sqrt(2.0)
TAIL = (
    0.2256758631446491,
    0.22566953041000726,
    0.2078437638365498,
    0.16853459369628254,
    0.1414582080030511,
    -0.005661972621845868,
    0.1691478544806666,
    -0.18293913558029784,
    0.05027141967490775,
)
F32 = jnp.float32
BF16 = jnp.bfloat16
ANY = pl.BlockSpec(memory_space=pl.ANY)
SMEM = pl.BlockSpec(memory_space=pltpu.SMEM)


def nt_dot(left, right):
    return lax.dot_general(left, right, (((1,), (1,)), ((), ())), preferred_element_type=F32)


def nn_dot(left, right):
    return jnp.dot(left, right, preferred_element_type=F32)


def centered(values):
    center = values - jnp.mean(values, axis=-1, keepdims=True)
    spread = jnp.mean(center * center, axis=-1, keepdims=True)
    scale = lax.rsqrt(spread + NORM_EPS)
    return center * scale, scale


def norm_back(unit, scale, grad):
    mean_grad = jnp.mean(grad, axis=-1, keepdims=True)
    mean_both = jnp.mean(grad * unit, axis=-1, keepdims=True)
    return scale * (grad - mean_grad - unit * mean_both)


def gelu_and_slope(up):
    size = jnp.abs(up)
    t = 1.0 / (1.0 + TAIL_SCALE * size)
    poly = jnp.full_like(t, TAIL[-1])
    for coef in TAIL[-2::-1]:
        poly = poly * t + coef
    bell = jnp.exp(-0.5 * up * up)
    tail = 0.5 * (t * poly) * bell
    share = jnp.where(up >= 0, 1.0 - tail, tail)
    return up * share, share + up * (bell * (1.0 / math.sqrt(2.0 * math.pi)))


def placements(pieces, jobs, place, sems):
    lo = place[0]
    core = place[1]
    copies = []
    for i, piece in enumerate(pieces):
        lo_at = lo if i % 2 == 0 else 1 - lo
        core_at = core if i < 2 else 1 - core
        hi_count, rows, _ = piece.shape
        for h in range(hi_count):
            row = pl.multiple_of(((h * 2 + lo_at) * 2 + core_at) * rows, rows)
            for column, width, target in jobs:
                copies.append(
                    pltpu.make_async_copy(
                        piece.at[h, :, pl.ds(column, width)],
                        target.at[pl.ds(row, rows), :],
                        sems.at[len(copies)],
                    )
                )
    return copies


def dp_placements(pieces, target, place, sems):
    copies = []
    for i, piece in enumerate(pieces):
        core_at = place[1] if i == 0 else 1 - place[1]
        dp_count, rows, _ = piece.shape
        for d in range(dp_count):
            row = pl.multiple_of((d * 2 + core_at) * rows, rows)
            copies.append(
                pltpu.make_async_copy(
                    piece.at[d], target.at[pl.ds(row, rows), :], sems.at[len(copies)]
                )
            )
    return copies


def head_masks(width):
    lane = lax.broadcasted_iota(jnp.int32, (1, width), 1)
    first = jnp.where(lane < width // 2, 1.0, 0.0)
    return first.astype(BF16), (1.0 - first).astype(BF16)


def fill_bias(place, lengths, row, bias):
    part = bias.shape[0] // 4
    for k in range(4):
        base = (place[2] ^ k) * part
        slot = lax.broadcasted_iota(jnp.int32, (part, bias.shape[1]), 0) + base
        bias[k * part : (k + 1) * part, :] = jnp.where(slot < lengths[row], 0.0, -1e30)


def qkv_body(place, x0, x1, x2, x3, p0, p1, p2, p3, vec, h_out, qkv_out, w_qkv, sems):
    row = pl.program_id(0)
    width = vec.shape[1]
    copies = placements((p0, p1, p2, p3), [(0, 3 * width, w_qkv)], place, sems)

    @pl.when(row == 0)
    def _():
        for copy in copies:
            copy.start()

    x = jnp.concatenate([ref[0] for ref in (x0, x1, x2, x3)], axis=0).astype(F32)
    unit, _ = centered(x)
    h = (unit * vec[0:1] + vec[1:2]).astype(BF16)
    h_out[...] = h

    @pl.when(row == 0)
    def _():
        for copy in copies:
            copy.wait()

    q = nn_dot(h, w_qkv[:, :width]).astype(BF16)
    qkv_out[:, :width] = q * jnp.asarray(1.0 / math.sqrt(width // HEADS), BF16)
    qkv_out[:, width:] = nn_dot(h, w_qkv[:, width:]).astype(BF16)


def attend_body(place, lengths, qkv, *refs):
    attn_out, lse_out, bias = refs[-3:]
    row = pl.program_id(0) + place[4]
    width = attn_out.shape[1]
    pair = 2 * (width // HEADS)
    fill_bias(place, lengths, row, bias)
    masks = head_masks(pair)
    for p in range(HEADS // 2):
        at = p * pair
        qp = qkv[:, at : at + pair]
        kp = qkv[:, width + at : width + at + pair]
        v_turned = qkv[:, 2 * width + at : 2 * width + at + pair].T
        outs = []
        for i in range(2):
            scores = nt_dot(kp, qp * masks[i]) + bias[...]
            top = jnp.max(scores, axis=0, keepdims=True)
            grown = jnp.exp(scores - top)
            total = jnp.sum(grown, axis=0, keepdims=True)
            lse_out[0, 2 * p + i : 2 * p + i + 1, :] = top + jnp.log(total)
            probs = (grown * (1.0 / total)).astype(BF16)
            outs.append(nn_dot(v_turned[i * (pair // 2) : (i + 1) * (pair // 2)], probs))
        attn_out[:, at : at + pair] = jnp.concatenate(outs, axis=0).T.astype(BF16)


def up_body(
    place, x0, x1, x2, x3, attn, p0, p1, p2, p3, vec,
    x_one_out, h_out, act_out, slope_out, w_out, w_up, sems,
):
    row = pl.program_id(0)
    width = vec.shape[1]
    hidden = w_up.shape[1]
    jobs = [(0, width, w_out), (width, hidden, w_up)]
    copies = placements((p0, p1, p2, p3), jobs, place, sems)

    @pl.when(row == 0)
    def _():
        for copy in copies:
            copy.start()
        for copy in copies:
            copy.wait()

    x = jnp.concatenate([ref[0] for ref in (x0, x1, x2, x3)], axis=0).astype(F32)
    x_one = x + (nn_dot(attn[...], w_out[...]) + vec[4:5])
    x_one_out[...] = x_one
    unit, _ = centered(x_one)
    h = (unit * vec[2:3] + vec[3:4]).astype(BF16)
    h_out[...] = h
    for j in range(hidden // width):
        columns = slice(j * width, (j + 1) * width)
        up = nn_dot(h, w_up[:, columns]) + vec[6 + j : 7 + j]
        act, slope = gelu_and_slope(up)
        act_out[:, columns] = act.astype(BF16)
        slope_out[:, columns] = slope.astype(BF16)


def write_parts(parts, half, y, column, value, dims):
    hi_count, lo_count, rows = dims
    quarter = value.shape[1]
    value = value.astype(BF16)
    for h in range(hi_count):
        for lo in range(lo_count):
            at = (h * lo_count + lo) * rows
            parts[half, lo, y, h, :, column : column + quarter] = value[at : at + rows]


def send_parts(parts, keep, send, place, sems):
    core = place[3]
    copies = []
    for i in range(parts.shape[1]):
        for j in range(2):
            lo_at, y_at = (place[5] ^ i, place[6] ^ j)
            for half, target in ((core, keep), (1 - core, send)):
                copies.append(
                    pltpu.make_async_copy(
                        parts.at[half, lo_at, y_at], target.at[i, j], sems.at[len(copies)]
                    )
                )
    for copy in copies:
        copy.start()
    for copy in copies:
        copy.wait()


def down_grad_body(dims, place, act, d0, d1, d2, d3, keep, send, dy_turned, parts, sems):
    part = d0.shape[1]
    for r in range(d0.shape[0]):
        for k, ref in enumerate((d0, d1, d2, d3)):
            at = (r * 4 + k) * part
            if k % 2 == 0:
                both = jnp.concatenate([ref[r], (d1, d3)[k // 2][r]], axis=0)
                dy_turned[:, at : at + 2 * part] = both.T
    quarter = act.shape[1] // 4
    for half in range(2):
        for y in range(2):
            at = (half * 2 + y) * quarter
            value = nn_dot(dy_turned[...], act[:, at : at + quarter])
            write_parts(parts, half, y, 0, value, dims)
    send_parts(parts, keep, send, place, sems)


def down_body(
    dims, place, x_one, h_two, attn, act, slope, d0, d1, d2, d3,
    b0, b1, b2, b3, c0, c1, vec,
    o0, o1, o2, o3, dx_out, dattn_out, vec_out, keep, send,
    w_out, w_up, w_down, h_turned, attn_turned, dup_all, dao_all, parts,
    up_sems, down_sems, out_sems,
):
    row = pl.program_id(0)
    width = vec.shape[1]
    hidden = w_up.shape[1]
    slots = x_one.shape[0]
    up_copies = placements((b0, b1, b2, b3), [(0, width, w_out), (width, hidden, w_up)], place, up_sems)
    down_copies = dp_placements((c0, c1), w_down, place, down_sems)

    @pl.when(row == 0)
    def _():
        vec_out[...] = jnp.zeros_like(vec_out)
        for copy in down_copies + up_copies:
            copy.start()
        for copy in down_copies + up_copies:
            copy.wait()

    here = pl.ds(pl.multiple_of(row * slots, slots), slots)
    dy = jnp.concatenate([ref[0] for ref in (d0, d1, d2, d3)], axis=0)
    dy_float = dy.astype(F32)
    h_turned[:, here] = h_two[...].T
    attn_turned[:, here] = attn[...].T
    result = (x_one[...] + (nt_dot(act[...], w_down[...]) + vec[5:6])).astype(BF16)
    part = slots // 4
    for k, out in enumerate((o0, o1, o2, o3)):
        out[0] = result[k * part : (k + 1) * part]
    for j in range(hidden // width):
        columns = slice(j * width, (j + 1) * width)
        dact = nn_dot(dy, w_down[:, columns])
        dup = (slope[:, columns].astype(F32) * dact).astype(BF16)
        dup_all[here, columns] = dup
        vec_out[6 + j : 7 + j] += jnp.sum(dup.astype(F32), axis=0, keepdims=True)
    dh = nt_dot(dup_all[here, :], w_up[...])
    unit, scale = centered(x_one[...])
    vec_out[2:3] += jnp.sum(dh * unit, axis=0, keepdims=True)
    vec_out[3:4] += jnp.sum(dh, axis=0, keepdims=True)
    dx = dy_float + norm_back(unit, scale, dh * vec[2:3])
    dx_out[...] = dx
    dao = dx.astype(BF16)
    dao_all[here, :] = dao
    vec_out[4:5] += jnp.sum(dao.astype(F32), axis=0, keepdims=True)
    vec_out[5:6] += jnp.sum(dy_float, axis=0, keepdims=True)
    dattn_out[...] = nt_dot(dao, w_out[...]).astype(BF16)

    @pl.when(row == pl.num_programs(0) - 1)
    def _():
        quarter = hidden // 4
        small = width // 4
        for half in range(2):
            for y in range(2):
                at = (half * 2 + y) * quarter
                value = nn_dot(h_turned[...], dup_all[:, at : at + quarter])
                write_parts(parts, half, y, 0, value, dims)
                at = (half * 2 + y) * small
                value = nn_dot(attn_turned[...], dao_all[:, at : at + small])
                write_parts(parts, half, y, quarter, value, dims)
        send_parts(parts, keep, send, place, out_sems)


def back_rows(
    place, lengths, qkv, lse, dattn, xs, dx, pieces, vec, outs, dqkv, vec_out, w_qkv, bias, sems
):
    step = pl.program_id(0)
    width = vec.shape[1]
    slots = qkv.shape[0]
    pair = 2 * (width // HEADS)
    score_scale = 1.0 / math.sqrt(width // HEADS)
    copies = placements(pieces, [(0, 3 * width, w_qkv)], place, sems)

    @pl.when(step == 0)
    def _():
        vec_out[...] = jnp.zeros_like(vec_out)
        for copy in copies:
            copy.start()

    fill_bias(place, lengths, step + place[4], bias)
    masks = head_masks(pair)
    for p in range(HEADS // 2):
        at = p * pair
        qp = qkv[:, at : at + pair]
        kp = qkv[:, width + at : width + at + pair]
        vp = qkv[:, 2 * width + at : 2 * width + at + pair]
        gp = dattn[:, at : at + pair]
        k_turned = kp.T
        probs_list, ds_list, dq_list, q_list, g_list = [], [], [], [], []
        for i in range(2):
            qh = qp * masks[i]
            gh = gp * masks[i]
            scores = nt_dot(kp, qh) + bias[...]
            probs = jnp.exp(scores - lse[0, 2 * p + i : 2 * p + i + 1, :])
            dprobs = nt_dot(vp, gh)
            inner = jnp.sum(probs * dprobs, axis=0, keepdims=True)
            ds = (probs * (dprobs - inner)).astype(BF16)
            dq_list.append(nn_dot(k_turned[i * (pair // 2) : (i + 1) * (pair // 2)], ds))
            probs_list.append(probs.astype(BF16))
            ds_list.append(ds)
            q_list.append(qh)
            g_list.append(gh)
        dq = jnp.concatenate(dq_list, axis=0).T * score_scale
        dk = nn_dot(jnp.concatenate(ds_list, axis=1), jnp.concatenate(q_list, axis=0))
        dv = nn_dot(jnp.concatenate(probs_list, axis=1), jnp.concatenate(g_list, axis=0))
        dqkv[:, at : at + pair] = dq.astype(BF16)
        dqkv[:, width + at : width + at + pair] = dk.astype(BF16)
        dqkv[:, 2 * width + at : 2 * width + at + pair] = dv.astype(BF16)

    @pl.when(step == 0)
    def _():
        for copy in copies:
            copy.wait()

    dh = nt_dot(dqkv[...], w_qkv[...])
    x = jnp.concatenate([ref[0] for ref in xs], axis=0).astype(F32)
    unit, scale = centered(x)
    vec_out[0:1] += jnp.sum(dh * unit, axis=0, keepdims=True)
    vec_out[1:2] += jnp.sum(dh, axis=0, keepdims=True)
    grad = (dx[...] + norm_back(unit, scale, dh * vec[0:1])).astype(BF16)
    part = slots // 4
    for k, out in enumerate(outs):
        out[0] = grad[k * part : (k + 1) * part]


def back_first_body(
    place, lengths, qkv, lse, dattn, x0, x1, x2, x3, dx, p0, p1, p2, p3, vec,
    o0, o1, o2, o3, dqkv_out, vec_out, w_qkv, bias, sems,
):
    back_rows(
        place, lengths, qkv, lse, dattn, (x0, x1, x2, x3), dx, (p0, p1, p2, p3), vec,
        (o0, o1, o2, o3), dqkv_out, vec_out, w_qkv, bias, sems,
    )


def back_last_body(
    dims, place, lengths, qkv, lse, dattn, x0, x1, x2, x3, dx, p0, p1, p2, p3, vec, h_one, before,
    u0, u1, u2, u3,
    o0, o1, o2, o3, vec_out, keep, send, dqkv, w_qkv, bias, h_turned, parts, sems, out_sems,
):
    step = pl.program_id(0)
    slots = qkv.shape[0]
    here = pl.ds(pl.multiple_of(step * slots, slots), slots)
    back_rows(
        place, lengths, qkv, lse, dattn, (x0, x1, x2, x3), dx, (p0, p1, p2, p3), vec,
        (o0, o1, o2, o3), dqkv.at[here], vec_out, w_qkv, bias, sems,
    )

    @pl.when(step == pl.num_programs(0) - 1)
    def _():
        count = before.shape[0]
        h_turned[...] = h_one[...].T
        quarter = before.shape[1] // 4
        for half in range(2):
            for y in range(2):
                at = (half * 2 + y) * quarter
                value = nn_dot(h_turned[:, :count], before[:, at : at + quarter])
                value = value + nn_dot(h_turned[:, count:], dqkv[:, at : at + quarter])
                write_parts(parts, half, y, 0, value, dims)
        send_parts(parts, keep, send, place, out_sems)


def add_body(with_vec, *refs):
    if with_vec:
        keep, got, *vecs = refs[:-4]
    else:
        keep, got = refs[:-4]
    outs = refs[-4:]
    rows = keep.shape[2]
    for k, out in enumerate(outs):
        value = (keep[k].astype(F32) + got[k].astype(F32)).astype(BF16)
        if not with_vec:
            out[...] = value
            continue
        out[:, :rows, :] = value
        out[:, rows:, :] = jnp.zeros((out.shape[0], 16, out.shape[2]), BF16)
        sums = vecs[0][...]
        for vec in vecs[1:]:
            sums = sums + vec[...]
        lanes = sums.shape[1] // out.shape[0]
        for h in range(out.shape[0]):
            out[h, rows:, :lanes] = sums[:, h * lanes : (h + 1) * lanes].astype(BF16)


def collect_body(place, p0, p1, p2, p3, out):
    for k, piece in enumerate((p0, p1, p2, p3)):
        out[place[2] ^ k] = piece[...]


def in_order(values, place):
    core, y = place[3], place[7]
    near = (jnp.where(y == 0, values[0], values[1]), jnp.where(y == 0, values[1], values[0]))
    far = (jnp.where(y == 0, values[2], values[3]), jnp.where(y == 0, values[3], values[2]))
    first = (jnp.where(core == 0, near[0], far[0]), jnp.where(core == 0, near[1], far[1]))
    second = (jnp.where(core == 0, far[0], near[0]), jnp.where(core == 0, far[1], near[1]))
    return (*first, *second)


def vec_sums(a0, a2, place, shard):
    lanes = 128
    own = a0[shard:, :lanes].astype(F32)
    far = a2[shard:, :lanes].astype(F32)
    both = own + far
    lane = lax.broadcasted_iota(jnp.int32, both.shape, 1) // (lanes // 2)
    return jnp.where(lane == place[8], both, 0.0)


def square_body(place, m0, m1, m2, m3, a0, a1, a2, a3, out):
    shard = m0.shape[0]
    values = []
    for mlp, attn in ((m0, a0), (m1, a1), (m2, a2), (m3, a3)):
        big = mlp[...].astype(F32)
        small = attn[:shard].astype(F32)
        values.append(jnp.sum(big * big) + jnp.sum(small * small))
    vec = vec_sums(a0, a2, place, shard)
    first, second, third, fourth = in_order(values, place)
    value = ((first + second) + (third + fourth)) + jnp.sum(vec * vec)
    out[...] = jnp.full(out.shape, value, F32)


def adam_parts(weight, moment, second, grad, decay, rate):
    moment_new = BETA_ONE * moment + (1.0 - BETA_ONE) * grad
    second_new = BETA_TWO * second + (1.0 - BETA_TWO) * grad * grad
    first_hat = moment_new * (1.0 / (1.0 - BETA_ONE**ADAM_STEP))
    second_hat = second_new * (1.0 / (1.0 - BETA_TWO**ADAM_STEP))
    step = first_hat / (jnp.sqrt(second_hat) + ADAM_EPS)
    return weight - rate * (step + decay * weight), moment_new, second_new


def adam_body(
    place, squares, m0, m1, m2, m3, a0, a1, a2, a3,
    attn_w, attn_m, attn_v, mlp_w, mlp_m, mlp_v, vec_w, vec_m, vec_v,
    norm_out, attn_wo, attn_mo, attn_vo, mlp_wo, mlp_mo, mlp_vo, vec_wo, vec_mo, vec_vo,
):
    shard = m0.shape[0]
    hidden = mlp_w.shape[2]
    quarter = hidden // 4
    wide = a0.shape[1]
    small = m0.shape[1] - 2 * quarter
    value = squares[0]
    for d in range(1, squares.shape[0]):
        value = value + squares[d]
    norm = jnp.sqrt(value)
    norm_out[...] = norm[0:1, 0:1]
    factor = (CLIP_NORM / jnp.maximum(norm, CLIP_NORM))[0:1, 0:1]
    rows, cols = vec_w.shape
    vec = vec_sums(a0, a2, place, shard)
    grad = (vec[:rows, :cols] + vec[:rows, cols : 2 * cols]) * factor
    parts = adam_parts(vec_w[...], vec_m[...], vec_v[...], grad, 0.0, VEC_RATE)
    for new, new_value in zip((vec_wo, vec_mo, vec_vo), parts):
        new[...] = new_value
    core, y = place[3], place[7]
    olds = (attn_w, attn_m, attn_v)
    news = (attn_wo, attn_mo, attn_vo)
    mlp_olds = (mlp_w, mlp_m, mlp_v)
    mlp_news = (mlp_wo, mlp_mo, mlp_vo)
    for i, (mlp, attn) in enumerate(((m0, a0), (m1, a1), (m2, a2), (m3, a3))):
        side = (core if i < 2 else 1 - core) * 2 + (y if i % 2 == 0 else 1 - y)

        def columns(base, size, side=side):
            return pl.ds(pl.multiple_of(base + side * size, 128), size)

        at = columns(0, wide)
        grad = attn[:shard].astype(F32) * factor
        for new, new_value in zip(news, adam_parts(*[o[:, at] for o in olds], grad, WEIGHT_DECAY, LEARN_RATE)):
            new[:, at] = new_value
        at = columns(4 * wide, small)
        grad = mlp[:, quarter : quarter + small].astype(F32) * factor
        for new, new_value in zip(news, adam_parts(*[o[:, at] for o in olds], grad, WEIGHT_DECAY, LEARN_RATE)):
            new[:, at] = new_value
        at = columns(0, quarter)
        for j, start in ((0, 0), (1, quarter + small)):
            grad = mlp[:, start : start + quarter].astype(F32) * factor
            parts = adam_parts(*[o[j, :, at] for o in mlp_olds], grad, WEIGHT_DECAY, LEARN_RATE)
            for new, new_value in zip(mlp_news, parts):
                new[j, :, at] = new_value


def shape_of(dims, dtype):
    return jax.ShapeDtypeStruct(dims, dtype)


def rows_spec(rows, cols):
    return pl.BlockSpec((rows, cols), lambda r: (r, 0))


def whole_spec(shape):
    return pl.BlockSpec(shape, lambda r: (0,) * len(shape))


def call(body, grid, in_specs, out_specs, out_shape, scratch, cost, name, aliases=None):
    return pl.pallas_call(
        body,
        grid=(grid,),
        in_specs=in_specs,
        out_specs=out_specs,
        out_shape=out_shape,
        scratch_shapes=scratch,
        input_output_aliases=aliases or {},
        compiler_params=pltpu.CompilerParams(
            vmem_limit_bytes=VMEM_BYTES, dimension_semantics=("arbitrary",)
        ),
        cost_estimate=pl.CostEstimate(
            flops=int(cost * 1e9), bytes_accessed=int(cost * 2e6), transcendentals=0
        ),
        name=name,
    )


def swap(value, axis):
    return lax.ppermute(value, axis, [(0, 1), (1, 0)])


def ordered(own, other, index, axis):
    first = jnp.where(index == 0, own, other)
    second = jnp.where(index == 0, other, own)
    return jnp.stack([first, second], axis)


def from_seq(pieces):
    moved = [pieces[0]]
    for k in range(1, 4):
        moved.append(lax.ppermute(pieces[k], ("y", "core"), [(j, j ^ k) for j in range(4)]))
    return moved


def spread_hi(half):
    hi_count = lax.axis_size("hi")
    spread = jnp.broadcast_to(half[None], (hi_count, *half.shape))
    return lax.all_to_all(spread, "hi", 0, 0)


def share(own):
    other = swap(own, "lo")
    return [own, other, swap(own, "core"), swap(other, "core")]


def settle(pieces, lo, core, groups=4):
    near = ordered(pieces[0], pieces[1], lo, 1)
    far = ordered(pieces[2], pieces[3], lo, 1)
    whole = ordered(near, far, core, 2)
    cols = whole.shape[-1]
    whole = whole.reshape(groups, 2, 2, -1, cols)
    return [whole[:, 0, 0], whole[:, 1, 0], whole[:, 0, 1], whole[:, 1, 1]]


def add_pair(keep, got):
    return (keep.astype(F32) + got.astype(F32)).astype(BF16)


def spread_plane(part):
    part = part.reshape(4, *part.shape[2:])
    return lax.all_to_all(part, ("lo", "y"), 0, 0)


def total(part):
    return jnp.sum(part.astype(F32), axis=0).astype(BF16)


def to_all(mine):
    side = swap(mine, "y")
    return [mine, side, swap(mine, "core"), swap(side, "core")]


def after(value, *others):
    return lax.optimization_barrier((value, *others))[0]


def in_columns(pieces, y, core):
    near = ordered(pieces[0], pieces[1], y, 1)
    far = ordered(pieces[2], pieces[3], y, 1)
    both = ordered(near, far, core, 1)
    return both.reshape(both.shape[0], -1).astype(F32)


def adam_update(weight, moment, second, grad, decay, rate):
    moment_new = BETA_ONE * moment + (1.0 - BETA_ONE) * grad
    second_new = BETA_TWO * second + (1.0 - BETA_TWO) * grad * grad
    first_hat = moment_new / (1.0 - BETA_ONE**ADAM_STEP)
    second_hat = second_new / (1.0 - BETA_TWO**ADAM_STEP)
    weight_new = weight - rate * (first_hat / (jnp.sqrt(second_hat) + ADAM_EPS) + decay * weight)
    return (weight_new, moment_new, second_new)


def on_device(
    tokens, cotangent, lengths, attn_w, attn_m, attn_v, mlp_w, mlp_m, mlp_v, vec_w, vec_m, vec_v
):
    lo = lax.axis_index("lo")
    y = lax.axis_index("y")
    core = lax.axis_index("core")
    hi_count = lax.axis_size("hi")
    me = y * 2 + core
    micro_count, row_count, part, width = tokens.shape
    hidden = mlp_w.shape[2]
    shard = attn_w.shape[0]
    slots = 4 * part
    rows = micro_count * row_count // 4
    count = rows * slots
    vec_rows, vec_cols = vec_w.shape
    half_rows = shard // 2
    fits = half_rows % 16 == 0

    flat_tokens = tokens.reshape(4, rows, part, width)
    flat_cot = cotangent.reshape(4, rows, part, width)

    def pick(stack, k):
        return lax.dynamic_index_in_dim(stack, me ^ k, 0, keepdims=False)

    def half_of(value):
        return lax.dynamic_slice_in_dim(value, core * half_rows, half_rows, 0)

    xs = from_seq([pick(flat_tokens, k) for k in range(4)])
    lanes = 128
    ride = jnp.pad(vec_w.reshape(-1), (0, half_rows * lanes - vec_w.size)).reshape(half_rows, lanes)
    first_half = jnp.concatenate([half_of(attn_w[:, : 3 * width]), ride], axis=1).astype(BF16)
    qkv_own = spread_hi(first_half)
    up_half = jnp.concatenate([half_of(attn_w[:, 3 * width :]), half_of(mlp_w[0])], axis=1)
    up_own = spread_hi(after(up_half.astype(BF16), qkv_own))
    qkv_own, xs[3] = lax.optimization_barrier((qkv_own, xs[3]))
    qkv_other = swap(qkv_own, "lo")
    qkv_pieces = [qkv_own, qkv_other, swap(qkv_own, "core"), swap(qkv_other, "core")]
    down_half = after(half_of(mlp_w[1]).astype(BF16), up_own)
    down_own = lax.all_gather(down_half, ("hi", "lo"), axis=0)
    vec_all = ordered(qkv_pieces[0][:, :, 3 * width :], qkv_pieces[1][:, :, 3 * width :], lo, 1)
    vec_all = vec_all.reshape(2 * hi_count, -1)[:, : vec_w.size].reshape(-1, vec_rows, vec_cols)
    vec_all = vec_all.transpose(1, 0, 2).reshape(vec_rows, width)
    vec_float = jnp.pad(vec_all.astype(F32), ((0, 16 - vec_rows), (0, 0)))

    if fits:
        places = [lo, core, me, core, 0 * lo, lo, y, y, lo]
        dims = (hi_count, 2, shard)
    else:
        qkv_pieces = settle(qkv_pieces, lo, core)
        places = [0 * lo, 0 * lo, me, core, 0 * lo, 0 * lo, 0 * lo, y, lo]
        dims = (1, 1, width)
    place = jnp.stack(places).astype(jnp.int32)
    flat = jnp.stack([*places[:5], 0 * lo, 0 * lo]).astype(jnp.int32)
    later = place.at[4].set(rows // 2)
    row_lengths = lax.dynamic_slice_in_dim(lengths.reshape(-1), me * rows, rows)

    slot_spec = pl.BlockSpec((1, part, width), lambda r: (r, 0, 0))
    vec_spec = whole_spec((16, width))
    lse_spec = pl.BlockSpec((1, HEADS, slots), lambda r: (r, 0, 0))
    wide = rows_spec(slots, hidden)
    narrow = rows_spec(slots, width)
    triple = rows_spec(slots, 3 * width)
    n_piece = 4 * qkv_pieces[0].shape[0]
    dma = pltpu.SemaphoreType.DMA
    h_one, qkv = call(
        qkv_body,
        rows,
        [SMEM, *[slot_spec] * 4, *[ANY] * 4, vec_spec],
        [narrow, triple],
        [shape_of((count, width), BF16), shape_of((count, 3 * width), BF16)],
        [pltpu.VMEM((width, 3 * width), BF16), dma((n_piece,))],
        7,
        "qkv",
    )(place, *xs, *qkv_pieces, vec_float)

    cot, qkv, up_own = lax.optimization_barrier((flat_cot, qkv, up_own))
    dys = from_seq([pick(cot, k) for k in range(4)])
    up_other = swap(up_own, "lo")

    def half_spec(block, base):
        zeros = (0,) * (len(block) - 1)
        return pl.BlockSpec(block, lambda r: (r + base, *zeros))

    def attend(qkv, base, before):
        return call(
            attend_body,
            rows // 2,
            [SMEM, SMEM, half_spec((slots, 3 * width), base), *[ANY] * len(before)],
            [half_spec((slots, width), base), half_spec((1, HEADS, slots), base)],
            [shape_of((count, width), BF16), shape_of((rows, HEADS, slots), F32)],
            [pltpu.VMEM((slots, slots), F32)],
            7,
            "attend",
            {3: 0, 4: 1} if before else None,
        )(later if base else place, row_lengths, qkv, *before)

    attn, lse = attend(qkv, 0, [])
    up_other, attn, lse = lax.optimization_barrier((up_other, attn, lse))
    attn, lse = attend(qkv, rows // 2, [attn, lse])
    up_pieces = [up_own, up_other, swap(up_own, "core"), swap(up_other, "core")]
    if not fits:
        up_pieces = settle(up_pieces, lo, core)
    x_one, h_two, act, slope = call(
        up_body,
        rows,
        [SMEM, *[slot_spec] * 4, narrow, *[ANY] * 4, vec_spec],
        [narrow, narrow, wide, wide],
        [
            shape_of((count, width), F32),
            shape_of((count, width), BF16),
            shape_of((count, hidden), BF16),
            shape_of((count, hidden), BF16),
        ],
        [pltpu.VMEM((width, width), BF16), pltpu.VMEM((width, hidden), BF16), dma((2 * n_piece,))],
        17,
        "up",
    )(place, *xs, attn, *up_pieces, vec_float)

    def parts_shape(quarter):
        return (dims[1], 2, dims[0], dims[2], quarter)


    def in_dp_order(value):
        if fits:
            return value
        value = value.reshape(2, hi_count, 2, shard, value.shape[-1])
        return value.transpose(2, 0, 1, 3, 4)

    turned = pltpu.VMEM((width, count), BF16)
    n_part = 4 * dims[1]
    shape = parts_shape(hidden // 4)
    down_keep, down_send = call(
        functools.partial(down_grad_body, dims),
        1,
        [SMEM, whole_spec(act.shape), *[whole_spec(xs[0].shape)] * 4],
        [ANY, ANY],
        [shape_of(shape, BF16)] * 2,
        [turned, pltpu.VMEM((2, *shape), BF16), dma((n_part,))],
        5,
        "down_grad",
    )(flat, act, *dys)
    down_got = swap(down_send, "core")
    down_far = swap(down_own, "core")
    down_pieces = [down_own, down_far]
    if not fits:
        whole = ordered(down_own, down_far, core, 1).reshape(8, 2, -1, hidden)
        down_pieces = [whole[:, 0], whole[:, 1]]
    n_down = 2 * down_pieces[0].shape[0]
    shape = parts_shape(hidden // 4 + width // 4)
    outs = call(
        functools.partial(down_body, dims),
        rows,
        [SMEM, narrow, narrow, narrow, wide, wide, *[slot_spec] * 4, *[ANY] * 6, vec_spec],
        [*[slot_spec] * 4, narrow, narrow, vec_spec, ANY, ANY],
        [
            *[shape_of((rows, part, width), BF16)] * 4,
            shape_of((count, width), F32),
            shape_of((count, width), BF16),
            shape_of((16, width), F32),
            shape_of(shape, BF16),
            shape_of(shape, BF16),
        ],
        [
            pltpu.VMEM((width, width), BF16),
            pltpu.VMEM((width, hidden), BF16),
            pltpu.VMEM((width, hidden), BF16),
            turned,
            turned,
            pltpu.VMEM((count, hidden), BF16),
            pltpu.VMEM((count, width), BF16),
            pltpu.VMEM((2, *shape), BF16),
            dma((2 * n_piece,)),
            dma((n_down,)),
            dma((n_part,)),
        ],
        20,
        "down",
    )(place, x_one, h_two, attn, act, slope, *dys, *up_pieces, *down_pieces, vec_float)
    results, (dx, dattn, vec_mlp, up_keep, up_send) = outs[:4], outs[4:]
    up_got = swap(up_send, "core")
    down_part = in_dp_order(add_pair(down_keep, down_got))
    down_part = down_part.reshape(4, *down_part.shape[2:])
    down_plane = lax.psum_scatter(down_part, ("lo", "y"), scatter_dimension=0)
    down_mine = lax.psum_scatter(down_plane, "hi", scatter_dimension=0)

    def collect(parts):
        return call(
            collect_body,
            1,
            [SMEM, *[whole_spec(parts[0].shape)] * 4],
            whole_spec((4, *parts[0].shape)),
            shape_of((4, *parts[0].shape), BF16),
            [],
            2,
            "collect",
        )(place, *parts).reshape(tokens.shape)

    results = from_seq(results)
    back_args = [lse, dattn, *xs, dx]
    weights = [*qkv_pieces, vec_float]

    def back_specs(base):
        return [
            SMEM,
            SMEM,
            half_spec((slots, 3 * width), base),
            half_spec((1, HEADS, slots), base),
            half_spec((slots, width), base),
            *[half_spec((1, part, width), base)] * 4,
            half_spec((slots, width), base),
            *[ANY] * 4,
            vec_spec,
        ]

    back_shapes = [shape_of((rows, part, width), BF16)] * 4
    back_scratch = [pltpu.VMEM((width, 3 * width), BF16), pltpu.VMEM((slots, slots), F32)]
    outs = call(
        back_first_body,
        rows // 2,
        back_specs(0),
        [*[half_spec((1, part, width), 0)] * 4, triple, vec_spec],
        [*back_shapes, shape_of((count // 2, 3 * width), BF16), shape_of((16, width), F32)],
        [*back_scratch, dma((n_piece,))],
        11,
        "back_first",
    )(place, row_lengths, after(qkv, up_send, down_part), *back_args, *weights)
    input_first, (grad_first, vec_first) = outs[:4], outs[4:]

    def add_call(keep, got, vecs):
        dims_of = (4, *keep.shape[2:])
        more = 16 if vecs else 0
        out = shape_of((dims_of[1], dims_of[2] + more, dims_of[3]), BF16)
        return call(
            functools.partial(add_body, bool(vecs)),
            1,
            [whole_spec(dims_of)] * 2 + [whole_spec(v.shape) for v in vecs],
            [whole_spec(out.shape)] * 4,
            [out] * 4,
            [],
            2,
            "add",
        )(keep.reshape(dims_of), got.reshape(dims_of), *vecs)

    def plane_sum(parts):
        moved = [parts[0]]
        for k in (2, 1, 3):
            perm = [(j, j ^ k) for j in range(4)]
            moved.append(lax.ppermute(parts[k], ("lo", "y"), perm))
        return moved

    def add_moved(moved):
        value = (moved[0].astype(F32) + moved[1].astype(F32)) + moved[2].astype(F32)
        return (value + moved[3].astype(F32)).astype(BF16)

    def plane_total(keep, got, extra):
        part = in_dp_order(add_pair(keep, got))
        if extra is not None:
            part = jnp.concatenate([part, extra], axis=3)
        return total(spread_plane(part))

    qkv_last = qkv
    output = collect(results)
    if fits:
        parts = add_call(after(up_keep, grad_first, *results), up_got, [])
        parts = lax.optimization_barrier((*parts, grad_first))
        qkv_last = after(qkv, *parts, down_plane)
        up_moved = plane_sum(parts[:4])
    quarter = 3 * width // 4
    shape = parts_shape(quarter)
    outs = call(
        functools.partial(back_last_body, dims),
        rows // 2,
        [
            *back_specs(rows // 2),
            whole_spec((count, width)),
            whole_spec((count // 2, 3 * width)),
            *[ANY] * 4,
        ],
        [*[half_spec((1, part, width), rows // 2)] * 4, vec_spec, ANY, ANY],
        [*back_shapes, shape_of((16, width), F32), shape_of(shape, BF16), shape_of(shape, BF16)],
        [
            pltpu.VMEM((count // 2, 3 * width), BF16),
            *back_scratch,
            turned,
            pltpu.VMEM((2, *shape), BF16),
            dma((n_piece,)),
            dma((n_part,)),
        ],
        13,
        "back_last",
        {17 + k: k for k in range(4)},
    )(later, row_lengths, qkv_last, *back_args, *weights, h_one, grad_first, *input_first)
    input_parts, (vec_last, qkv_keep, qkv_send) = outs[:4], outs[4:]
    if fits:
        qkv_send = after(qkv_send, *up_moved)
    qkv_got = swap(qkv_send, "core")
    vecs = [vec_mlp, vec_first, vec_last]

    if fits:
        parts = add_call(qkv_keep, qkv_got, vecs)
        qkv_moved = plane_sum(parts)
        up_mine = total(lax.all_to_all(add_moved(up_moved), "hi", 0, 0))
        qkv_mine = total(lax.all_to_all(add_moved(qkv_moved), "hi", 0, 0))
    else:
        vec_total = (vec_mlp + vec_first + vec_last).reshape(16, hi_count, 2, vec_cols)
        vec_total = vec_total.transpose(1, 0, 2, 3).reshape(1, 1, hi_count, 16, 2 * vec_cols)
        vec_total = jnp.pad(vec_total.astype(BF16), ((0, 0),) * 4 + ((0, quarter - 2 * vec_cols),))
        vec_total = jnp.broadcast_to(vec_total, (2, 2, *vec_total.shape[2:]))
        up_mine = total(lax.all_to_all(plane_total(up_keep, up_got, None), "hi", 0, 0))
        qkv_mine = plane_total(qkv_keep, qkv_got, vec_total)
        qkv_mine = total(lax.all_to_all(qkv_mine, "hi", 0, 0))
    mlp_pieces = to_all(jnp.concatenate([up_mine, down_mine], axis=1))
    attn_pieces = to_all(qkv_mine)
    input_grad = collect(from_seq(input_parts))

    dp_count = 2 * hi_count
    if fits:
        pieces = [*mlp_pieces, *attn_pieces]
        piece_specs = [whole_spec(p.shape) for p in pieces]
        squares_shape = (dp_count, 8, 128)
        squares = call(
            square_body,
            1,
            [SMEM, *piece_specs],
            whole_spec(squares_shape),
            shape_of(squares_shape, F32),
            [],
            2,
            "squares",
        )(place, *pieces)
        squares = lax.all_to_all(squares, ("hi", "lo"), 0, 0)
        states = [attn_w, attn_m, attn_v, mlp_w, mlp_m, mlp_v, vec_w, vec_m, vec_v]
        state_specs = [whole_spec(v.shape) for v in states]
        norm, *new = call(
            adam_body,
            1,
            [SMEM, whole_spec(squares_shape), *piece_specs, *state_specs],
            [whole_spec((1, 1)), *state_specs],
            [shape_of((1, 1), F32), *[shape_of(v.shape, F32) for v in states]],
            [],
            6,
            "adam",
        )(place, squares, *pieces, *states)
        return (output, input_grad, *new, norm.reshape(()))

    vec_sum = attn_pieces[0][shard:].astype(F32) + attn_pieces[2][shard:].astype(F32)
    vec_sum = jnp.where(lo == 0, vec_sum[:, :vec_cols], vec_sum[:, vec_cols : 2 * vec_cols])
    vec_sum = vec_sum[:vec_rows]
    up_at = hidden // 4
    out_at = up_at + width // 4
    up_sum = in_columns([p[:, :up_at] for p in mlp_pieces], y, core)
    out_sum = in_columns([p[:, up_at:out_at] for p in mlp_pieces], y, core)
    down_sum = in_columns([p[:, out_at:] for p in mlp_pieces], y, core)
    qkv_sum = in_columns([p[:shard] for p in attn_pieces], y, core)
    attn_sum = jnp.concatenate([qkv_sum, out_sum], axis=1)
    mlp_sum = jnp.stack([up_sum, down_sum])
    square = jnp.sum(attn_sum * attn_sum) + jnp.sum(mlp_sum * mlp_sum) + jnp.sum(vec_sum * vec_sum)
    squares = lax.all_to_all(jnp.full((dp_count, 8, 128), square), ("hi", "lo"), 0, 0)
    grad_norm = jnp.sqrt(jnp.sum(squares[:, 0, 0]))
    clip_factor = CLIP_NORM / jnp.maximum(grad_norm, CLIP_NORM)
    attn_new = adam_update(
        attn_w, attn_m, attn_v, attn_sum * clip_factor, WEIGHT_DECAY, LEARN_RATE
    )
    mlp_new = adam_update(mlp_w, mlp_m, mlp_v, mlp_sum * clip_factor, WEIGHT_DECAY, LEARN_RATE)
    vec_new = adam_update(vec_w, vec_m, vec_v, vec_sum * clip_factor, 0.0, VEC_RATE)
    return (output, input_grad, *attn_new, *mlp_new, *vec_new, grad_norm)


def solution(mesh):
    dp_count = mesh.shape["dp"]
    seq_count = mesh.shape["seq"]
    fine = jax.sharding.Mesh(
        mesh.devices.reshape(dp_count // 2, 2, seq_count // 2, 2), ("hi", "lo", "y", "core")
    )
    dp = ("hi", "lo")
    seq = ("y", "core")
    acts = P(None, dp, seq, None)
    attn = P(dp, None)
    mlp = P(None, dp, None)
    vec = P(None, dp)
    return jax.shard_map(
        on_device,
        mesh=fine,
        in_specs=(acts, acts, P(None, dp), attn, attn, attn, mlp, mlp, mlp, vec, vec, vec),
        out_specs=(acts, acts, attn, attn, attn, mlp, mlp, mlp, vec, vec, vec, P()),
        check_vma=False,
    )
```

```python
import functools
import math

import jax
import jax.numpy as jnp
from jax import lax
from jax.experimental import pallas as pl
from jax.experimental.pallas import tpu as pltpu
from jax.sharding import PartitionSpec as P

HEADS = 8
ADAM_STEP = 10
CLIP_NORM = 1.0
BETA_ONE = 0.9
BETA_TWO = 0.999
LEARN_RATE = 0.08
VEC_RATE = 0.4
WEIGHT_DECAY = 0.01
ADAM_EPS = 1e-08
NORM_EPS = 1e-05
VMEM_BYTES = 63 * 1024 * 1024

F32 = jnp.float32
BF16 = jnp.bfloat16
ANY = pl.BlockSpec(memory_space=pl.ANY)
SMEM = pl.BlockSpec(memory_space=pltpu.SMEM)


def nt_dot(left, right):
    return lax.dot_general(left, right, (((1,), (1,)), ((), ())), preferred_element_type=F32)


def nn_dot(left, right):
    return jnp.dot(left, right, preferred_element_type=F32)


def centered(values):
    center = values - jnp.mean(values, axis=-1, keepdims=True)
    spread = jnp.mean(center * center, axis=-1, keepdims=True)
    scale = lax.rsqrt(spread + NORM_EPS)
    return center * scale, scale


def norm_back(unit, scale, grad):
    mean_grad = jnp.mean(grad, axis=-1, keepdims=True)
    mean_both = jnp.mean(grad * unit, axis=-1, keepdims=True)
    return scale * (grad - mean_grad - unit * mean_both)


def gelu_and_slope(up):
    share = 0.5 + 0.5 * lax.erf(up * (1.0 / math.sqrt(2.0)))
    bell = jnp.exp2(up * up * (-0.5 * math.log2(math.e)))
    return up * share, share + up * (bell * (1.0 / math.sqrt(2.0 * math.pi)))


def load_slots(refs):
    return jnp.concatenate([ref[i] for i in range(refs[0].shape[0]) for ref in refs], axis=0)


def store_slots(refs, value):
    rows, part, _ = refs[0].shape
    for i in range(rows):
        for k, ref in enumerate(refs):
            at = (i * 4 + k) * part
            ref[i] = value[at : at + part]


def placements(pieces, jobs, place, sems):
    lo = place[0]
    core = place[1]
    copies = []
    for i, piece in enumerate(pieces):
        lo_at = lo if i % 2 == 0 else 1 - lo
        core_at = core if i < 2 else 1 - core
        hi_count, rows, _ = piece.shape
        for h in range(hi_count):
            row = pl.multiple_of(((h * 2 + lo_at) * 2 + core_at) * rows, rows)
            for column, width, target in jobs:
                copies.append(
                    pltpu.make_async_copy(
                        piece.at[h, :, pl.ds(column, width)],
                        target.at[pl.ds(row, rows), :],
                        sems.at[len(copies)],
                    )
                )
    return copies


def pair_placements(pieces, target, place, sems):
    copies = []
    for i, piece in enumerate(pieces):
        core_at = place[1] if i == 0 else 1 - place[1]
        hi_count, _, rows, _ = piece.shape
        for h in range(hi_count):
            for j in range(2):
                row = pl.multiple_of(((h * 2 + (place[0] ^ j)) * 2 + core_at) * rows, rows)
                copies.append(
                    pltpu.make_async_copy(
                        piece.at[h, j], target.at[pl.ds(row, rows), :], sems.at[len(copies)]
                    )
                )
    return copies


def head_masks(width):
    lane = lax.broadcasted_iota(jnp.int32, (1, width), 1)
    first = jnp.where(lane < width // 2, 1.0, 0.0)
    return first.astype(BF16), (1.0 - first).astype(BF16)


def fill_bias(place, lengths, row, bias):
    part = bias.shape[0] // 4
    for k in range(4):
        base = (place[2] ^ k) * part
        slot = lax.broadcasted_iota(jnp.int32, (part, bias.shape[1]), 0) + base
        bias[k * part : (k + 1) * part, :] = jnp.where(slot < lengths[row], 0.0, -1e30)


def qkv_body(place, x0, x1, x2, x3, p0, p1, p2, p3, vec, h_out, qkv_out, w_qkv, sems):
    row = pl.program_id(0)
    width = vec.shape[1]
    copies = placements((p0, p1, p2, p3), [(0, 3 * width, w_qkv)], place, sems)

    @pl.when(row == 0)
    def _():
        for copy in copies:
            copy.start()

    x = load_slots((x0, x1, x2, x3)).astype(F32)
    unit, _ = centered(x)
    h = (unit * vec[0:1] + vec[1:2]).astype(BF16)
    h_out[...] = h

    @pl.when(row == 0)
    def _():
        for copy in copies:
            copy.wait()

    q = nn_dot(h, w_qkv[:, :width]).astype(BF16)
    qkv_out[:, :width] = q * jnp.asarray(1.0 / math.sqrt(width // HEADS), BF16)
    qkv_out[:, width:] = nn_dot(h, w_qkv[:, width:]).astype(BF16)


def attend_body(place, lengths, qkv, *refs):
    attn_out, lse_out, bias = refs[-3:]
    row = pl.program_id(0) + place[4]
    width = attn_out.shape[1]
    pair = 2 * (width // HEADS)
    fill_bias(place, lengths, row, bias)
    masks = head_masks(pair)
    for p in range(HEADS // 2):
        at = p * pair
        qp = qkv[:, at : at + pair]
        kp = qkv[:, width + at : width + at + pair]
        v_turned = qkv[:, 2 * width + at : 2 * width + at + pair].T
        outs = []
        for i in range(2):
            scores = nt_dot(kp, qp * masks[i]) + bias[...]
            top = jnp.max(scores, axis=0, keepdims=True)
            grown = jnp.exp(scores - top)
            total = jnp.sum(grown, axis=0, keepdims=True)
            lse_out[0, 2 * p + i : 2 * p + i + 1, :] = top + jnp.log(total)
            probs = (grown * (1.0 / total)).astype(BF16)
            outs.append(nn_dot(v_turned[i * (pair // 2) : (i + 1) * (pair // 2)], probs))
        attn_out[:, at : at + pair] = jnp.concatenate(outs, axis=0).T.astype(BF16)


def write_parts(parts, half, y, column, value, dims):
    hi_count, lo_count, rows = dims
    quarter = value.shape[1]
    value = value.astype(BF16)
    for h in range(hi_count):
        for lo in range(lo_count):
            at = (h * lo_count + lo) * rows
            parts[half, lo, y, h, :, column : column + quarter] = value[at : at + rows]


def send_copies(parts, half, y, keep, send, place, sems):
    mine = half == place[3]
    copies = []
    for i in range(parts.shape[1]):
        for target, wanted in ((keep, mine), (send, jnp.logical_not(mine))):
            lo_count = parts.shape[1]
            copy = pltpu.make_async_copy(
                parts.at[half, i, y],
                target.at[(place[5] ^ i) if lo_count > 1 else 0, place[6] ^ y],
                sems.at[half, i, y],
            )
            copies.append((wanted, copy))
    return copies


def start_all(copies):
    for wanted, copy in copies:
        pl.when(wanted)(copy.start)


def wait_all(copies):
    for wanted, copy in copies:
        pl.when(wanted)(copy.wait)


def mlp_body(
    dims, place, x0, x1, x2, x3, attn, d0, d1, d2, d3, b0, b1, b2, b3, c0, c1, vec,
    o0, o1, o2, o3, dx_out, dattn_out, vec_out, up_keep, up_send, down_keep, down_send,
    w_out, w_up, w_down, h_turned, attn_turned, dy_turned, act_all, dup_all, dao_all,
    up_parts, down_parts, out_sems, up_sems, down_sems, part_sems, more_sems,
):
    row = pl.program_id(0)
    width = vec.shape[1]
    hidden = w_up.shape[1]
    slots = attn.shape[0]
    out_copies = placements((b0, b1, b2, b3), [(0, width, w_out)], place, out_sems)
    up_copies = placements((b0, b1, b2, b3), [(width, hidden, w_up)], place, up_sems)
    down_copies = pair_placements((c0, c1), w_down, place, down_sems)

    def arrived(copies):
        @pl.when(row == 0)
        def _():
            for copy in copies:
                copy.wait()

    @pl.when(row == 0)
    def _():
        vec_out[...] = jnp.zeros_like(vec_out)
        for copy in out_copies + up_copies + down_copies:
            copy.start()

    here = pl.ds(pl.multiple_of(row * slots, slots), slots)
    x = load_slots((x0, x1, x2, x3)).astype(F32)
    dy = load_slots((d0, d1, d2, d3))
    dy_turned[:, here] = dy.T
    attn_turned[:, here] = attn[...].T
    arrived(out_copies)
    x_one = x + (nn_dot(attn[...], w_out[...]) + vec[4:5])
    unit, scale = centered(x_one)
    h = (unit * vec[2:3] + vec[3:4]).astype(BF16)
    h_turned[:, here] = h.T
    arrived(up_copies)
    arrived(down_copies)
    for j in range(hidden // width):
        columns = slice(j * width, (j + 1) * width)
        up = nn_dot(h, w_up[:, columns]) + vec[6 + j : 7 + j]
        act, slope = gelu_and_slope(up)
        act_all[here, columns] = act.astype(BF16)
        dup = (slope * nn_dot(dy, w_down[:, columns])).astype(BF16)
        dup_all[here, columns] = dup
        vec_out[6 + j : 7 + j] += jnp.sum(dup.astype(F32), axis=0, keepdims=True)
    result = x_one + (nt_dot(act_all[here, :], w_down[...]) + vec[5:6])
    store_slots((o0, o1, o2, o3), result.astype(BF16))
    dh = nt_dot(dup_all[here, :], w_up[...])
    vec_out[2:3] += jnp.sum(dh * unit, axis=0, keepdims=True)
    vec_out[3:4] += jnp.sum(dh, axis=0, keepdims=True)
    dy_float = dy.astype(F32)
    dx = dy_float + norm_back(unit, scale, dh * vec[2:3])
    dx_out[...] = dx
    dao = dx.astype(BF16)
    dao_all[here, :] = dao
    vec_out[4:5] += jnp.sum(dao.astype(F32), axis=0, keepdims=True)
    vec_out[5:6] += jnp.sum(dy_float, axis=0, keepdims=True)
    dattn_out[...] = nt_dot(dao, w_out[...]).astype(BF16)

    @pl.when(row == pl.num_programs(0) - 1)
    def _():
        quarter = hidden // 4
        small = width // 4
        copies = []
        for half in range(2):
            for y in range(2):
                at = (half * 2 + y) * quarter
                value = nn_dot(h_turned[...], dup_all[:, at : at + quarter])
                write_parts(up_parts, half, y, 0, value, dims)
                value = nn_dot(dy_turned[...], act_all[:, at : at + quarter])
                write_parts(down_parts, half, y, 0, value, dims)
                at = (half * 2 + y) * small
                value = nn_dot(attn_turned[...], dao_all[:, at : at + small])
                write_parts(up_parts, half, y, quarter, value, dims)
                these = send_copies(up_parts, half, y, up_keep, up_send, place, part_sems)
                these += send_copies(down_parts, half, y, down_keep, down_send, place, more_sems)
                start_all(these)
                copies += these
        wait_all(copies)


def back_rows(
    place, lengths, qkv, lse, dattn, xs, dx, pieces, vec, outs, dqkv, vec_out, w_qkv, bias, sems
):
    step = pl.program_id(0)
    width = vec.shape[1]
    slots = qkv.shape[0]
    pair = 2 * (width // HEADS)
    score_scale = 1.0 / math.sqrt(width // HEADS)
    copies = placements(pieces, [(0, 3 * width, w_qkv)], place, sems)

    @pl.when(step == 0)
    def _():
        vec_out[...] = jnp.zeros_like(vec_out)
        for copy in copies:
            copy.start()

    fill_bias(place, lengths, step + place[4], bias)
    masks = head_masks(pair)
    for p in range(HEADS // 2):
        at = p * pair
        qp = qkv[:, at : at + pair]
        kp = qkv[:, width + at : width + at + pair]
        vp = qkv[:, 2 * width + at : 2 * width + at + pair]
        gp = dattn[:, at : at + pair]
        k_turned = kp.T
        probs_list, ds_list, dq_list, q_list, g_list = [], [], [], [], []
        for i in range(2):
            qh = qp * masks[i]
            gh = gp * masks[i]
            scores = nt_dot(kp, qh) + bias[...]
            probs = jnp.exp(scores - lse[0, 2 * p + i : 2 * p + i + 1, :])
            dprobs = nt_dot(vp, gh)
            inner = jnp.sum(probs * dprobs, axis=0, keepdims=True)
            ds = (probs * (dprobs - inner)).astype(BF16)
            dq_list.append(nn_dot(k_turned[i * (pair // 2) : (i + 1) * (pair // 2)], ds))
            probs_list.append(probs.astype(BF16))
            ds_list.append(ds)
            q_list.append(qh)
            g_list.append(gh)
        dq = jnp.concatenate(dq_list, axis=0).T * score_scale
        dk = nn_dot(jnp.concatenate(ds_list, axis=1), jnp.concatenate(q_list, axis=0))
        dv = nn_dot(jnp.concatenate(probs_list, axis=1), jnp.concatenate(g_list, axis=0))
        dqkv[:, at : at + pair] = dq.astype(BF16)
        dqkv[:, width + at : width + at + pair] = dk.astype(BF16)
        dqkv[:, 2 * width + at : 2 * width + at + pair] = dv.astype(BF16)

    @pl.when(step == 0)
    def _():
        for copy in copies:
            copy.wait()

    dh = nt_dot(dqkv[...], w_qkv[...])
    x = load_slots(xs).astype(F32)
    unit, scale = centered(x)
    vec_out[0:1] += jnp.sum(dh * unit, axis=0, keepdims=True)
    vec_out[1:2] += jnp.sum(dh, axis=0, keepdims=True)
    grad = (dx[...] + norm_back(unit, scale, dh * vec[0:1])).astype(BF16)
    store_slots(outs, grad)


def back_first_body(
    place, lengths, qkv, lse, dattn, x0, x1, x2, x3, dx, p0, p1, p2, p3, vec,
    o0, o1, o2, o3, dqkv_out, vec_out, w_qkv, bias, sems,
):
    back_rows(
        place, lengths, qkv, lse, dattn, (x0, x1, x2, x3), dx, (p0, p1, p2, p3), vec,
        (o0, o1, o2, o3), dqkv_out, vec_out, w_qkv, bias, sems,
    )


def back_last_body(
    dims, place, lengths, qkv, lse, dattn, x0, x1, x2, x3, dx, p0, p1, p2, p3, vec, h_one, before,
    u0, u1, u2, u3,
    o0, o1, o2, o3, vec_out, keep, send, dqkv, w_qkv, bias, h_turned, parts, sems, out_sems,
):
    step = pl.program_id(0)
    slots = qkv.shape[0]
    here = pl.ds(pl.multiple_of(step * slots, slots), slots)
    back_rows(
        place, lengths, qkv, lse, dattn, (x0, x1, x2, x3), dx, (p0, p1, p2, p3), vec,
        (o0, o1, o2, o3), dqkv.at[here], vec_out, w_qkv, bias, sems,
    )

    @pl.when(step == pl.num_programs(0) - 1)
    def _():
        count = before.shape[0]
        h_turned[...] = h_one[...].T
        quarter = before.shape[1] // 4
        copies = []
        for half in range(2):
            for y in range(2):
                at = (half * 2 + y) * quarter
                value = nn_dot(h_turned[:, :count], before[:, at : at + quarter])
                value = value + nn_dot(h_turned[:, count:], dqkv[:, at : at + quarter])
                write_parts(parts, half, y, 0, value, dims)
                these = send_copies(parts, half, y, keep, send, place, out_sems)
                start_all(these)
                copies += these
        wait_all(copies)


def add_mlp_body(keep, got, down_keep, down_got, *outs):
    for k in range(4):
        outs[k][...] = (keep[k].astype(F32) + got[k].astype(F32)).astype(BF16)
        outs[4][:, k] = (down_keep[k].astype(F32) + down_got[k].astype(F32)).astype(BF16)


def add_qkv_body(keep, got, v0, v1, v2, *outs):
    rows = keep.shape[2]
    sums = v0[...] + v1[...] + v2[...]
    for k, out in enumerate(outs):
        out[:, :rows, :] = (keep[k].astype(F32) + got[k].astype(F32)).astype(BF16)
        out[:, rows:, :] = jnp.zeros((out.shape[0], 16, out.shape[2]), BF16)
        lanes = sums.shape[1] // out.shape[0]
        for h in range(out.shape[0]):
            out[h, rows:, :lanes] = sums[:, h * lanes : (h + 1) * lanes].astype(BF16)


def collect_body(place, p0, p1, p2, p3, out):
    for k, piece in enumerate((p0, p1, p2, p3)):
        out[place[2] ^ k] = piece[...]


def in_order(values, place):
    core, y = place[3], place[7]
    near = (jnp.where(y == 0, values[0], values[1]), jnp.where(y == 0, values[1], values[0]))
    far = (jnp.where(y == 0, values[2], values[3]), jnp.where(y == 0, values[3], values[2]))
    first = (jnp.where(core == 0, near[0], far[0]), jnp.where(core == 0, near[1], far[1]))
    second = (jnp.where(core == 0, far[0], near[0]), jnp.where(core == 0, far[1], near[1]))
    return (*first, *second)


def vec_sums(a0, a2, place, shard):
    lanes = 128
    own = a0[shard:, :lanes].astype(F32)
    far = a2[shard:, :lanes].astype(F32)
    both = own + far
    lane = lax.broadcasted_iota(jnp.int32, both.shape, 1) // (lanes // 2)
    return jnp.where(lane == place[8], both, 0.0)


def square_body(place, m0, m1, m2, m3, a0, a1, a2, a3, out):
    shard = m0.shape[0]
    values = []
    for mlp, attn in ((m0, a0), (m1, a1), (m2, a2), (m3, a3)):
        big = mlp[...].astype(F32)
        small = attn[:shard].astype(F32)
        values.append(jnp.sum(big * big) + jnp.sum(small * small))
    vec = vec_sums(a0, a2, place, shard)
    first, second, third, fourth = in_order(values, place)
    value = ((first + second) + (third + fourth)) + jnp.sum(vec * vec)
    out[...] = jnp.full(out.shape, value, F32)


def adam_parts(weight, moment, second, grad, decay, rate):
    moment_new = BETA_ONE * moment + (1.0 - BETA_ONE) * grad
    second_new = BETA_TWO * second + (1.0 - BETA_TWO) * grad * grad
    first_hat = moment_new * (1.0 / (1.0 - BETA_ONE**ADAM_STEP))
    second_hat = second_new * (1.0 / (1.0 - BETA_TWO**ADAM_STEP))
    step = first_hat / (jnp.sqrt(second_hat) + ADAM_EPS)
    return weight - rate * (step + decay * weight), moment_new, second_new


def adam_body(
    place, squares, m0, m1, m2, m3, a0, a1, a2, a3,
    attn_w, attn_m, attn_v, mlp_w, mlp_m, mlp_v, vec_w, vec_m, vec_v,
    norm_out, attn_wo, attn_mo, attn_vo, mlp_wo, mlp_mo, mlp_vo, vec_wo, vec_mo, vec_vo,
):
    shard = m0.shape[0]
    hidden = mlp_w.shape[2]
    quarter = hidden // 4
    wide = a0.shape[1]
    small = m0.shape[1] - 2 * quarter
    value = squares[0]
    for d in range(1, squares.shape[0]):
        value = value + squares[d]
    norm = jnp.sqrt(value)
    norm_out[...] = norm[0:1, 0:1]
    factor = (CLIP_NORM / jnp.maximum(norm, CLIP_NORM))[0:1, 0:1]
    rows, cols = vec_w.shape
    vec = vec_sums(a0, a2, place, shard)
    grad = (vec[:rows, :cols] + vec[:rows, cols : 2 * cols]) * factor
    parts = adam_parts(vec_w[...], vec_m[...], vec_v[...], grad, 0.0, VEC_RATE)
    for new, new_value in zip((vec_wo, vec_mo, vec_vo), parts):
        new[...] = new_value
    core, y = place[3], place[7]
    olds = (attn_w, attn_m, attn_v)
    news = (attn_wo, attn_mo, attn_vo)
    mlp_olds = (mlp_w, mlp_m, mlp_v)
    mlp_news = (mlp_wo, mlp_mo, mlp_vo)
    for i, (mlp, attn) in enumerate(((m0, a0), (m1, a1), (m2, a2), (m3, a3))):
        side = (core if i < 2 else 1 - core) * 2 + (y if i % 2 == 0 else 1 - y)

        def columns(base, size, side=side):
            return pl.ds(pl.multiple_of(base + side * size, 128), size)

        at = columns(0, wide)
        grad = attn[:shard].astype(F32) * factor
        for new, new_value in zip(news, adam_parts(*[o[:, at] for o in olds], grad, WEIGHT_DECAY, LEARN_RATE)):
            new[:, at] = new_value
        at = columns(4 * wide, small)
        grad = mlp[:, quarter : quarter + small].astype(F32) * factor
        for new, new_value in zip(news, adam_parts(*[o[:, at] for o in olds], grad, WEIGHT_DECAY, LEARN_RATE)):
            new[:, at] = new_value
        at = columns(0, quarter)
        for j, start in ((0, 0), (1, quarter + small)):
            grad = mlp[:, start : start + quarter].astype(F32) * factor
            parts = adam_parts(*[o[j, :, at] for o in mlp_olds], grad, WEIGHT_DECAY, LEARN_RATE)
            for new, new_value in zip(mlp_news, parts):
                new[j, :, at] = new_value


def shape_of(dims, dtype):
    return jax.ShapeDtypeStruct(dims, dtype)


def rows_spec(rows, cols):
    return pl.BlockSpec((rows, cols), lambda r: (r, 0))


def whole_spec(shape):
    return pl.BlockSpec(shape, lambda r: (0,) * len(shape))


def call(body, grid, in_specs, out_specs, out_shape, scratch, cost, name, aliases=None):
    return pl.pallas_call(
        body,
        grid=(grid,),
        in_specs=in_specs,
        out_specs=out_specs,
        out_shape=out_shape,
        scratch_shapes=scratch,
        input_output_aliases=aliases or {},
        compiler_params=pltpu.CompilerParams(
            vmem_limit_bytes=VMEM_BYTES, dimension_semantics=("arbitrary",)
        ),
        cost_estimate=pl.CostEstimate(
            flops=int(cost * 1e9), bytes_accessed=int(cost * 2e6), transcendentals=0
        ),
        name=name,
    )


def swap(value, axis):
    return lax.ppermute(value, axis, [(0, 1), (1, 0)])


def ordered(own, other, index, axis):
    first = jnp.where(index == 0, own, other)
    second = jnp.where(index == 0, other, own)
    return jnp.stack([first, second], axis)


def from_seq(pieces):
    moved = [pieces[0]]
    for k in range(1, 4):
        moved.append(lax.ppermute(pieces[k], ("y", "core"), [(j, j ^ k) for j in range(4)]))
    return moved


def spread_hi(half):
    hi_count = lax.axis_size("hi")
    spread = jnp.broadcast_to(half[None], (hi_count, *half.shape))
    return lax.all_to_all(spread, "hi", 0, 0)


def share(own):
    other = swap(own, "lo")
    return [own, other, swap(own, "core"), swap(other, "core")]


def settle(pieces, lo, core, groups=4):
    near = ordered(pieces[0], pieces[1], lo, 1)
    far = ordered(pieces[2], pieces[3], lo, 1)
    whole = ordered(near, far, core, 2)
    cols = whole.shape[-1]
    whole = whole.reshape(groups, 2, 2, -1, cols)
    return [whole[:, 0, 0], whole[:, 1, 0], whole[:, 0, 1], whole[:, 1, 1]]


def add_pair(keep, got):
    return (keep.astype(F32) + got.astype(F32)).astype(BF16)


def spread_plane(part):
    part = part.reshape(4, *part.shape[2:])
    return lax.all_to_all(part, ("lo", "y"), 0, 0)


def total(part):
    return jnp.sum(part.astype(F32), axis=0).astype(BF16)


def to_all(mine):
    return [mine] + [
        lax.ppermute(mine, ("y", "core"), [(j, j ^ k) for j in range(4)]) for k in (2, 1, 3)
    ]


def after(value, *others):
    return lax.optimization_barrier((value, *others))[0]


def in_columns(pieces, y, core):
    near = ordered(pieces[0], pieces[1], y, 1)
    far = ordered(pieces[2], pieces[3], y, 1)
    both = ordered(near, far, core, 1)
    return both.reshape(both.shape[0], -1).astype(F32)


def adam_update(weight, moment, second, grad, decay, rate):
    moment_new = BETA_ONE * moment + (1.0 - BETA_ONE) * grad
    second_new = BETA_TWO * second + (1.0 - BETA_TWO) * grad * grad
    first_hat = moment_new / (1.0 - BETA_ONE**ADAM_STEP)
    second_hat = second_new / (1.0 - BETA_TWO**ADAM_STEP)
    weight_new = weight - rate * (first_hat / (jnp.sqrt(second_hat) + ADAM_EPS) + decay * weight)
    return (weight_new, moment_new, second_new)


def on_device(
    tokens, cotangent, lengths, attn_w, attn_m, attn_v, mlp_w, mlp_m, mlp_v, vec_w, vec_m, vec_v
):
    lo = lax.axis_index("lo")
    y = lax.axis_index("y")
    core = lax.axis_index("core")
    hi_count = lax.axis_size("hi")
    me = y * 2 + core
    micro_count, row_count, part, width = tokens.shape
    hidden = mlp_w.shape[2]
    shard = attn_w.shape[0]
    slots = 4 * part
    rows = micro_count * row_count // 4
    count = rows * slots
    vec_rows, vec_cols = vec_w.shape
    half_rows = shard // 2
    fits = half_rows % 16 == 0

    flat_tokens = tokens.reshape(4, rows, part, width)
    flat_cot = cotangent.reshape(4, rows, part, width)

    def pick(stack, k):
        return lax.dynamic_index_in_dim(stack, me ^ k, 0, keepdims=False)

    def half_of(value):
        return lax.dynamic_slice_in_dim(value, core * half_rows, half_rows, 0)

    xs = from_seq([pick(flat_tokens, k) for k in range(4)])
    lanes = 128
    ride = jnp.pad(vec_w.reshape(-1), (0, half_rows * lanes - vec_w.size)).reshape(half_rows, lanes)
    first_half = jnp.concatenate([half_of(attn_w[:, : 3 * width]), ride], axis=1).astype(BF16)
    qkv_own = spread_hi(first_half)
    up_half = jnp.concatenate([half_of(attn_w[:, 3 * width :]), half_of(mlp_w[0])], axis=1)
    up_own = spread_hi(after(up_half.astype(BF16), qkv_own))
    qkv_own, xs[3] = lax.optimization_barrier((qkv_own, xs[3]))
    qkv_other = swap(qkv_own, "lo")
    qkv_pieces = [qkv_own, qkv_other, swap(qkv_own, "core"), swap(qkv_other, "core")]
    vec_all = ordered(qkv_pieces[0][:, :, 3 * width :], qkv_pieces[1][:, :, 3 * width :], lo, 1)
    vec_all = vec_all.reshape(2 * hi_count, -1)[:, : vec_w.size].reshape(-1, vec_rows, vec_cols)
    vec_all = vec_all.transpose(1, 0, 2).reshape(vec_rows, width)
    vec_float = jnp.pad(vec_all.astype(F32), ((0, 16 - vec_rows), (0, 0)))

    if fits:
        places = [lo, core, me, core, 0 * lo, lo, y, y, lo]
        dims = (hi_count, 2, shard)
    else:
        qkv_pieces = settle(qkv_pieces, lo, core)
        places = [0 * lo, 0 * lo, me, core, 0 * lo, 0 * lo, 0 * lo, y, lo]
        dims = (1, 1, width)
    place = jnp.stack(places).astype(jnp.int32)
    later = place.at[4].set(rows // 2)
    row_lengths = lax.dynamic_slice_in_dim(lengths.reshape(-1), me * rows, rows)

    vec_spec = whole_spec((16, width))
    lse_spec = pl.BlockSpec((1, HEADS, slots), lambda r: (r, 0, 0))
    group = 2 if rows % 2 == 0 else 1
    slot_spec = pl.BlockSpec((group, part, width), lambda r: (r, 0, 0))
    narrow = rows_spec(group * slots, width)
    wide_qkv = rows_spec(group * slots, 3 * width)
    triple = rows_spec(slots, 3 * width)
    n_piece = 4 * qkv_pieces[0].shape[0]
    dma = pltpu.SemaphoreType.DMA
    h_one, qkv = call(
        qkv_body,
        rows // group,
        [SMEM, *[slot_spec] * 4, *[ANY] * 4, vec_spec],
        [narrow, wide_qkv],
        [shape_of((count, width), BF16), shape_of((count, 3 * width), BF16)],
        [pltpu.VMEM((width, 3 * width), BF16), dma((n_piece,))],
        7,
        "qkv",
    )(place, *xs, *qkv_pieces, vec_float)

    down_half = after(half_of(mlp_w[1]).astype(BF16), qkv_other)
    down_pair = jnp.stack(lax.optimization_barrier((down_half, swap(down_half, "lo"), h_one))[:2])
    down_own = spread_hi(after(down_pair, up_own))
    cot, qkv, up_own = lax.optimization_barrier((flat_cot, qkv, up_own))
    dys = from_seq([pick(cot, k) for k in range(4)])
    up_other = swap(up_own, "lo")

    def half_spec(block, base):
        zeros = (0,) * (len(block) - 1)
        return pl.BlockSpec(block, lambda r: (r + base, *zeros))

    def attend(qkv, base, steps, before):
        return call(
            attend_body,
            steps,
            [SMEM, SMEM, half_spec((slots, 3 * width), base), *[ANY] * len(before)],
            [half_spec((slots, width), base), half_spec((1, HEADS, slots), base)],
            [shape_of((count, width), BF16), shape_of((rows, HEADS, slots), F32)],
            [pltpu.VMEM((slots, slots), F32)],
            4 * steps,
            "attend",
            {3: 0, 4: 1} if before else None,
        )(place.at[4].set(base), row_lengths, qkv, *before)

    up_far = swap(up_own, "core")
    attn, lse = attend(qkv, 0, rows - 1, [])
    up_other, up_far, attn, lse, *dys = lax.optimization_barrier(
        (up_other, up_far, attn, lse, *dys)
    )
    attn, lse = attend(qkv, rows - 1, 1, [attn, lse])
    up_pieces = [up_own, up_other, up_far, swap(up_other, "core")]
    down_own = after(down_own, attn)
    down_far = swap(down_own, "core")
    down_pieces = [down_own, down_far]
    if not fits:
        up_pieces = settle(up_pieces, lo, core)
        split = settle([p[:, j] for p in down_pieces for j in range(2)], lo, core)
        down_pieces = [jnp.stack(split[:2], axis=1), jnp.stack(split[2:], axis=1)]
    n_down = 4 * down_pieces[0].shape[0]

    def parts_shape(quarter):
        return (dims[1], 2, dims[0], dims[2], quarter)

    def in_dp_order(value):
        if fits:
            return value
        value = value.reshape(2, hi_count, 2, shard, value.shape[-1])
        return value.transpose(2, 0, 1, 3, 4)

    turned = pltpu.VMEM((width, count), BF16)
    shape = parts_shape(hidden // 4 + width // 4)
    down_shape = parts_shape(hidden // 4)
    outs = call(
        functools.partial(mlp_body, dims),
        rows // group,
        [SMEM, *[slot_spec] * 4, narrow, *[slot_spec] * 4, *[ANY] * 6, vec_spec],
        [*[slot_spec] * 4, narrow, narrow, vec_spec, *[ANY] * 4],
        [
            *[shape_of((rows, part, width), BF16)] * 4,
            shape_of((count, width), F32),
            shape_of((count, width), BF16),
            shape_of((16, width), F32),
            *[shape_of(shape, BF16)] * 2,
            *[shape_of(down_shape, BF16)] * 2,
        ],
        [
            pltpu.VMEM((width, width), BF16),
            pltpu.VMEM((width, hidden), BF16),
            pltpu.VMEM((width, hidden), BF16),
            turned,
            turned,
            turned,
            pltpu.VMEM((count, hidden), BF16),
            pltpu.VMEM((count, hidden), BF16),
            pltpu.VMEM((count, width), BF16),
            pltpu.VMEM((2, *shape), BF16),
            pltpu.VMEM((2, *down_shape), BF16),
            dma((n_piece,)),
            dma((n_piece,)),
            dma((n_down,)),
            dma((2, dims[1], 2)),
            dma((2, dims[1], 2)),
        ],
        24,
        "mlp",
    )(place, *xs, attn, *dys, *up_pieces, *down_pieces, vec_float)
    results, (dx, dattn, vec_mlp, up_keep, up_send, down_keep, down_send) = outs[:4], outs[4:]
    up_got = swap(up_send, "core")
    down_got = swap(down_send, "core")

    def collect(parts):
        return call(
            collect_body,
            1,
            [SMEM, *[whole_spec(parts[0].shape)] * 4],
            whole_spec((4, *parts[0].shape)),
            shape_of((4, *parts[0].shape), BF16),
            [],
            2,
            "collect",
        )(place, *parts).reshape(tokens.shape)

    results = from_seq(results)
    lead = 2
    lead_count = lead * slots
    back_args = [lse, dattn, *xs, dx]
    weights = [*qkv_pieces, vec_float]

    def back_specs(base):
        return [
            SMEM,
            SMEM,
            half_spec((slots, 3 * width), base),
            half_spec((1, HEADS, slots), base),
            half_spec((slots, width), base),
            *[half_spec((1, part, width), base)] * 4,
            half_spec((slots, width), base),
            *[ANY] * 4,
            vec_spec,
        ]

    back_shapes = [shape_of((rows, part, width), BF16)] * 4
    back_scratch = [pltpu.VMEM((width, 3 * width), BF16), pltpu.VMEM((slots, slots), F32)]
    outs = call(
        back_first_body,
        lead,
        back_specs(0),
        [*[half_spec((1, part, width), 0)] * 4, triple, vec_spec],
        [*back_shapes, shape_of((lead_count, 3 * width), BF16), shape_of((16, width), F32)],
        [*back_scratch, dma((n_piece,))],
        11,
        "back_first",
    )(place, row_lengths, after(qkv, up_send, down_send), *back_args, *weights)
    input_first, (grad_first, vec_first) = outs[:4], outs[4:]

    def add_call(body, args, outs):
        args = [a.reshape(4, *a.shape[2:]) if a.ndim > 2 else a for a in args]
        return call(
            body,
            1,
            [whole_spec(a.shape) for a in args],
            [whole_spec(o.shape) for o in outs],
            outs,
            [],
            3,
            "add",
        )(*args)

    def plane_sum(parts):
        moved = [parts[0]]
        for k in (2, 1, 3):
            perm = [(j, j ^ k) for j in range(4)]
            moved.append(lax.ppermute(parts[k], ("lo", "y"), perm))
        return moved

    def add_moved(moved):
        value = (moved[0].astype(F32) + moved[1].astype(F32)) + moved[2].astype(F32)
        return (value + moved[3].astype(F32)).astype(BF16)

    def plane_total(keep, got, extra):
        part = in_dp_order(add_pair(keep, got))
        if extra is not None:
            part = jnp.concatenate([part, extra], axis=3)
        return total(spread_plane(part))

    qkv_last = qkv
    output = collect(results)
    if fits:
        args = [up_keep, up_got, down_keep, down_got]
        args = lax.optimization_barrier((*args, grad_first, *results))[:4]
        piece = shape_of(up_keep.shape[2:], BF16)
        by_hi = shape_of((hi_count, 4, *down_keep.shape[3:]), BF16)
        *parts, down_part = add_call(add_mlp_body, args, [*[piece] * 4, by_hi])
        qkv_last = after(qkv, *parts, down_part)
        up_moved = plane_sum(parts)
        down_part = total(lax.all_to_all(down_part, "hi", 0, 0))
    quarter = 3 * width // 4
    shape = parts_shape(quarter)
    outs = call(
        functools.partial(back_last_body, dims),
        rows - lead,
        [
            *back_specs(lead),
            whole_spec((count, width)),
            whole_spec((lead_count, 3 * width)),
            *[ANY] * 4,
        ],
        [*[half_spec((1, part, width), lead)] * 4, vec_spec, ANY, ANY],
        [*back_shapes, shape_of((16, width), F32), shape_of(shape, BF16), shape_of(shape, BF16)],
        [
            pltpu.VMEM((count - lead_count, 3 * width), BF16),
            *back_scratch,
            turned,
            pltpu.VMEM((2, *shape), BF16),
            dma((n_piece,)),
            dma((2, dims[1], 2)),
        ],
        13,
        "back_last",
        {17 + k: k for k in range(4)},
    )(place.at[4].set(lead), row_lengths, qkv_last, *back_args, *weights, h_one, grad_first, *input_first)
    input_parts, (vec_last, qkv_keep, qkv_send) = outs[:4], outs[4:]
    if fits:
        qkv_send = after(qkv_send, *up_moved)
    qkv_got = swap(qkv_send, "core")
    vecs = [vec_mlp, vec_first, vec_last]

    if fits:
        _, _, _, more_rows, more_cols = qkv_keep.shape
        piece = shape_of((hi_count, more_rows + 16, more_cols), BF16)
        parts = add_call(add_qkv_body, [qkv_keep, qkv_got, *vecs], [piece] * 4)
        qkv_moved = plane_sum(parts)
        down_moved = plane_sum([down_part[k] for k in range(4)])
        up_plane = after(add_moved(up_moved), *parts)
        up_mine = total(lax.all_to_all(up_plane, "hi", 0, 0))
        qkv_mine = total(lax.all_to_all(add_moved(qkv_moved), "hi", 0, 0))
        down_mine = add_moved(down_moved)
    else:
        vec_total = (vec_mlp + vec_first + vec_last).reshape(16, hi_count, 2, vec_cols)
        vec_total = vec_total.transpose(1, 0, 2, 3).reshape(1, 1, hi_count, 16, 2 * vec_cols)
        vec_total = jnp.pad(vec_total.astype(BF16), ((0, 0),) * 4 + ((0, quarter - 2 * vec_cols),))
        vec_total = jnp.broadcast_to(vec_total, (2, 2, *vec_total.shape[2:]))
        up_mine = total(lax.all_to_all(plane_total(up_keep, up_got, None), "hi", 0, 0))
        down_mine = total(lax.all_to_all(plane_total(down_keep, down_got, None), "hi", 0, 0))
        qkv_mine = plane_total(qkv_keep, qkv_got, vec_total)
        qkv_mine = total(lax.all_to_all(qkv_mine, "hi", 0, 0))
    mlp_mine = jnp.concatenate([up_mine, down_mine], axis=1)
    mlp_pieces = to_all(mlp_mine)
    attn_pieces = to_all(after(qkv_mine, *mlp_pieces))
    input_grad = collect(from_seq(lax.optimization_barrier((*input_parts, *attn_pieces))[:4]))

    dp_count = 2 * hi_count
    if fits:
        pieces = [*mlp_pieces, *attn_pieces]
        piece_specs = [whole_spec(p.shape) for p in pieces]
        squares_shape = (dp_count, 8, 128)
        squares = call(
            square_body,
            1,
            [SMEM, *piece_specs],
            whole_spec(squares_shape),
            shape_of(squares_shape, F32),
            [],
            2,
            "squares",
        )(place, *pieces)
        squares = lax.all_to_all(squares, ("hi", "lo"), 0, 0)
        states = [attn_w, attn_m, attn_v, mlp_w, mlp_m, mlp_v, vec_w, vec_m, vec_v]
        state_specs = [whole_spec(v.shape) for v in states]
        norm, *new = call(
            adam_body,
            1,
            [SMEM, whole_spec(squares_shape), *piece_specs, *state_specs],
            [whole_spec((1, 1)), *state_specs],
            [shape_of((1, 1), F32), *[shape_of(v.shape, F32) for v in states]],
            [],
            6,
            "adam",
        )(place, squares, *pieces, *states)
        return (output, input_grad, *new, norm.reshape(()))

    vec_sum = attn_pieces[0][shard:].astype(F32) + attn_pieces[2][shard:].astype(F32)
    vec_sum = jnp.where(lo == 0, vec_sum[:, :vec_cols], vec_sum[:, vec_cols : 2 * vec_cols])
    vec_sum = vec_sum[:vec_rows]
    up_at = hidden // 4
    out_at = up_at + width // 4
    up_sum = in_columns([p[:, :up_at] for p in mlp_pieces], y, core)
    out_sum = in_columns([p[:, up_at:out_at] for p in mlp_pieces], y, core)
    down_sum = in_columns([p[:, out_at:] for p in mlp_pieces], y, core)
    qkv_sum = in_columns([p[:shard] for p in attn_pieces], y, core)
    attn_sum = jnp.concatenate([qkv_sum, out_sum], axis=1)
    mlp_sum = jnp.stack([up_sum, down_sum])
    square = jnp.sum(attn_sum * attn_sum) + jnp.sum(mlp_sum * mlp_sum) + jnp.sum(vec_sum * vec_sum)
    squares = lax.all_to_all(jnp.full((dp_count, 8, 128), square), ("hi", "lo"), 0, 0)
    grad_norm = jnp.sqrt(jnp.sum(squares[:, 0, 0]))
    clip_factor = CLIP_NORM / jnp.maximum(grad_norm, CLIP_NORM)
    attn_new = adam_update(
        attn_w, attn_m, attn_v, attn_sum * clip_factor, WEIGHT_DECAY, LEARN_RATE
    )
    mlp_new = adam_update(mlp_w, mlp_m, mlp_v, mlp_sum * clip_factor, WEIGHT_DECAY, LEARN_RATE)
    vec_new = adam_update(vec_w, vec_m, vec_v, vec_sum * clip_factor, 0.0, VEC_RATE)
    return (output, input_grad, *attn_new, *mlp_new, *vec_new, grad_norm)


def solution(mesh):
    dp_count = mesh.shape["dp"]
    seq_count = mesh.shape["seq"]
    fine = jax.sharding.Mesh(
        mesh.devices.reshape(dp_count // 2, 2, seq_count // 2, 2), ("hi", "lo", "y", "core")
    )
    dp = ("hi", "lo")
    seq = ("y", "core")
    acts = P(None, dp, seq, None)
    attn = P(dp, None)
    mlp = P(None, dp, None)
    vec = P(None, dp)
    return jax.shard_map(
        on_device,
        mesh=fine,
        in_specs=(acts, acts, P(None, dp), attn, attn, attn, mlp, mlp, mlp, vec, vec, vec),
        out_specs=(acts, acts, attn, attn, attn, mlp, mlp, mlp, vec, vec, vec, P()),
        check_vma=False,
    )
```

```python
import functools
import math

import jax
import jax.numpy as jnp
from jax import lax
from jax.experimental import pallas as pl
from jax.experimental.pallas import tpu as pltpu
from jax.sharding import PartitionSpec as P

HEADS = 8
ADAM_STEP = 10
CLIP_NORM = 1.0
BETA_ONE = 0.9
BETA_TWO = 0.999
LEARN_RATE = 0.08
VEC_RATE = 0.4
WEIGHT_DECAY = 0.01
ADAM_EPS = 1e-08
NORM_EPS = 1e-05
VMEM_BYTES = 63 * 1024 * 1024

F32 = jnp.float32
BF16 = jnp.bfloat16
ANY = pl.BlockSpec(memory_space=pl.ANY)
SMEM = pl.BlockSpec(memory_space=pltpu.SMEM)


def nt_dot(left, right):
    return lax.dot_general(left, right, (((1,), (1,)), ((), ())), preferred_element_type=F32)


def nn_dot(left, right):
    return jnp.dot(left, right, preferred_element_type=F32)


def centered(values):
    center = values - jnp.mean(values, axis=-1, keepdims=True)
    spread = jnp.mean(center * center, axis=-1, keepdims=True)
    scale = lax.rsqrt(spread + NORM_EPS)
    return center * scale, scale


def norm_back(unit, scale, grad):
    mean_grad = jnp.mean(grad, axis=-1, keepdims=True)
    mean_both = jnp.mean(grad * unit, axis=-1, keepdims=True)
    return scale * (grad - mean_grad - unit * mean_both)


def gelu_and_slope(up):
    share = 0.5 + 0.5 * lax.erf(up * (1.0 / math.sqrt(2.0)))
    bell = jnp.exp2(up * up * (-0.5 * math.log2(math.e)))
    return up * share, share + up * (bell * (1.0 / math.sqrt(2.0 * math.pi)))


def load_slots(refs):
    return jnp.concatenate([ref[i] for i in range(refs[0].shape[0]) for ref in refs], axis=0)


def store_slots(refs, value):
    rows, part, _ = refs[0].shape
    for i in range(rows):
        for k, ref in enumerate(refs):
            at = (i * 4 + k) * part
            ref[i] = value[at : at + part]


def placements(pieces, jobs, place, sems):
    lo = place[0]
    core = place[1]
    copies = []
    for i, piece in enumerate(pieces):
        lo_at = lo if i % 2 == 0 else 1 - lo
        core_at = core if i < 2 else 1 - core
        hi_count, rows, _ = piece.shape
        for h in range(hi_count):
            row = pl.multiple_of(((h * 2 + lo_at) * 2 + core_at) * rows, rows)
            for column, width, target, at in jobs:
                copies.append(
                    pltpu.make_async_copy(
                        piece.at[h, :, pl.ds(column, width)],
                        target.at[pl.ds(row, rows), pl.ds(at, width)],
                        sems.at[len(copies)],
                    )
                )
    return copies


def pair_placements(pieces, target, place, sems):
    copies = []
    for i, piece in enumerate(pieces):
        core_at = place[1] if i == 0 else 1 - place[1]
        hi_count, _, rows, _ = piece.shape
        for h in range(hi_count):
            for j in range(2):
                row = pl.multiple_of(((h * 2 + (place[0] ^ j)) * 2 + core_at) * rows, rows)
                copies.append(
                    pltpu.make_async_copy(
                        piece.at[h, j],
                        target.at[pl.ds(row, rows), pl.ds(0, piece.shape[-1])],
                        sems.at[len(copies)],
                    )
                )
    return copies


def head_masks(width):
    lane = lax.broadcasted_iota(jnp.int32, (1, width), 1)
    first = jnp.where(lane < width // 2, 1.0, 0.0)
    return first.astype(BF16), (1.0 - first).astype(BF16)


def fill_bias(place, lengths, row, bias):
    part = bias.shape[0] // 4
    for k in range(4):
        base = (place[2] ^ k) * part
        slot = lax.broadcasted_iota(jnp.int32, (part, bias.shape[1]), 0) + base
        bias[k * part : (k + 1) * part, :] = jnp.where(slot < lengths[row], 0.0, -1e30)


def qkv_body(place, x0, x1, x2, x3, p0, p1, p2, p3, vec, h_out, qkv_out, w_qkv, sems):
    row = pl.program_id(0)
    width = vec.shape[1]
    copies = placements((p0, p1, p2, p3), [(0, 3 * width, w_qkv, 0)], place, sems)

    @pl.when(row == 0)
    def _():
        for copy in copies:
            copy.start()

    x = load_slots((x0, x1, x2, x3)).astype(F32)
    unit, _ = centered(x)
    h = (unit * vec[0:1] + vec[1:2]).astype(BF16)
    h_out[...] = h

    @pl.when(row == 0)
    def _():
        for copy in copies:
            copy.wait()

    q = nn_dot(h, w_qkv[:, :width]).astype(BF16)
    qkv_out[:, :width] = q * jnp.asarray(1.0 / math.sqrt(width // HEADS), BF16)
    qkv_out[:, width:] = nn_dot(h, w_qkv[:, width:]).astype(BF16)


def attend_body(place, lengths, qkv, *refs):
    attn_out, lse_out, bias = refs[-3:]
    row = pl.program_id(0) + place[4]
    width = attn_out.shape[1]
    pair = 2 * (width // HEADS)
    fill_bias(place, lengths, row, bias)
    masks = head_masks(pair)
    for p in range(HEADS // 2):
        at = p * pair
        qp = qkv[:, at : at + pair]
        kp = qkv[:, width + at : width + at + pair]
        v_turned = qkv[:, 2 * width + at : 2 * width + at + pair].T
        outs = []
        for i in range(2):
            scores = nt_dot(kp, qp * masks[i]) + bias[...]
            top = jnp.max(scores, axis=0, keepdims=True)
            grown = jnp.exp(scores - top)
            total = jnp.sum(grown, axis=0, keepdims=True)
            lse_out[0, 2 * p + i : 2 * p + i + 1, :] = top + jnp.log(total)
            probs = (grown * (1.0 / total)).astype(BF16)
            outs.append(nn_dot(v_turned[i * (pair // 2) : (i + 1) * (pair // 2)], probs))
        attn_out[:, at : at + pair] = jnp.concatenate(outs, axis=0).T.astype(BF16)


def write_parts(parts, half, y, column, value, dims):
    hi_count, lo_count, rows = dims
    quarter = value.shape[1]
    value = value.astype(BF16)
    for h in range(hi_count):
        for lo in range(lo_count):
            at = (h * lo_count + lo) * rows
            parts[half, lo, y, h, :, column : column + quarter] = value[at : at + rows]


def send_copies(parts, half, y, keep, send, place, sems):
    mine = half == place[3]
    copies = []
    for i in range(parts.shape[1]):
        for target, wanted in ((keep, mine), (send, jnp.logical_not(mine))):
            lo_count = parts.shape[1]
            copy = pltpu.make_async_copy(
                parts.at[half, i, y],
                target.at[(place[5] ^ i) if lo_count > 1 else 0, place[6] ^ y],
                sems.at[half, i, y],
            )
            copies.append((wanted, copy))
    return copies


def start_all(copies):
    for wanted, copy in copies:
        pl.when(wanted)(copy.start)


def wait_all(copies):
    for wanted, copy in copies:
        pl.when(wanted)(copy.wait)


def mlp_body(
    dims, place, x0, x1, x2, x3, attn, d0, d1, d2, d3, b0, b1, b2, b3, c0, c1, vec,
    o0, o1, o2, o3, dx_out, dattn_out, vec_out, up_keep, up_send, down_keep, down_send,
    w_out, w_up, w_down, h_turned, attn_turned, dy_turned, act_all, dup_all, dao_all,
    up_parts, down_parts, out_sems, up_sems, down_sems, part_sems, more_sems,
):
    row = pl.program_id(0)
    width = vec.shape[1]
    hidden = w_up.shape[1]
    slots = attn.shape[0]
    out_copies = placements((b0, b1, b2, b3), [(0, width, w_out, 0)], place, out_sems)
    split = c0.shape[-1]
    jobs = [(width, hidden, w_up, 0), (width + hidden, hidden - split, w_down, split)]
    up_copies = placements((b0, b1, b2, b3), jobs, place, up_sems)
    down_copies = pair_placements((c0, c1), w_down, place, down_sems)

    def arrived(copies):
        @pl.when(row == 0)
        def _():
            for copy in copies:
                copy.wait()

    @pl.when(row == 0)
    def _():
        vec_out[...] = jnp.zeros_like(vec_out)
        for copy in out_copies + up_copies + down_copies:
            copy.start()

    here = pl.ds(pl.multiple_of(row * slots, slots), slots)
    x = load_slots((x0, x1, x2, x3)).astype(F32)
    dy = load_slots((d0, d1, d2, d3))
    dy_turned[:, here] = dy.T
    attn_turned[:, here] = attn[...].T
    arrived(out_copies)
    x_one = x + (nn_dot(attn[...], w_out[...]) + vec[4:5])
    unit, scale = centered(x_one)
    h = (unit * vec[2:3] + vec[3:4]).astype(BF16)
    h_turned[:, here] = h.T
    arrived(up_copies)
    arrived(down_copies)
    for j in range(hidden // width):
        columns = slice(j * width, (j + 1) * width)
        up = nn_dot(h, w_up[:, columns]) + vec[6 + j : 7 + j]
        act, slope = gelu_and_slope(up)
        act_all[here, columns] = act.astype(BF16)
        dup = (slope * nn_dot(dy, w_down[:, columns])).astype(BF16)
        dup_all[here, columns] = dup
        vec_out[6 + j : 7 + j] += jnp.sum(dup.astype(F32), axis=0, keepdims=True)
    result = x_one + (nt_dot(act_all[here, :], w_down[...]) + vec[5:6])
    store_slots((o0, o1, o2, o3), result.astype(BF16))
    dh = nt_dot(dup_all[here, :], w_up[...])
    vec_out[2:3] += jnp.sum(dh * unit, axis=0, keepdims=True)
    vec_out[3:4] += jnp.sum(dh, axis=0, keepdims=True)
    dy_float = dy.astype(F32)
    dx = dy_float + norm_back(unit, scale, dh * vec[2:3])
    dx_out[...] = dx
    dao = dx.astype(BF16)
    dao_all[here, :] = dao
    vec_out[4:5] += jnp.sum(dao.astype(F32), axis=0, keepdims=True)
    vec_out[5:6] += jnp.sum(dy_float, axis=0, keepdims=True)
    dattn_out[...] = nt_dot(dao, w_out[...]).astype(BF16)

    @pl.when(row == pl.num_programs(0) - 1)
    def _():
        quarter = hidden // 4
        small = width // 4
        copies = []
        for half in range(2):
            for y in range(2):
                at = (half * 2 + y) * quarter
                value = nn_dot(h_turned[...], dup_all[:, at : at + quarter])
                write_parts(up_parts, half, y, 0, value, dims)
                value = nn_dot(dy_turned[...], act_all[:, at : at + quarter])
                write_parts(down_parts, half, y, 0, value, dims)
                at = (half * 2 + y) * small
                value = nn_dot(attn_turned[...], dao_all[:, at : at + small])
                write_parts(up_parts, half, y, quarter, value, dims)
                these = send_copies(up_parts, half, y, up_keep, up_send, place, part_sems)
                these += send_copies(down_parts, half, y, down_keep, down_send, place, more_sems)
                start_all(these)
                copies += these
        wait_all(copies)


def back_rows(
    place, lengths, qkv, lse, dattn, xs, dx, pieces, vec, sums, outs, dqkv, vec_out, w_qkv, bias, sems
):
    step = pl.program_id(0)
    width = vec.shape[1]
    slots = qkv.shape[0]
    pair = 2 * (width // HEADS)
    score_scale = 1.0 / math.sqrt(width // HEADS)
    copies = placements(pieces, [(0, 3 * width, w_qkv, 0)], place, sems)

    @pl.when(step == 0)
    def _():
        vec_out[...] = sums[...]
        for copy in copies:
            copy.start()

    fill_bias(place, lengths, step + place[4], bias)
    masks = head_masks(pair)
    for p in range(HEADS // 2):
        at = p * pair
        qp = qkv[:, at : at + pair]
        kp = qkv[:, width + at : width + at + pair]
        vp = qkv[:, 2 * width + at : 2 * width + at + pair]
        gp = dattn[:, at : at + pair]
        k_turned = kp.T
        probs_list, ds_list, dq_list, q_list, g_list = [], [], [], [], []
        for i in range(2):
            qh = qp * masks[i]
            gh = gp * masks[i]
            scores = nt_dot(kp, qh) + bias[...]
            probs = jnp.exp(scores - lse[0, 2 * p + i : 2 * p + i + 1, :])
            dprobs = nt_dot(vp, gh)
            inner = jnp.sum(probs * dprobs, axis=0, keepdims=True)
            ds = (probs * (dprobs - inner)).astype(BF16)
            dq_list.append(nn_dot(k_turned[i * (pair // 2) : (i + 1) * (pair // 2)], ds))
            probs_list.append(probs.astype(BF16))
            ds_list.append(ds)
            q_list.append(qh)
            g_list.append(gh)
        dq = jnp.concatenate(dq_list, axis=0).T * score_scale
        dk = nn_dot(jnp.concatenate(ds_list, axis=1), jnp.concatenate(q_list, axis=0))
        dv = nn_dot(jnp.concatenate(probs_list, axis=1), jnp.concatenate(g_list, axis=0))
        dqkv[:, at : at + pair] = dq.astype(BF16)
        dqkv[:, width + at : width + at + pair] = dk.astype(BF16)
        dqkv[:, 2 * width + at : 2 * width + at + pair] = dv.astype(BF16)

    @pl.when(step == 0)
    def _():
        for copy in copies:
            copy.wait()

    dh = nt_dot(dqkv[...], w_qkv[...])
    x = load_slots(xs).astype(F32)
    unit, scale = centered(x)
    vec_out[0:1] += jnp.sum(dh * unit, axis=0, keepdims=True)
    vec_out[1:2] += jnp.sum(dh, axis=0, keepdims=True)
    grad = (dx[...] + norm_back(unit, scale, dh * vec[0:1])).astype(BF16)
    store_slots(outs, grad)


def back_first_body(
    place, lengths, qkv, lse, dattn, x0, x1, x2, x3, dx, p0, p1, p2, p3, vec, sums,
    o0, o1, o2, o3, dqkv_out, vec_out, w_qkv, bias, sems,
):
    back_rows(
        place, lengths, qkv, lse, dattn, (x0, x1, x2, x3), dx, (p0, p1, p2, p3), vec, sums,
        (o0, o1, o2, o3), dqkv_out, vec_out, w_qkv, bias, sems,
    )


def back_last_body(
    dims, place, lengths, qkv, lse, dattn, x0, x1, x2, x3, dx, p0, p1, p2, p3, vec, sums,
    h_one, before,
    o0, o1, o2, o3, vec_out, keep, send, dqkv, w_qkv, bias, h_turned, parts, sems, out_sems,
):
    step = pl.program_id(0)
    slots = qkv.shape[0]
    here = pl.ds(pl.multiple_of(step * slots, slots), slots)
    back_rows(
        place, lengths, qkv, lse, dattn, (x0, x1, x2, x3), dx, (p0, p1, p2, p3), vec, sums,
        (o0, o1, o2, o3), dqkv.at[here], vec_out, w_qkv, bias, sems,
    )

    @pl.when(step == pl.num_programs(0) - 1)
    def _():
        count = before.shape[0]
        h_turned[...] = h_one[...].T
        quarter = before.shape[1] // 4
        copies = []
        for half in range(2):
            for y in range(2):
                at = (half * 2 + y) * quarter
                value = nn_dot(h_turned[:, :count], before[:, at : at + quarter])
                value = value + nn_dot(h_turned[:, count:], dqkv[:, at : at + quarter])
                write_parts(parts, half, y, 0, value, dims)
                these = send_copies(parts, half, y, keep, send, place, out_sems)
                start_all(these)
                copies += these
        wait_all(copies)


def add_mlp_body(keep, got, down_keep, down_got, *outs):
    for k in range(4):
        outs[k][...] = (keep[k].astype(F32) + got[k].astype(F32)).astype(BF16)
        outs[4][:, k] = (down_keep[k].astype(F32) + down_got[k].astype(F32)).astype(BF16)


def add_qkv_body(keep, got, vec, *outs):
    rows = keep.shape[2]
    sums = vec[...]
    for k, out in enumerate(outs):
        out[:, :rows, :] = (keep[k].astype(F32) + got[k].astype(F32)).astype(BF16)
        out[:, rows:, :] = jnp.zeros((out.shape[0], 16, out.shape[2]), BF16)
        lanes = sums.shape[1] // out.shape[0]
        for h in range(out.shape[0]):
            out[h, rows:, :lanes] = sums[:, h * lanes : (h + 1) * lanes].astype(BF16)


def collect_body(place, *refs):
    out = refs[-1]
    at = 0
    for i in range(0, len(refs) - 1, 4):
        count = refs[i].shape[0]
        for k in range(4):
            out[place[2] ^ k, at : at + count] = refs[i + k][...]
        at += count


def in_order(values, place):
    core, y = place[3], place[7]
    near = (jnp.where(y == 0, values[0], values[1]), jnp.where(y == 0, values[1], values[0]))
    far = (jnp.where(y == 0, values[2], values[3]), jnp.where(y == 0, values[3], values[2]))
    first = (jnp.where(core == 0, near[0], far[0]), jnp.where(core == 0, near[1], far[1]))
    second = (jnp.where(core == 0, far[0], near[0]), jnp.where(core == 0, far[1], near[1]))
    return (*first, *second)


def vec_sums(a0, a2, place, shard):
    lanes = 128
    own = a0[shard:, :lanes].astype(F32)
    far = a2[shard:, :lanes].astype(F32)
    both = own + far
    lane = lax.broadcasted_iota(jnp.int32, both.shape, 1) // (lanes // 2)
    return jnp.where(lane == place[8], both, 0.0)


def square_mlp_body(place, m0, m1, m2, m3, out):
    values = []
    for mlp in (m0, m1, m2, m3):
        value = mlp[...].astype(F32)
        values.append(jnp.sum(value * value))
    first, second, third, fourth = in_order(values, place)
    out[...] = jnp.full(out.shape, (first + second) + (third + fourth), F32)


def square_body(place, before, a0, a1, a2, a3, out):
    shard = a0.shape[0] - 16
    values = []
    for attn in (a0, a1, a2, a3):
        value = attn[:shard].astype(F32)
        values.append(jnp.sum(value * value))
    vec = vec_sums(a0, a2, place, shard)
    first, second, third, fourth = in_order(values, place)
    value = ((first + second) + (third + fourth)) + jnp.sum(vec * vec)
    total_value = before[...] + value
    for d in range(out.shape[0]):
        out[d] = total_value


def adam_parts(weight, moment, second, grad, decay, rate):
    moment_new = BETA_ONE * moment + (1.0 - BETA_ONE) * grad
    second_new = BETA_TWO * second + (1.0 - BETA_TWO) * grad * grad
    first_hat = moment_new * (1.0 / (1.0 - BETA_ONE**ADAM_STEP))
    second_hat = second_new * (1.0 / (1.0 - BETA_TWO**ADAM_STEP))
    step = first_hat / (jnp.sqrt(second_hat) + ADAM_EPS)
    return weight - rate * (step + decay * weight), moment_new, second_new


def adam_body(
    place, squares, m0, m1, m2, m3, a0, a1, a2, a3,
    attn_w, attn_m, attn_v, mlp_w, mlp_m, mlp_v, vec_w, vec_m, vec_v,
    norm_out, attn_wo, attn_mo, attn_vo, mlp_wo, mlp_mo, mlp_vo, vec_wo, vec_mo, vec_vo,
):
    shard = m0.shape[0]
    hidden = mlp_w.shape[2]
    quarter = hidden // 4
    wide = a0.shape[1]
    small = m0.shape[1] - 2 * quarter
    value = squares[0]
    for d in range(1, squares.shape[0]):
        value = value + squares[d]
    norm = jnp.sqrt(value)
    norm_out[...] = norm[0:1, 0:1]
    factor = (CLIP_NORM / jnp.maximum(norm, CLIP_NORM))[0:1, 0:1]
    rows, cols = vec_w.shape
    vec = vec_sums(a0, a2, place, shard)
    grad = (vec[:rows, :cols] + vec[:rows, cols : 2 * cols]) * factor
    parts = adam_parts(vec_w[...], vec_m[...], vec_v[...], grad, 0.0, VEC_RATE)
    for new, new_value in zip((vec_wo, vec_mo, vec_vo), parts):
        new[...] = new_value
    core, y = place[3], place[7]
    olds = (attn_w, attn_m, attn_v)
    news = (attn_wo, attn_mo, attn_vo)
    mlp_olds = (mlp_w, mlp_m, mlp_v)
    mlp_news = (mlp_wo, mlp_mo, mlp_vo)
    for i, (mlp, attn) in enumerate(((m0, a0), (m1, a1), (m2, a2), (m3, a3))):
        side = (core if i < 2 else 1 - core) * 2 + (y if i % 2 == 0 else 1 - y)

        def columns(base, size, side=side):
            return pl.ds(pl.multiple_of(base + side * size, 128), size)

        at = columns(0, wide)
        grad = attn[:shard].astype(F32) * factor
        for new, new_value in zip(news, adam_parts(*[o[:, at] for o in olds], grad, WEIGHT_DECAY, LEARN_RATE)):
            new[:, at] = new_value
        at = columns(4 * wide, small)
        grad = mlp[:, quarter : quarter + small].astype(F32) * factor
        for new, new_value in zip(news, adam_parts(*[o[:, at] for o in olds], grad, WEIGHT_DECAY, LEARN_RATE)):
            new[:, at] = new_value
        at = columns(0, quarter)
        for j, start in ((0, 0), (1, quarter + small)):
            grad = mlp[:, start : start + quarter].astype(F32) * factor
            parts = adam_parts(*[o[j, :, at] for o in mlp_olds], grad, WEIGHT_DECAY, LEARN_RATE)
            for new, new_value in zip(mlp_news, parts):
                new[j, :, at] = new_value


def shape_of(dims, dtype):
    return jax.ShapeDtypeStruct(dims, dtype)


def rows_spec(rows, cols):
    return pl.BlockSpec((rows, cols), lambda r: (r, 0))


def whole_spec(shape):
    return pl.BlockSpec(shape, lambda r: (0,) * len(shape))


def call(body, grid, in_specs, out_specs, out_shape, scratch, cost, name, aliases=None):
    return pl.pallas_call(
        body,
        grid=(grid,),
        in_specs=in_specs,
        out_specs=out_specs,
        out_shape=out_shape,
        scratch_shapes=scratch,
        input_output_aliases=aliases or {},
        compiler_params=pltpu.CompilerParams(
            vmem_limit_bytes=VMEM_BYTES, dimension_semantics=("arbitrary",)
        ),
        cost_estimate=pl.CostEstimate(
            flops=int(cost * 1e9), bytes_accessed=int(cost * 2e6), transcendentals=0
        ),
        name=name,
    )


def swap(value, axis):
    return lax.ppermute(value, axis, [(0, 1), (1, 0)])


def ordered(own, other, index, axis):
    first = jnp.where(index == 0, own, other)
    second = jnp.where(index == 0, other, own)
    return jnp.stack([first, second], axis)


def from_seq(pieces):
    moved = [pieces[0]]
    for k in range(1, 4):
        moved.append(lax.ppermute(pieces[k], ("y", "core"), [(j, j ^ k) for j in range(4)]))
    return moved


def spread_hi(half):
    hi_count = lax.axis_size("hi")
    spread = jnp.broadcast_to(half[None], (hi_count, *half.shape))
    return lax.all_to_all(spread, "hi", 0, 0)


def share(own):
    other = swap(own, "lo")
    return [own, other, swap(own, "core"), swap(other, "core")]


def settle(pieces, lo, core, groups=4):
    near = ordered(pieces[0], pieces[1], lo, 1)
    far = ordered(pieces[2], pieces[3], lo, 1)
    whole = ordered(near, far, core, 2)
    cols = whole.shape[-1]
    whole = whole.reshape(groups, 2, 2, -1, cols)
    return [whole[:, 0, 0], whole[:, 1, 0], whole[:, 0, 1], whole[:, 1, 1]]


def add_pair(keep, got):
    return (keep.astype(F32) + got.astype(F32)).astype(BF16)


def spread_plane(part):
    part = part.reshape(4, *part.shape[2:])
    return lax.all_to_all(part, ("lo", "y"), 0, 0)


def total(part):
    return jnp.sum(part.astype(F32), axis=0).astype(BF16)


def to_all(mine):
    return [mine] + [
        lax.ppermute(mine, ("y", "core"), [(j, j ^ k) for j in range(4)]) for k in (2, 1, 3)
    ]


def after(value, *others):
    return lax.optimization_barrier((value, *others))[0]


def in_columns(pieces, y, core):
    near = ordered(pieces[0], pieces[1], y, 1)
    far = ordered(pieces[2], pieces[3], y, 1)
    both = ordered(near, far, core, 1)
    return both.reshape(both.shape[0], -1).astype(F32)


def adam_update(weight, moment, second, grad, decay, rate):
    moment_new = BETA_ONE * moment + (1.0 - BETA_ONE) * grad
    second_new = BETA_TWO * second + (1.0 - BETA_TWO) * grad * grad
    first_hat = moment_new / (1.0 - BETA_ONE**ADAM_STEP)
    second_hat = second_new / (1.0 - BETA_TWO**ADAM_STEP)
    weight_new = weight - rate * (first_hat / (jnp.sqrt(second_hat) + ADAM_EPS) + decay * weight)
    return (weight_new, moment_new, second_new)


def on_device(
    tokens, cotangent, lengths, attn_w, attn_m, attn_v, mlp_w, mlp_m, mlp_v, vec_w, vec_m, vec_v
):
    lo = lax.axis_index("lo")
    y = lax.axis_index("y")
    core = lax.axis_index("core")
    hi_count = lax.axis_size("hi")
    me = y * 2 + core
    micro_count, row_count, part, width = tokens.shape
    hidden = mlp_w.shape[2]
    shard = attn_w.shape[0]
    slots = 4 * part
    rows = micro_count * row_count // 4
    count = rows * slots
    vec_rows, vec_cols = vec_w.shape
    half_rows = shard // 2
    fits = half_rows % 16 == 0

    flat_tokens = tokens.reshape(4, rows, part, width)
    flat_cot = cotangent.reshape(4, rows, part, width)

    def pick(stack, k):
        return lax.dynamic_index_in_dim(stack, me ^ k, 0, keepdims=False)

    def half_of(value):
        return lax.dynamic_slice_in_dim(value, core * half_rows, half_rows, 0)

    xs = from_seq([pick(flat_tokens, k) for k in range(4)])
    lanes = 128
    ride = jnp.pad(vec_w.reshape(-1), (0, half_rows * lanes - vec_w.size)).reshape(half_rows, lanes)
    first_half = jnp.concatenate([half_of(attn_w[:, : 3 * width]), ride], axis=1).astype(BF16)
    qkv_own = spread_hi(first_half)
    split = 3 * hidden // 4
    up_half = jnp.concatenate(
        [half_of(attn_w[:, 3 * width :]), half_of(mlp_w[0]), half_of(mlp_w[1, :, split:])], axis=1
    )
    up_own = spread_hi(after(up_half.astype(BF16), qkv_own))
    qkv_own, xs[3] = lax.optimization_barrier((qkv_own, xs[3]))
    qkv_other = swap(qkv_own, "lo")
    qkv_pieces = [qkv_own, qkv_other, swap(qkv_own, "core"), swap(qkv_other, "core")]
    vec_all = ordered(qkv_pieces[0][:, :, 3 * width :], qkv_pieces[1][:, :, 3 * width :], lo, 1)
    vec_all = vec_all.reshape(2 * hi_count, -1)[:, : vec_w.size].reshape(-1, vec_rows, vec_cols)
    vec_all = vec_all.transpose(1, 0, 2).reshape(vec_rows, width)
    vec_float = jnp.pad(vec_all.astype(F32), ((0, 16 - vec_rows), (0, 0)))

    if fits:
        places = [lo, core, me, core, 0 * lo, lo, y, y, lo]
        dims = (hi_count, 2, shard)
    else:
        qkv_pieces = settle(qkv_pieces, lo, core)
        places = [0 * lo, 0 * lo, me, core, 0 * lo, 0 * lo, 0 * lo, y, lo]
        dims = (1, 1, width)
    place = jnp.stack(places).astype(jnp.int32)
    later = place.at[4].set(rows // 2)
    row_lengths = lax.dynamic_slice_in_dim(lengths.reshape(-1), me * rows, rows)

    vec_spec = whole_spec((16, width))
    lse_spec = pl.BlockSpec((1, HEADS, slots), lambda r: (r, 0, 0))
    group = 2 if rows % 2 == 0 else 1
    slot_spec = pl.BlockSpec((group, part, width), lambda r: (r, 0, 0))
    narrow = rows_spec(group * slots, width)
    wide_qkv = rows_spec(group * slots, 3 * width)
    triple = rows_spec(slots, 3 * width)
    n_piece = 4 * qkv_pieces[0].shape[0]
    dma = pltpu.SemaphoreType.DMA
    h_one, qkv = call(
        qkv_body,
        rows // group,
        [SMEM, *[slot_spec] * 4, *[ANY] * 4, vec_spec],
        [narrow, wide_qkv],
        [shape_of((count, width), BF16), shape_of((count, 3 * width), BF16)],
        [pltpu.VMEM((width, 3 * width), BF16), dma((n_piece,))],
        7,
        "qkv",
    )(place, *xs, *qkv_pieces, vec_float)

    down_half = after(half_of(mlp_w[1, :, :split]).astype(BF16), qkv_other)
    down_pair = jnp.stack(lax.optimization_barrier((down_half, swap(down_half, "lo"), h_one))[:2])
    down_own = spread_hi(after(down_pair, up_own))
    cot = after(flat_cot, qkv_other)
    dys = from_seq([pick(cot, k) for k in range(4)])
    qkv, up_own = lax.optimization_barrier((qkv, up_own))
    up_other = swap(up_own, "lo")

    def half_spec(block, base):
        zeros = (0,) * (len(block) - 1)
        return pl.BlockSpec(block, lambda r: (r + base, *zeros))

    def attend(qkv, base, steps, before):
        return call(
            attend_body,
            steps,
            [SMEM, SMEM, half_spec((slots, 3 * width), base), *[ANY] * len(before)],
            [half_spec((slots, width), base), half_spec((1, HEADS, slots), base)],
            [shape_of((count, width), BF16), shape_of((rows, HEADS, slots), F32)],
            [pltpu.VMEM((slots, slots), F32)],
            4 * steps,
            "attend",
            {3: 0, 4: 1} if before else None,
        )(place.at[4].set(base), row_lengths, qkv, *before)

    up_far = swap(up_own, "core")
    attn, lse = attend(qkv, 0, rows - 1, [])
    up_other, up_far, attn, lse, *dys = lax.optimization_barrier(
        (up_other, up_far, attn, lse, *dys)
    )
    attn, lse = attend(qkv, rows - 1, 1, [attn, lse])
    up_pieces = [up_own, up_other, up_far, swap(up_other, "core")]
    down_own = after(down_own, attn)
    down_far = swap(down_own, "core")
    down_pieces = [down_own, down_far]
    if not fits:
        up_pieces = settle(up_pieces, lo, core)
        split = settle([p[:, j] for p in down_pieces for j in range(2)], lo, core)
        down_pieces = [jnp.stack(split[:2], axis=1), jnp.stack(split[2:], axis=1)]
    n_down = 4 * down_pieces[0].shape[0]

    def parts_shape(quarter):
        return (dims[1], 2, dims[0], dims[2], quarter)

    def in_dp_order(value):
        if fits:
            return value
        value = value.reshape(2, hi_count, 2, shard, value.shape[-1])
        return value.transpose(2, 0, 1, 3, 4)

    turned = pltpu.VMEM((width, count), BF16)
    shape = parts_shape(hidden // 4 + width // 4)
    down_shape = parts_shape(hidden // 4)
    outs = call(
        functools.partial(mlp_body, dims),
        rows // group,
        [SMEM, *[slot_spec] * 4, narrow, *[slot_spec] * 4, *[ANY] * 6, vec_spec],
        [*[slot_spec] * 4, narrow, narrow, vec_spec, *[ANY] * 4],
        [
            *[shape_of((rows, part, width), BF16)] * 4,
            shape_of((count, width), F32),
            shape_of((count, width), BF16),
            shape_of((16, width), F32),
            *[shape_of(shape, BF16)] * 2,
            *[shape_of(down_shape, BF16)] * 2,
        ],
        [
            pltpu.VMEM((width, width), BF16),
            pltpu.VMEM((width, hidden), BF16),
            pltpu.VMEM((width, hidden), BF16),
            turned,
            turned,
            turned,
            pltpu.VMEM((count, hidden), BF16),
            pltpu.VMEM((count, hidden), BF16),
            pltpu.VMEM((count, width), BF16),
            pltpu.VMEM((2, *shape), BF16),
            pltpu.VMEM((2, *down_shape), BF16),
            dma((n_piece,)),
            dma((2 * n_piece,)),
            dma((n_down,)),
            dma((2, dims[1], 2)),
            dma((2, dims[1], 2)),
        ],
        24,
        "mlp",
    )(place, *xs, attn, *dys, *up_pieces, *down_pieces, vec_float)
    results, (dx, dattn, vec_mlp, up_keep, up_send, down_keep, down_send) = outs[:4], outs[4:]
    up_got = swap(up_send, "core")
    down_got = swap(down_send, "core")

    def collect(parts):
        out = (4, rows, part, width)
        return call(
            collect_body,
            1,
            [SMEM, *[whole_spec(p.shape) for p in parts]],
            whole_spec(out),
            shape_of(out, BF16),
            [],
            2,
            "collect",
        )(place, *parts).reshape(tokens.shape)

    results = from_seq(results)
    lead = 2
    lead_count = lead * slots
    back_args = [lse, dattn, *xs, dx]
    weights = [*qkv_pieces, vec_float]

    def back_specs(base):
        return [
            SMEM,
            SMEM,
            half_spec((slots, 3 * width), base),
            half_spec((1, HEADS, slots), base),
            half_spec((slots, width), base),
            *[half_spec((1, part, width), base)] * 4,
            half_spec((slots, width), base),
            *[ANY] * 4,
            vec_spec,
            vec_spec,
        ]

    first_shapes = [shape_of((lead, part, width), BF16)] * 4
    last_shapes = [shape_of((rows - lead, part, width), BF16)] * 4
    back_scratch = [pltpu.VMEM((width, 3 * width), BF16), pltpu.VMEM((slots, slots), F32)]
    outs = call(
        back_first_body,
        lead,
        back_specs(0),
        [*[half_spec((1, part, width), 0)] * 4, triple, vec_spec],
        [*first_shapes, shape_of((lead_count, 3 * width), BF16), shape_of((16, width), F32)],
        [*back_scratch, dma((n_piece,))],
        11,
        "back_first",
    )(place, row_lengths, after(qkv, up_send, down_send), *back_args, *weights, vec_mlp)
    input_first, (grad_first, vec_first) = outs[:4], outs[4:]

    def add_call(body, args, outs):
        args = [a.reshape(4, *a.shape[2:]) if a.ndim > 2 else a for a in args]
        return call(
            body,
            1,
            [whole_spec(a.shape) for a in args],
            [whole_spec(o.shape) for o in outs],
            outs,
            [],
            3,
            "add",
        )(*args)

    def plane_sum(parts):
        moved = [parts[0]]
        for k in (2, 1, 3):
            perm = [(j, j ^ k) for j in range(4)]
            moved.append(lax.ppermute(parts[k], ("lo", "y"), perm))
        return moved

    def add_moved(moved):
        value = (moved[0].astype(F32) + moved[1].astype(F32)) + moved[2].astype(F32)
        return (value + moved[3].astype(F32)).astype(BF16)

    def plane_total(keep, got, extra):
        part = in_dp_order(add_pair(keep, got))
        if extra is not None:
            part = jnp.concatenate([part, extra], axis=3)
        return total(spread_plane(part))

    input_first = from_seq(input_first)
    qkv_last = qkv
    output = collect(results)
    if fits:
        args = [up_keep, up_got, down_keep, down_got]
        args = lax.optimization_barrier((*args, grad_first, *results))[:4]
        piece = shape_of(up_keep.shape[2:], BF16)
        by_hi = shape_of((hi_count, 4, *down_keep.shape[3:]), BF16)
        *parts, down_part = add_call(add_mlp_body, args, [*[piece] * 4, by_hi])
        qkv_last = after(qkv, *parts, down_part)
        up_moved = plane_sum(parts)
        down_part = total(lax.all_to_all(down_part, "hi", 0, 0))
    quarter = 3 * width // 4
    shape = parts_shape(quarter)
    outs = call(
        functools.partial(back_last_body, dims),
        rows - lead,
        [
            *back_specs(lead),
            whole_spec((count, width)),
            whole_spec((lead_count, 3 * width)),
        ],
        [*[half_spec((1, part, width), 0)] * 4, vec_spec, ANY, ANY],
        [*last_shapes, shape_of((16, width), F32), shape_of(shape, BF16), shape_of(shape, BF16)],
        [
            pltpu.VMEM((count - lead_count, 3 * width), BF16),
            *back_scratch,
            turned,
            pltpu.VMEM((2, *shape), BF16),
            dma((n_piece,)),
            dma((2, dims[1], 2)),
        ],
        13,
        "back_last",
    )(place.at[4].set(lead), row_lengths, qkv_last, *back_args, *weights, vec_first, h_one, grad_first)
    input_last, (vec_last, qkv_keep, qkv_send) = outs[:4], outs[4:]
    if fits:
        qkv_send = after(qkv_send, *up_moved, *input_first)
    qkv_got = swap(qkv_send, "core")

    if fits:
        _, _, _, more_rows, more_cols = qkv_keep.shape
        piece = shape_of((hi_count, more_rows + 16, more_cols), BF16)
        parts = add_call(add_qkv_body, [qkv_keep, qkv_got, vec_last], [piece] * 4)
        qkv_moved = plane_sum(parts)
        down_moved = plane_sum([down_part[k] for k in range(4)])
        up_plane = after(add_moved(up_moved), *parts)
        up_mine = total(lax.all_to_all(up_plane, "hi", 0, 0))
        down_mine = add_moved(down_moved)
        qkv_plane = after(add_moved(qkv_moved), up_mine, down_mine)
        qkv_mine = total(lax.all_to_all(qkv_plane, "hi", 0, 0))
    else:
        vec_total = vec_last.reshape(16, hi_count, 2, vec_cols)
        vec_total = vec_total.transpose(1, 0, 2, 3).reshape(1, 1, hi_count, 16, 2 * vec_cols)
        vec_total = jnp.pad(vec_total.astype(BF16), ((0, 0),) * 4 + ((0, quarter - 2 * vec_cols),))
        vec_total = jnp.broadcast_to(vec_total, (2, 2, *vec_total.shape[2:]))
        up_mine = total(lax.all_to_all(plane_total(up_keep, up_got, None), "hi", 0, 0))
        down_mine = total(lax.all_to_all(plane_total(down_keep, down_got, None), "hi", 0, 0))
        qkv_mine = plane_total(qkv_keep, qkv_got, vec_total)
        qkv_mine = total(lax.all_to_all(qkv_mine, "hi", 0, 0))
    mlp_mine = jnp.concatenate([up_mine, down_mine], axis=1)
    mlp_pieces = to_all(mlp_mine)
    attn_pieces = to_all(after(qkv_mine, *mlp_pieces))
    input_last = from_seq(lax.optimization_barrier((*input_last, *attn_pieces))[:4])
    input_grad = collect([*input_first, *input_last])

    dp_count = 2 * hi_count
    if fits:
        pieces = [*mlp_pieces, *attn_pieces]
        piece_specs = [whole_spec(p.shape) for p in pieces]
        squares_shape = (dp_count, 8, 128)
        mlp_square = call(
            square_mlp_body,
            1,
            [SMEM, *piece_specs[:4]],
            whole_spec((8, 128)),
            shape_of((8, 128), F32),
            [],
            2,
            "mlp_squares",
        )(place, *mlp_pieces)
        squares = call(
            square_body,
            1,
            [SMEM, whole_spec((8, 128)), *piece_specs[4:]],
            whole_spec(squares_shape),
            shape_of(squares_shape, F32),
            [],
            1,
            "squares",
        )(place, mlp_square, *attn_pieces)
        squares = lax.all_to_all(squares, ("hi", "lo"), 0, 0)
        states = [attn_w, attn_m, attn_v, mlp_w, mlp_m, mlp_v, vec_w, vec_m, vec_v]
        state_specs = [whole_spec(v.shape) for v in states]
        norm, *new = call(
            adam_body,
            1,
            [SMEM, whole_spec(squares_shape), *piece_specs, *state_specs],
            [whole_spec((1, 1)), *state_specs],
            [shape_of((1, 1), F32), *[shape_of(v.shape, F32) for v in states]],
            [],
            6,
            "adam",
        )(place, squares, *pieces, *states)
        return (output, input_grad, *new, norm.reshape(()))

    vec_sum = attn_pieces[0][shard:].astype(F32) + attn_pieces[2][shard:].astype(F32)
    vec_sum = jnp.where(lo == 0, vec_sum[:, :vec_cols], vec_sum[:, vec_cols : 2 * vec_cols])
    vec_sum = vec_sum[:vec_rows]
    up_at = hidden // 4
    out_at = up_at + width // 4
    up_sum = in_columns([p[:, :up_at] for p in mlp_pieces], y, core)
    out_sum = in_columns([p[:, up_at:out_at] for p in mlp_pieces], y, core)
    down_sum = in_columns([p[:, out_at:] for p in mlp_pieces], y, core)
    qkv_sum = in_columns([p[:shard] for p in attn_pieces], y, core)
    attn_sum = jnp.concatenate([qkv_sum, out_sum], axis=1)
    mlp_sum = jnp.stack([up_sum, down_sum])
    square = jnp.sum(attn_sum * attn_sum) + jnp.sum(mlp_sum * mlp_sum) + jnp.sum(vec_sum * vec_sum)
    squares = lax.all_to_all(jnp.full((dp_count, 8, 128), square), ("hi", "lo"), 0, 0)
    grad_norm = jnp.sqrt(jnp.sum(squares[:, 0, 0]))
    clip_factor = CLIP_NORM / jnp.maximum(grad_norm, CLIP_NORM)
    attn_new = adam_update(
        attn_w, attn_m, attn_v, attn_sum * clip_factor, WEIGHT_DECAY, LEARN_RATE
    )
    mlp_new = adam_update(mlp_w, mlp_m, mlp_v, mlp_sum * clip_factor, WEIGHT_DECAY, LEARN_RATE)
    vec_new = adam_update(vec_w, vec_m, vec_v, vec_sum * clip_factor, 0.0, VEC_RATE)
    return (output, input_grad, *attn_new, *mlp_new, *vec_new, grad_norm)


def solution(mesh):
    dp_count = mesh.shape["dp"]
    seq_count = mesh.shape["seq"]
    fine = jax.sharding.Mesh(
        mesh.devices.reshape(dp_count // 2, 2, seq_count // 2, 2), ("hi", "lo", "y", "core")
    )
    dp = ("hi", "lo")
    seq = ("y", "core")
    acts = P(None, dp, seq, None)
    attn = P(dp, None)
    mlp = P(None, dp, None)
    vec = P(None, dp)
    return jax.shard_map(
        on_device,
        mesh=fine,
        in_specs=(acts, acts, P(None, dp), attn, attn, attn, mlp, mlp, mlp, vec, vec, vec),
        out_specs=(acts, acts, attn, attn, attn, mlp, mlp, mlp, vec, vec, vec, P()),
        check_vma=False,
    )
```

```python
import functools
import math

import jax
import jax.numpy as jnp
from jax import lax
from jax.experimental import pallas as pl
from jax.experimental.pallas import tpu as pltpu
from jax.sharding import PartitionSpec as P

HEADS = 8
ADAM_STEP = 10
CLIP_NORM = 1.0
BETA_ONE = 0.9
BETA_TWO = 0.999
LEARN_RATE = 0.08
VEC_RATE = 0.4
WEIGHT_DECAY = 0.01
ADAM_EPS = 1e-08
NORM_EPS = 1e-05
VMEM_BYTES = 65408 * 1024

F32 = jnp.float32
BF16 = jnp.bfloat16
ANY = pl.BlockSpec(memory_space=pl.ANY)
SMEM = pl.BlockSpec(memory_space=pltpu.SMEM)


def nt_dot(left, right):
    return lax.dot_general(left, right, (((1,), (1,)), ((), ())), preferred_element_type=F32)


def nn_dot(left, right):
    return jnp.dot(left, right, preferred_element_type=F32)


def centered(values):
    center = values - jnp.mean(values, axis=-1, keepdims=True)
    spread = jnp.mean(center * center, axis=-1, keepdims=True)
    scale = lax.rsqrt(spread + NORM_EPS)
    return center * scale, scale


def norm_back(unit, scale, grad):
    mean_grad = jnp.mean(grad, axis=-1, keepdims=True)
    mean_both = jnp.mean(grad * unit, axis=-1, keepdims=True)
    return scale * (grad - mean_grad - unit * mean_both)


def gelu_and_slope(up):
    share = 0.5 + 0.5 * lax.erf(up * (1.0 / math.sqrt(2.0)))
    bell = jnp.exp2(up * up * (-0.5 * math.log2(math.e)))
    return up * share, share + up * (bell * (1.0 / math.sqrt(2.0 * math.pi)))


def load_slots(refs):
    return jnp.concatenate([ref[i] for i in range(refs[0].shape[0]) for ref in refs], axis=0)


def store_slots(refs, value):
    rows, part, _ = refs[0].shape
    for i in range(rows):
        for k, ref in enumerate(refs):
            at = (i * 4 + k) * part
            ref[i] = value[at : at + part]


def placements(pieces, jobs, place, sems):
    lo = place[0]
    core = place[1]
    copies = []
    for i, piece in enumerate(pieces):
        lo_at = lo if i % 2 == 0 else 1 - lo
        core_at = core if i < 2 else 1 - core
        hi_count, rows, _ = piece.shape
        for h in range(hi_count):
            row = pl.multiple_of(((h * 2 + lo_at) * 2 + core_at) * rows, rows)
            for column, width, target, at in jobs:
                copies.append(
                    pltpu.make_async_copy(
                        piece.at[h, :, pl.ds(column, width)],
                        target.at[pl.ds(row, rows), pl.ds(at, width)],
                        sems.at[len(copies)],
                    )
                )
    return copies


def pair_placements(pieces, target, place, sems):
    copies = []
    for i, piece in enumerate(pieces):
        core_at = place[1] if i == 0 else 1 - place[1]
        hi_count, _, rows, _ = piece.shape
        for h in range(hi_count):
            for j in range(2):
                row = pl.multiple_of(((h * 2 + (place[0] ^ j)) * 2 + core_at) * rows, rows)
                copies.append(
                    pltpu.make_async_copy(
                        piece.at[h, j],
                        target.at[pl.ds(row, rows), pl.ds(0, piece.shape[-1])],
                        sems.at[len(copies)],
                    )
                )
    return copies


def head_masks(width):
    lane = lax.broadcasted_iota(jnp.int32, (1, width), 1)
    first = jnp.where(lane < width // 2, 1.0, 0.0)
    return first.astype(BF16), (1.0 - first).astype(BF16)


def fill_bias(place, lengths, row, bias):
    part = bias.shape[0] // 4
    for k in range(4):
        base = (place[2] ^ k) * part
        slot = lax.broadcasted_iota(jnp.int32, (part, bias.shape[1]), 0) + base
        bias[k * part : (k + 1) * part, :] = jnp.where(slot < lengths[row], 0.0, -1e30)


def qkv_body(place, x0, x1, x2, x3, p0, p1, p2, p3, vec, h_out, qkv_out, w_qkv, sems):
    row = pl.program_id(0)
    width = vec.shape[1]
    copies = placements((p0, p1, p2, p3), [(0, 3 * width, w_qkv, 0)], place, sems)

    @pl.when(row == 0)
    def _():
        for copy in copies:
            copy.start()

    x = load_slots((x0, x1, x2, x3)).astype(F32)
    unit, _ = centered(x)
    h = (unit * vec[0:1] + vec[1:2]).astype(BF16)
    h_out[...] = h

    @pl.when(row == 0)
    def _():
        for copy in copies:
            copy.wait()

    q = nn_dot(h, w_qkv[:, :width]).astype(BF16)
    qkv_out[:, :width] = q * jnp.asarray(1.0 / math.sqrt(width // HEADS), BF16)
    qkv_out[:, width:] = nn_dot(h, w_qkv[:, width:]).astype(BF16)


def attend_body(place, lengths, qkv, *refs):
    attn_out, lse_out, bias = refs[-3:]
    row = pl.program_id(0) + place[4]
    width = attn_out.shape[1]
    pair = 2 * (width // HEADS)
    half = pair // 2
    fill_bias(place, lengths, row, bias)
    masks = head_masks(pair)

    def score(h):
        at = (h // 2) * pair
        return nt_dot(qkv[:, width + at : width + at + pair], qkv[:, at : at + pair] * masks[h % 2])

    def soft(h, scores):
        scores = scores + bias[...]
        top = jnp.max(scores, axis=0, keepdims=True)
        grown = jnp.exp(scores - top)
        total = jnp.sum(grown, axis=0, keepdims=True)
        lse_out[0, h : h + 1, :] = top + jnp.log(total)
        return (grown * (1.0 / total)).astype(BF16)

    def value(h, turned, probs):
        return nn_dot(turned[(h % 2) * half : (h % 2 + 1) * half], probs)

    turned = [qkv[:, 2 * width + p * pair : 2 * width + (p + 1) * pair].T for p in range(HEADS // 2)]
    scores = [score(h) for h in range(HEADS)]
    probs = [soft(h, scores[h]) for h in range(HEADS)]
    outs = [value(h, turned[h // 2], probs[h]) for h in range(HEADS)]
    for p in range(HEADS // 2):
        attn_out[:, p * pair : (p + 1) * pair] = jnp.concatenate(outs[2 * p : 2 * p + 2], axis=0).T.astype(BF16)


def write_parts(parts, half, y, column, value, dims):
    hi_count, lo_count, rows = dims
    quarter = value.shape[1]
    value = value.astype(BF16)
    for h in range(hi_count):
        for lo in range(lo_count):
            at = (h * lo_count + lo) * rows
            parts[half, lo, y, h, :, column : column + quarter] = value[at : at + rows]


def send_copies(parts, half, y, keep, send, place, sems):
    mine = half == place[3]
    copies = []
    for i in range(parts.shape[1]):
        for target, wanted in ((keep, mine), (send, jnp.logical_not(mine))):
            lo_count = parts.shape[1]
            copy = pltpu.make_async_copy(
                parts.at[half, i, y],
                target.at[(place[5] ^ i) if lo_count > 1 else 0, place[6] ^ y],
                sems.at[half, i, y],
            )
            copies.append((wanted, copy))
    return copies


def start_all(copies):
    for wanted, copy in copies:
        pl.when(wanted)(copy.start)


def wait_all(copies):
    for wanted, copy in copies:
        pl.when(wanted)(copy.wait)


def mlp_body(
    dims, place, x0, x1, x2, x3, attn, d0, d1, d2, d3, b0, b1, b2, b3, c0, c1, vec,
    o0, o1, o2, o3, dx_out, dattn_out, vec_out, up_keep, up_send, down_keep, down_send,
    w_out, w_up, w_down, h_turned, attn_turned, dy_turned, act_all, dup_all, dao_all,
    up_parts, down_parts, out_sems, up_sems, down_sems, part_sems, more_sems,
):
    row = pl.program_id(0)
    width = vec.shape[1]
    hidden = w_up.shape[1]
    slots = attn.shape[0]
    out_copies = placements((b0, b1, b2, b3), [(0, width, w_out, 0)], place, out_sems)
    split = c0.shape[-1]
    jobs = [(width, hidden, w_up, 0), (width + hidden, hidden - split, w_down, split)]
    up_copies = placements((b0, b1, b2, b3), jobs, place, up_sems)
    down_copies = pair_placements((c0, c1), w_down, place, down_sems)

    def arrived(copies):
        @pl.when(row == 0)
        def _():
            for copy in copies:
                copy.wait()

    @pl.when(row == 0)
    def _():
        vec_out[...] = jnp.zeros_like(vec_out)
        for copy in out_copies + up_copies + down_copies:
            copy.start()

    here = pl.ds(pl.multiple_of(row * slots, slots), slots)
    x = load_slots((x0, x1, x2, x3)).astype(F32)
    dy = load_slots((d0, d1, d2, d3))
    dy_turned[:, here] = dy.T
    attn_turned[:, here] = attn[...].T
    arrived(out_copies)
    x_one = x + (nn_dot(attn[...], w_out[...]) + vec[4:5])
    unit, scale = centered(x_one)
    h = (unit * vec[2:3] + vec[3:4]).astype(BF16)
    h_turned[:, here] = h.T
    arrived(up_copies)
    arrived(down_copies)
    for j in range(hidden // width):
        columns = slice(j * width, (j + 1) * width)
        up = nn_dot(h, w_up[:, columns]) + vec[6 + j : 7 + j]
        act, slope = gelu_and_slope(up)
        act_all[here, columns] = act.astype(BF16)
        dup = (slope * nn_dot(dy, w_down[:, columns])).astype(BF16)
        dup_all[here, columns] = dup
        vec_out[6 + j : 7 + j] += jnp.sum(dup.astype(F32), axis=0, keepdims=True)
    result = x_one + (nt_dot(act_all[here, :], w_down[...]) + vec[5:6])
    store_slots((o0, o1, o2, o3), result.astype(BF16))
    dh = nt_dot(dup_all[here, :], w_up[...])
    vec_out[2:3] += jnp.sum(dh * unit, axis=0, keepdims=True)
    vec_out[3:4] += jnp.sum(dh, axis=0, keepdims=True)
    dy_float = dy.astype(F32)
    dx = dy_float + norm_back(unit, scale, dh * vec[2:3])
    dx_out[...] = dx
    dao = dx.astype(BF16)
    dao_all[here, :] = dao
    vec_out[4:5] += jnp.sum(dao.astype(F32), axis=0, keepdims=True)
    vec_out[5:6] += jnp.sum(dy_float, axis=0, keepdims=True)
    dattn_out[...] = nt_dot(dao, w_out[...]).astype(BF16)

    @pl.when(row == pl.num_programs(0) - 1)
    def _():
        quarter = hidden // 4
        small = width // 4
        copies = []
        for half in range(2):
            for y in range(2):
                at = (half * 2 + y) * quarter
                value = nn_dot(h_turned[...], dup_all[:, at : at + quarter])
                write_parts(up_parts, half, y, 0, value, dims)
                value = nn_dot(dy_turned[...], act_all[:, at : at + quarter])
                write_parts(down_parts, half, y, 0, value, dims)
                at = (half * 2 + y) * small
                value = nn_dot(attn_turned[...], dao_all[:, at : at + small])
                write_parts(up_parts, half, y, quarter, value, dims)
                these = send_copies(up_parts, half, y, up_keep, up_send, place, part_sems)
                these += send_copies(down_parts, half, y, down_keep, down_send, place, more_sems)
                start_all(these)
                copies += these
        wait_all(copies)


def back_rows(
    place, lengths, qkv, lse, dattn, xs, dx, pieces, vec, sums, outs, dqkv, vec_out, w_qkv, bias, sems
):
    step = pl.program_id(0)
    width = vec.shape[1]
    slots = qkv.shape[0]
    pair = 2 * (width // HEADS)
    score_scale = 1.0 / math.sqrt(width // HEADS)
    copies = placements(pieces, [(0, 3 * width, w_qkv, 0)], place, sems)

    @pl.when(step == 0)
    def _():
        vec_out[...] = sums[...]
        for copy in copies:
            copy.start()

    fill_bias(place, lengths, step + place[4], bias)
    masks = head_masks(pair)
    half = pair // 2
    pairs = range(HEADS // 2)

    def part(base, p):
        return qkv[:, base + p * pair : base + (p + 1) * pair]

    grads = [dattn[:, p * pair : (p + 1) * pair] for p in pairs]
    qs = [part(0, h // 2) * masks[h % 2] for h in range(HEADS)]
    gs = [grads[h // 2] * masks[h % 2] for h in range(HEADS)]
    k_turned = [part(width, p).T for p in pairs]
    scores = [nt_dot(part(width, h // 2), qs[h]) for h in range(HEADS)]
    dprobs = [nt_dot(part(2 * width, h // 2), gs[h]) for h in range(HEADS)]
    probs_low, ds = [], []
    for h in range(HEADS):
        probs = jnp.exp(scores[h] + bias[...] - lse[0, h : h + 1, :])
        inner = jnp.sum(probs * dprobs[h], axis=0, keepdims=True)
        ds.append((probs * (dprobs[h] - inner)).astype(BF16))
        probs_low.append(probs.astype(BF16))
    dqs = [nn_dot(k_turned[h // 2][(h % 2) * half : (h % 2 + 1) * half], ds[h]) for h in range(HEADS)]
    for p in pairs:
        two = slice(2 * p, 2 * p + 2)
        queries, given = jnp.concatenate(qs[two], axis=0), jnp.concatenate(gs[two], axis=0)
        dk = nn_dot(jnp.concatenate(ds[two], axis=1), queries)
        dv = nn_dot(jnp.concatenate(probs_low[two], axis=1), given)
        dq = jnp.concatenate(dqs[two], axis=0).T * score_scale
        dqkv[:, p * pair : (p + 1) * pair] = dq.astype(BF16)
        dqkv[:, width + p * pair : width + (p + 1) * pair] = dk.astype(BF16)
        dqkv[:, 2 * width + p * pair : 2 * width + (p + 1) * pair] = dv.astype(BF16)

    @pl.when(step == 0)
    def _():
        for copy in copies:
            copy.wait()

    dh = nt_dot(dqkv[...], w_qkv[...])
    x = load_slots(xs).astype(F32)
    unit, scale = centered(x)
    vec_out[0:1] += jnp.sum(dh * unit, axis=0, keepdims=True)
    vec_out[1:2] += jnp.sum(dh, axis=0, keepdims=True)
    grad = (dx[...] + norm_back(unit, scale, dh * vec[0:1])).astype(BF16)
    store_slots(outs, grad)


def back_first_body(
    place, lengths, qkv, lse, dattn, x0, x1, x2, x3, dx, p0, p1, p2, p3, vec, sums,
    o0, o1, o2, o3, dqkv_out, vec_out, w_qkv, bias, sems,
):
    back_rows(
        place, lengths, qkv, lse, dattn, (x0, x1, x2, x3), dx, (p0, p1, p2, p3), vec, sums,
        (o0, o1, o2, o3), dqkv_out, vec_out, w_qkv, bias, sems,
    )


def back_last_body(
    dims, place, lengths, qkv, lse, dattn, x0, x1, x2, x3, dx, p0, p1, p2, p3, vec, sums,
    h_one, before,
    o0, o1, o2, o3, vec_out, keep, send, dqkv, w_qkv, bias, h_turned, parts, sems, out_sems,
):
    step = pl.program_id(0)
    slots = qkv.shape[0]
    here = pl.ds(pl.multiple_of(step * slots, slots), slots)
    back_rows(
        place, lengths, qkv, lse, dattn, (x0, x1, x2, x3), dx, (p0, p1, p2, p3), vec, sums,
        (o0, o1, o2, o3), dqkv.at[here], vec_out, w_qkv, bias, sems,
    )

    @pl.when(step == pl.num_programs(0) - 1)
    def _():
        count = before.shape[0]
        h_turned[...] = h_one[...].T
        quarter = before.shape[1] // 4
        copies = []
        for half in range(2):
            for y in range(2):
                at = (half * 2 + y) * quarter
                value = nn_dot(h_turned[:, :count], before[:, at : at + quarter])
                value = value + nn_dot(h_turned[:, count:], dqkv[:, at : at + quarter])
                write_parts(parts, half, y, 0, value, dims)
                these = send_copies(parts, half, y, keep, send, place, out_sems)
                start_all(these)
                copies += these
        wait_all(copies)


def add_mlp_body(keep, got, down_keep, down_got, *outs):
    for k in range(4):
        outs[k][...] = (keep[k].astype(F32) + got[k].astype(F32)).astype(BF16)
        outs[4][:, k] = (down_keep[k].astype(F32) + down_got[k].astype(F32)).astype(BF16)


def add_qkv_body(keep, got, vec, *outs):
    rows = keep.shape[2]
    sums = vec[...]
    for k, out in enumerate(outs):
        out[:, :rows, :] = (keep[k].astype(F32) + got[k].astype(F32)).astype(BF16)
        out[:, rows:, :] = jnp.zeros((out.shape[0], 16, out.shape[2]), BF16)
        lanes = sums.shape[1] // out.shape[0]
        for h in range(out.shape[0]):
            out[h, rows:, :lanes] = sums[:, h * lanes : (h + 1) * lanes].astype(BF16)


def collect_body(place, *refs):
    out = refs[-1]
    at = 0
    for i in range(0, len(refs) - 1, 4):
        count = refs[i].shape[0]
        for k in range(4):
            out[place[2] ^ k, at : at + count] = refs[i + k][...]
        at += count


def in_order(values, place):
    core, y = place[3], place[7]
    near = (jnp.where(y == 0, values[0], values[1]), jnp.where(y == 0, values[1], values[0]))
    far = (jnp.where(y == 0, values[2], values[3]), jnp.where(y == 0, values[3], values[2]))
    first = (jnp.where(core == 0, near[0], far[0]), jnp.where(core == 0, near[1], far[1]))
    second = (jnp.where(core == 0, far[0], near[0]), jnp.where(core == 0, far[1], near[1]))
    return (*first, *second)


def vec_sums(a0, a2, place, shard):
    lanes = 128
    own = a0[shard:, :lanes].astype(F32)
    far = a2[shard:, :lanes].astype(F32)
    both = own + far
    lane = lax.broadcasted_iota(jnp.int32, both.shape, 1) // (lanes // 2)
    return jnp.where(lane == place[8], both, 0.0)


def square_mlp_body(place, m0, m1, m2, m3, out):
    values = []
    for mlp in (m0, m1, m2, m3):
        value = mlp[...].astype(F32)
        values.append(jnp.sum(value * value))
    first, second, third, fourth = in_order(values, place)
    out[...] = jnp.full(out.shape, (first + second) + (third + fourth), F32)


def square_body(place, before, a0, a1, a2, a3, out):
    shard = a0.shape[0] - 16
    values = []
    for attn in (a0, a1, a2, a3):
        value = attn[:shard].astype(F32)
        values.append(jnp.sum(value * value))
    vec = vec_sums(a0, a2, place, shard)
    first, second, third, fourth = in_order(values, place)
    value = ((first + second) + (third + fourth)) + jnp.sum(vec * vec)
    total_value = before[...] + value
    for d in range(out.shape[0]):
        out[d] = total_value


def adam_parts(weight, moment, second, grad, decay, rate):
    moment_new = BETA_ONE * moment + (1.0 - BETA_ONE) * grad
    second_new = BETA_TWO * second + (1.0 - BETA_TWO) * grad * grad
    first_hat = moment_new * (1.0 / (1.0 - BETA_ONE**ADAM_STEP))
    second_hat = second_new * (1.0 / (1.0 - BETA_TWO**ADAM_STEP))
    step = first_hat / (jnp.sqrt(second_hat) + ADAM_EPS)
    return weight - rate * (step + decay * weight), moment_new, second_new


def adam_body(
    place, squares, m0, m1, m2, m3, a0, a1, a2, a3,
    attn_w, attn_m, attn_v, mlp_w, mlp_m, mlp_v, vec_w, vec_m, vec_v,
    norm_out, attn_wo, attn_mo, attn_vo, mlp_wo, mlp_mo, mlp_vo, vec_wo, vec_mo, vec_vo,
):
    shard = m0.shape[0]
    hidden = mlp_w.shape[2]
    quarter = hidden // 4
    wide = a0.shape[1]
    small = m0.shape[1] - 2 * quarter
    value = squares[0]
    for d in range(1, squares.shape[0]):
        value = value + squares[d]
    norm = jnp.sqrt(value)
    norm_out[...] = norm[0:1, 0:1]
    factor = (CLIP_NORM / jnp.maximum(norm, CLIP_NORM))[0:1, 0:1]
    rows, cols = vec_w.shape
    vec = vec_sums(a0, a2, place, shard)
    grad = (vec[:rows, :cols] + vec[:rows, cols : 2 * cols]) * factor
    parts = adam_parts(vec_w[...], vec_m[...], vec_v[...], grad, 0.0, VEC_RATE)
    for new, new_value in zip((vec_wo, vec_mo, vec_vo), parts):
        new[...] = new_value
    core, y = place[3], place[7]
    olds = (attn_w, attn_m, attn_v)
    news = (attn_wo, attn_mo, attn_vo)
    mlp_olds = (mlp_w, mlp_m, mlp_v)
    mlp_news = (mlp_wo, mlp_mo, mlp_vo)
    for i, (mlp, attn) in enumerate(((m0, a0), (m1, a1), (m2, a2), (m3, a3))):
        side = (core if i < 2 else 1 - core) * 2 + (y if i % 2 == 0 else 1 - y)

        def columns(base, size, side=side):
            return pl.ds(pl.multiple_of(base + side * size, 128), size)

        at = columns(0, wide)
        grad = attn[:shard].astype(F32) * factor
        for new, new_value in zip(news, adam_parts(*[o[:, at] for o in olds], grad, WEIGHT_DECAY, LEARN_RATE)):
            new[:, at] = new_value
        at = columns(4 * wide, small)
        grad = mlp[:, quarter : quarter + small].astype(F32) * factor
        for new, new_value in zip(news, adam_parts(*[o[:, at] for o in olds], grad, WEIGHT_DECAY, LEARN_RATE)):
            new[:, at] = new_value
        at = columns(0, quarter)
        for j, start in ((0, 0), (1, quarter + small)):
            grad = mlp[:, start : start + quarter].astype(F32) * factor
            parts = adam_parts(*[o[j, :, at] for o in mlp_olds], grad, WEIGHT_DECAY, LEARN_RATE)
            for new, new_value in zip(mlp_news, parts):
                new[j, :, at] = new_value


def shape_of(dims, dtype):
    return jax.ShapeDtypeStruct(dims, dtype)


def rows_spec(rows, cols):
    return pl.BlockSpec((rows, cols), lambda r: (r, 0))


def whole_spec(shape):
    return pl.BlockSpec(shape, lambda r: (0,) * len(shape))


def call(body, grid, in_specs, out_specs, out_shape, scratch, cost, name, aliases=None):
    return pl.pallas_call(
        body,
        grid=(grid,),
        in_specs=in_specs,
        out_specs=out_specs,
        out_shape=out_shape,
        scratch_shapes=scratch,
        input_output_aliases=aliases or {},
        compiler_params=pltpu.CompilerParams(
            vmem_limit_bytes=VMEM_BYTES, dimension_semantics=("arbitrary",)
        ),
        cost_estimate=pl.CostEstimate(
            flops=int(cost * 1e9), bytes_accessed=int(cost * 2e6), transcendentals=0
        ),
        name=name,
    )


def swap(value, axis):
    return lax.ppermute(value, axis, [(0, 1), (1, 0)])


def ordered(own, other, index, axis):
    first = jnp.where(index == 0, own, other)
    second = jnp.where(index == 0, other, own)
    return jnp.stack([first, second], axis)


def from_seq(pieces):
    moved = [pieces[0]]
    for k in range(1, 4):
        moved.append(lax.ppermute(pieces[k], ("y", "core"), [(j, j ^ k) for j in range(4)]))
    return moved


def spread_hi(half):
    hi_count = lax.axis_size("hi")
    spread = jnp.broadcast_to(half[None], (hi_count, *half.shape))
    return lax.all_to_all(spread, "hi", 0, 0)


def share(own):
    other = swap(own, "lo")
    return [own, other, swap(own, "core"), swap(other, "core")]


def settle(pieces, lo, core, groups=4):
    near = ordered(pieces[0], pieces[1], lo, 1)
    far = ordered(pieces[2], pieces[3], lo, 1)
    whole = ordered(near, far, core, 2)
    cols = whole.shape[-1]
    whole = whole.reshape(groups, 2, 2, -1, cols)
    return [whole[:, 0, 0], whole[:, 1, 0], whole[:, 0, 1], whole[:, 1, 1]]


def add_pair(keep, got):
    return (keep.astype(F32) + got.astype(F32)).astype(BF16)


def spread_plane(part):
    part = part.reshape(4, *part.shape[2:])
    return lax.all_to_all(part, ("lo", "y"), 0, 0)


def total(part):
    return jnp.sum(part.astype(F32), axis=0).astype(BF16)


def to_all(mine):
    return [mine] + [
        lax.ppermute(mine, ("y", "core"), [(j, j ^ k) for j in range(4)]) for k in (2, 1, 3)
    ]


def after(value, *others):
    return lax.optimization_barrier((value, *others))[0]


def in_columns(pieces, y, core):
    near = ordered(pieces[0], pieces[1], y, 1)
    far = ordered(pieces[2], pieces[3], y, 1)
    both = ordered(near, far, core, 1)
    return both.reshape(both.shape[0], -1).astype(F32)


def adam_update(weight, moment, second, grad, decay, rate):
    moment_new = BETA_ONE * moment + (1.0 - BETA_ONE) * grad
    second_new = BETA_TWO * second + (1.0 - BETA_TWO) * grad * grad
    first_hat = moment_new / (1.0 - BETA_ONE**ADAM_STEP)
    second_hat = second_new / (1.0 - BETA_TWO**ADAM_STEP)
    weight_new = weight - rate * (first_hat / (jnp.sqrt(second_hat) + ADAM_EPS) + decay * weight)
    return (weight_new, moment_new, second_new)


def on_device(
    tokens, cotangent, lengths, attn_w, attn_m, attn_v, mlp_w, mlp_m, mlp_v, vec_w, vec_m, vec_v
):
    lo = lax.axis_index("lo")
    y = lax.axis_index("y")
    core = lax.axis_index("core")
    hi_count = lax.axis_size("hi")
    me = y * 2 + core
    micro_count, row_count, part, width = tokens.shape
    hidden = mlp_w.shape[2]
    shard = attn_w.shape[0]
    slots = 4 * part
    rows = micro_count * row_count // 4
    count = rows * slots
    vec_rows, vec_cols = vec_w.shape
    half_rows = shard // 2
    fits = half_rows % 16 == 0

    flat_tokens = tokens.reshape(4, rows, part, width)
    flat_cot = cotangent.reshape(4, rows, part, width)

    def pick(stack, k):
        return lax.dynamic_index_in_dim(stack, me ^ k, 0, keepdims=False)

    def half_of(value):
        return lax.dynamic_slice_in_dim(value, core * half_rows, half_rows, 0)

    xs = from_seq([pick(flat_tokens, k) for k in range(4)])
    lanes = 128
    ride = jnp.pad(vec_w.reshape(-1), (0, half_rows * lanes - vec_w.size)).reshape(half_rows, lanes)
    first_half = jnp.concatenate([half_of(attn_w[:, : 3 * width]), ride], axis=1).astype(BF16)
    qkv_own = spread_hi(first_half)
    split = 3 * hidden // 4
    up_half = jnp.concatenate(
        [half_of(attn_w[:, 3 * width :]), half_of(mlp_w[0]), half_of(mlp_w[1, :, split:])], axis=1
    )
    up_own = spread_hi(after(up_half.astype(BF16), qkv_own))
    qkv_own, xs[3] = lax.optimization_barrier((qkv_own, xs[3]))
    qkv_other = swap(qkv_own, "lo")
    qkv_pieces = [qkv_own, qkv_other, swap(qkv_own, "core"), swap(qkv_other, "core")]
    vec_all = ordered(qkv_pieces[0][:, :, 3 * width :], qkv_pieces[1][:, :, 3 * width :], lo, 1)
    vec_all = vec_all.reshape(2 * hi_count, -1)[:, : vec_w.size].reshape(-1, vec_rows, vec_cols)
    vec_all = vec_all.transpose(1, 0, 2).reshape(vec_rows, width)
    vec_float = jnp.pad(vec_all.astype(F32), ((0, 16 - vec_rows), (0, 0)))

    if fits:
        places = [lo, core, me, core, 0 * lo, lo, y, y, lo]
        dims = (hi_count, 2, shard)
    else:
        qkv_pieces = settle(qkv_pieces, lo, core)
        places = [0 * lo, 0 * lo, me, core, 0 * lo, 0 * lo, 0 * lo, y, lo]
        dims = (1, 1, width)
    place = jnp.stack(places).astype(jnp.int32)
    later = place.at[4].set(rows // 2)
    row_lengths = lax.dynamic_slice_in_dim(lengths.reshape(-1), me * rows, rows)

    vec_spec = whole_spec((16, width))
    lse_spec = pl.BlockSpec((1, HEADS, slots), lambda r: (r, 0, 0))
    group = 2 if rows % 2 == 0 else 1
    slot_spec = pl.BlockSpec((group, part, width), lambda r: (r, 0, 0))
    narrow = rows_spec(group * slots, width)
    wide_qkv = rows_spec(group * slots, 3 * width)
    triple = rows_spec(slots, 3 * width)
    n_piece = 4 * qkv_pieces[0].shape[0]
    dma = pltpu.SemaphoreType.DMA
    h_one, qkv = call(
        qkv_body,
        rows // group,
        [SMEM, *[slot_spec] * 4, *[ANY] * 4, vec_spec],
        [narrow, wide_qkv],
        [shape_of((count, width), BF16), shape_of((count, 3 * width), BF16)],
        [pltpu.VMEM((width, 3 * width), BF16), dma((n_piece,))],
        7,
        "qkv",
    )(place, *xs, *qkv_pieces, vec_float)

    down_half = after(half_of(mlp_w[1, :, :split]).astype(BF16), qkv_other)
    down_pair = jnp.stack(lax.optimization_barrier((down_half, swap(down_half, "lo"), h_one))[:2])
    down_own = spread_hi(after(down_pair, up_own))
    cot = after(flat_cot, qkv_other)
    dys = from_seq([pick(cot, k) for k in range(4)])
    qkv, up_own = lax.optimization_barrier((qkv, up_own))
    up_other = swap(up_own, "lo")

    def half_spec(block, base):
        zeros = (0,) * (len(block) - 1)
        return pl.BlockSpec(block, lambda r: (r + base, *zeros))

    def attend(qkv, base, steps, before):
        return call(
            attend_body,
            steps,
            [SMEM, SMEM, half_spec((slots, 3 * width), base), *[ANY] * len(before)],
            [half_spec((slots, width), base), half_spec((1, HEADS, slots), base)],
            [shape_of((count, width), BF16), shape_of((rows, HEADS, slots), F32)],
            [pltpu.VMEM((slots, slots), F32)],
            4 * steps,
            "attend",
            {3: 0, 4: 1} if before else None,
        )(place.at[4].set(base), row_lengths, qkv, *before)

    up_far = swap(up_own, "core")
    attn, lse = attend(qkv, 0, rows - 1, [])
    up_other, up_far, attn, lse, *dys = lax.optimization_barrier(
        (up_other, up_far, attn, lse, *dys)
    )
    attn, lse = attend(qkv, rows - 1, 1, [attn, lse])
    up_pieces = [up_own, up_other, up_far, swap(up_other, "core")]
    down_own = after(down_own, attn)
    down_far = swap(down_own, "core")
    down_pieces = [down_own, down_far]
    if not fits:
        up_pieces = settle(up_pieces, lo, core)
        split = settle([p[:, j] for p in down_pieces for j in range(2)], lo, core)
        down_pieces = [jnp.stack(split[:2], axis=1), jnp.stack(split[2:], axis=1)]
    n_down = 4 * down_pieces[0].shape[0]

    def parts_shape(quarter):
        return (dims[1], 2, dims[0], dims[2], quarter)

    def in_dp_order(value):
        if fits:
            return value
        value = value.reshape(2, hi_count, 2, shard, value.shape[-1])
        return value.transpose(2, 0, 1, 3, 4)

    turned = pltpu.VMEM((width, count), BF16)
    shape = parts_shape(hidden // 4 + width // 4)
    down_shape = parts_shape(hidden // 4)
    outs = call(
        functools.partial(mlp_body, dims),
        rows // group,
        [SMEM, *[slot_spec] * 4, narrow, *[slot_spec] * 4, *[ANY] * 6, vec_spec],
        [*[slot_spec] * 4, narrow, narrow, vec_spec, *[ANY] * 4],
        [
            *[shape_of((rows, part, width), BF16)] * 4,
            shape_of((count, width), F32),
            shape_of((count, width), BF16),
            shape_of((16, width), F32),
            *[shape_of(shape, BF16)] * 2,
            *[shape_of(down_shape, BF16)] * 2,
        ],
        [
            pltpu.VMEM((width, width), BF16),
            pltpu.VMEM((width, hidden), BF16),
            pltpu.VMEM((width, hidden), BF16),
            turned,
            turned,
            turned,
            pltpu.VMEM((count, hidden), BF16),
            pltpu.VMEM((count, hidden), BF16),
            pltpu.VMEM((count, width), BF16),
            pltpu.VMEM((2, *shape), BF16),
            pltpu.VMEM((2, *down_shape), BF16),
            dma((n_piece,)),
            dma((2 * n_piece,)),
            dma((n_down,)),
            dma((2, dims[1], 2)),
            dma((2, dims[1], 2)),
        ],
        24,
        "mlp",
    )(place, *xs, attn, *dys, *up_pieces, *down_pieces, vec_float)
    results, (dx, dattn, vec_mlp, up_keep, up_send, down_keep, down_send) = outs[:4], outs[4:]
    up_got = swap(up_send, "core")
    down_got = swap(down_send, "core")

    def collect(parts):
        out = (4, rows, part, width)
        return call(
            collect_body,
            1,
            [SMEM, *[whole_spec(p.shape) for p in parts]],
            whole_spec(out),
            shape_of(out, BF16),
            [],
            2,
            "collect",
        )(place, *parts).reshape(tokens.shape)

    results = from_seq(results)
    lead = 2
    lead_count = lead * slots
    back_args = [lse, dattn, *xs, dx]
    weights = [*qkv_pieces, vec_float]

    def back_specs(base):
        return [
            SMEM,
            SMEM,
            half_spec((slots, 3 * width), base),
            half_spec((1, HEADS, slots), base),
            half_spec((slots, width), base),
            *[half_spec((1, part, width), base)] * 4,
            half_spec((slots, width), base),
            *[ANY] * 4,
            vec_spec,
            vec_spec,
        ]

    first_shapes = [shape_of((lead, part, width), BF16)] * 4
    last_shapes = [shape_of((rows - lead, part, width), BF16)] * 4
    back_scratch = [pltpu.VMEM((width, 3 * width), BF16), pltpu.VMEM((slots, slots), F32)]
    outs = call(
        back_first_body,
        lead,
        back_specs(0),
        [*[half_spec((1, part, width), 0)] * 4, triple, vec_spec],
        [*first_shapes, shape_of((lead_count, 3 * width), BF16), shape_of((16, width), F32)],
        [*back_scratch, dma((n_piece,))],
        11,
        "back_first",
    )(place, row_lengths, after(qkv, up_send, down_send), *back_args, *weights, vec_mlp)
    input_first, (grad_first, vec_first) = outs[:4], outs[4:]

    def add_call(body, args, outs):
        args = [a.reshape(4, *a.shape[2:]) if a.ndim > 2 else a for a in args]
        return call(
            body,
            1,
            [whole_spec(a.shape) for a in args],
            [whole_spec(o.shape) for o in outs],
            outs,
            [],
            3,
            "add",
        )(*args)

    def plane_sum(parts):
        moved = [parts[0]]
        for k in (2, 1, 3):
            perm = [(j, j ^ k) for j in range(4)]
            moved.append(lax.ppermute(parts[k], ("lo", "y"), perm))
        return moved

    def add_moved(moved):
        value = (moved[0].astype(F32) + moved[1].astype(F32)) + moved[2].astype(F32)
        return (value + moved[3].astype(F32)).astype(BF16)

    def plane_total(keep, got, extra):
        part = in_dp_order(add_pair(keep, got))
        if extra is not None:
            part = jnp.concatenate([part, extra], axis=3)
        return total(spread_plane(part))

    input_first = from_seq(input_first)
    qkv_last = qkv
    output = collect(results)
    if fits:
        args = [up_keep, up_got, down_keep, down_got]
        args = lax.optimization_barrier((*args, grad_first, *results))[:4]
        piece = shape_of(up_keep.shape[2:], BF16)
        by_hi = shape_of((hi_count, 4, *down_keep.shape[3:]), BF16)
        *parts, down_part = add_call(add_mlp_body, args, [*[piece] * 4, by_hi])
        qkv_last = after(qkv, *parts, down_part)
        up_moved = plane_sum(parts)
        down_part = total(lax.all_to_all(down_part, "hi", 0, 0))
    quarter = 3 * width // 4
    shape = parts_shape(quarter)
    outs = call(
        functools.partial(back_last_body, dims),
        rows - lead,
        [
            *back_specs(lead),
            whole_spec((count, width)),
            whole_spec((lead_count, 3 * width)),
        ],
        [*[half_spec((1, part, width), 0)] * 4, vec_spec, ANY, ANY],
        [*last_shapes, shape_of((16, width), F32), shape_of(shape, BF16), shape_of(shape, BF16)],
        [
            pltpu.VMEM((count - lead_count, 3 * width), BF16),
            *back_scratch,
            turned,
            pltpu.VMEM((2, *shape), BF16),
            dma((n_piece,)),
            dma((2, dims[1], 2)),
        ],
        13,
        "back_last",
    )(place.at[4].set(lead), row_lengths, qkv_last, *back_args, *weights, vec_first, h_one, grad_first)
    input_last, (vec_last, qkv_keep, qkv_send) = outs[:4], outs[4:]
    if fits:
        qkv_send = after(qkv_send, *up_moved, *input_first)
    qkv_got = swap(qkv_send, "core")

    input_last = from_seq(input_last)
    if fits:
        _, _, _, more_rows, more_cols = qkv_keep.shape
        piece = shape_of((hi_count, more_rows + 16, more_cols), BF16)
        parts = add_call(add_qkv_body, [qkv_keep, qkv_got, vec_last], [piece] * 4)
        qkv_moved = plane_sum(parts)
        down_moved = plane_sum([down_part[k] for k in range(4)])
        up_plane = after(add_moved(up_moved), *parts)
        up_mine = total(lax.all_to_all(up_plane, "hi", 0, 0))
        down_mine = add_moved(down_moved)
        qkv_moved = lax.optimization_barrier((*qkv_moved, *input_last))[:4]
        qkv_plane = after(add_moved(qkv_moved), up_mine)
        qkv_mine = total(lax.all_to_all(qkv_plane, "hi", 0, 0))
    else:
        vec_total = vec_last.reshape(16, hi_count, 2, vec_cols)
        vec_total = vec_total.transpose(1, 0, 2, 3).reshape(1, 1, hi_count, 16, 2 * vec_cols)
        vec_total = jnp.pad(vec_total.astype(BF16), ((0, 0),) * 4 + ((0, quarter - 2 * vec_cols),))
        vec_total = jnp.broadcast_to(vec_total, (2, 2, *vec_total.shape[2:]))
        up_mine = total(lax.all_to_all(plane_total(up_keep, up_got, None), "hi", 0, 0))
        down_mine = total(lax.all_to_all(plane_total(down_keep, down_got, None), "hi", 0, 0))
        qkv_mine = plane_total(qkv_keep, qkv_got, vec_total)
        qkv_mine = total(lax.all_to_all(qkv_mine, "hi", 0, 0))
    mlp_mine = jnp.concatenate([up_mine, down_mine], axis=1)
    mlp_pieces = to_all(mlp_mine)
    attn_pieces = to_all(after(qkv_mine, *mlp_pieces))
    input_grad = collect([*input_first, *input_last])

    dp_count = 2 * hi_count
    if fits:
        pieces = [*mlp_pieces, *attn_pieces]
        piece_specs = [whole_spec(p.shape) for p in pieces]
        squares_shape = (dp_count, 8, 128)
        mlp_square = call(
            square_mlp_body,
            1,
            [SMEM, *piece_specs[:4]],
            whole_spec((8, 128)),
            shape_of((8, 128), F32),
            [],
            2,
            "mlp_squares",
        )(place, *mlp_pieces)
        squares = call(
            square_body,
            1,
            [SMEM, whole_spec((8, 128)), *piece_specs[4:]],
            whole_spec(squares_shape),
            shape_of(squares_shape, F32),
            [],
            1,
            "squares",
        )(place, mlp_square, *attn_pieces)
        squares = lax.all_to_all(squares, ("hi", "lo"), 0, 0)
        states = [attn_w, attn_m, attn_v, mlp_w, mlp_m, mlp_v, vec_w, vec_m, vec_v]
        state_specs = [whole_spec(v.shape) for v in states]
        norm, *new = call(
            adam_body,
            1,
            [SMEM, whole_spec(squares_shape), *piece_specs, *state_specs],
            [whole_spec((1, 1)), *state_specs],
            [shape_of((1, 1), F32), *[shape_of(v.shape, F32) for v in states]],
            [],
            6,
            "adam",
        )(place, squares, *pieces, *states)
        return (output, input_grad, *new, norm.reshape(()))

    vec_sum = attn_pieces[0][shard:].astype(F32) + attn_pieces[2][shard:].astype(F32)
    vec_sum = jnp.where(lo == 0, vec_sum[:, :vec_cols], vec_sum[:, vec_cols : 2 * vec_cols])
    vec_sum = vec_sum[:vec_rows]
    up_at = hidden // 4
    out_at = up_at + width // 4
    up_sum = in_columns([p[:, :up_at] for p in mlp_pieces], y, core)
    out_sum = in_columns([p[:, up_at:out_at] for p in mlp_pieces], y, core)
    down_sum = in_columns([p[:, out_at:] for p in mlp_pieces], y, core)
    qkv_sum = in_columns([p[:shard] for p in attn_pieces], y, core)
    attn_sum = jnp.concatenate([qkv_sum, out_sum], axis=1)
    mlp_sum = jnp.stack([up_sum, down_sum])
    square = jnp.sum(attn_sum * attn_sum) + jnp.sum(mlp_sum * mlp_sum) + jnp.sum(vec_sum * vec_sum)
    squares = lax.all_to_all(jnp.full((dp_count, 8, 128), square), ("hi", "lo"), 0, 0)
    grad_norm = jnp.sqrt(jnp.sum(squares[:, 0, 0]))
    clip_factor = CLIP_NORM / jnp.maximum(grad_norm, CLIP_NORM)
    attn_new = adam_update(
        attn_w, attn_m, attn_v, attn_sum * clip_factor, WEIGHT_DECAY, LEARN_RATE
    )
    mlp_new = adam_update(mlp_w, mlp_m, mlp_v, mlp_sum * clip_factor, WEIGHT_DECAY, LEARN_RATE)
    vec_new = adam_update(vec_w, vec_m, vec_v, vec_sum * clip_factor, 0.0, VEC_RATE)
    return (output, input_grad, *attn_new, *mlp_new, *vec_new, grad_norm)


def solution(mesh):
    dp_count = mesh.shape["dp"]
    seq_count = mesh.shape["seq"]
    fine = jax.sharding.Mesh(
        mesh.devices.reshape(dp_count // 2, 2, seq_count // 2, 2), ("hi", "lo", "y", "core")
    )
    dp = ("hi", "lo")
    seq = ("y", "core")
    acts = P(None, dp, seq, None)
    attn = P(dp, None)
    mlp = P(None, dp, None)
    vec = P(None, dp)
    return jax.shard_map(
        on_device,
        mesh=fine,
        in_specs=(acts, acts, P(None, dp), attn, attn, attn, mlp, mlp, mlp, vec, vec, vec),
        out_specs=(acts, acts, attn, attn, attn, mlp, mlp, mlp, vec, vec, vec, P()),
        check_vma=False,
    )
```

```python
import functools
import math

import jax
import jax.numpy as jnp
from jax import lax
from jax.experimental import pallas as pl
from jax.experimental.pallas import tpu as pltpu
from jax.sharding import PartitionSpec as P

HEADS = 8
ADAM_STEP = 10
CLIP_NORM = 1.0
BETA_ONE = 0.9
BETA_TWO = 0.999
LEARN_RATE = 0.08
VEC_RATE = 0.4
WEIGHT_DECAY = 0.01
ADAM_EPS = 1e-08
NORM_EPS = 1e-05

LIMITS = {"squares": 4, "mlp_squares": 4, "collect": 6, "attend": 8}
LIMIT = 63
F32 = jnp.float32
BF16 = jnp.bfloat16
ANY = pl.BlockSpec(memory_space=pl.ANY)
SMEM = pl.BlockSpec(memory_space=pltpu.SMEM)


def nt_dot(left, right):
    return lax.dot_general(left, right, (((1,), (1,)), ((), ())), preferred_element_type=F32)


def nn_dot(left, right):
    return jnp.dot(left, right, preferred_element_type=F32)


def centered(values):
    center = values - jnp.mean(values, axis=-1, keepdims=True)
    spread = jnp.mean(center * center, axis=-1, keepdims=True)
    scale = lax.rsqrt(spread + NORM_EPS)
    return center * scale, scale


def norm_back(unit, scale, grad):
    mean_grad = jnp.mean(grad, axis=-1, keepdims=True)
    mean_both = jnp.mean(grad * unit, axis=-1, keepdims=True)
    return scale * (grad - mean_grad - unit * mean_both)


def gelu_and_slope(up):
    share = 0.5 + 0.5 * lax.erf(up * (1.0 / math.sqrt(2.0)))
    bell = jnp.exp2(up * up * (-0.5 * math.log2(math.e)))
    return up * share, share + up * (bell * (1.0 / math.sqrt(2.0 * math.pi)))


def load_slots(refs):
    return jnp.concatenate([ref[i] for i in range(refs[0].shape[0]) for ref in refs], axis=0)


def store_slots(refs, value):
    rows, part, _ = refs[0].shape
    for i in range(rows):
        for k, ref in enumerate(refs):
            at = (i * 4 + k) * part
            ref[i] = value[at : at + part]


def placements(pieces, jobs, place, sems):
    lo = place[0]
    core = place[1]
    copies = []
    for i, piece in enumerate(pieces):
        lo_at = lo if i % 2 == 0 else 1 - lo
        core_at = core if i < 2 else 1 - core
        hi_count, rows, _ = piece.shape
        for h in range(hi_count):
            row = pl.multiple_of(((h * 2 + lo_at) * 2 + core_at) * rows, rows)
            for column, width, target, at in jobs:
                copies.append(
                    pltpu.make_async_copy(
                        piece.at[h, :, pl.ds(column, width)],
                        target.at[pl.ds(row, rows), pl.ds(at, width)],
                        sems.at[len(copies)],
                    )
                )
    return copies


def pair_placements(pieces, target, place, sems):
    copies = []
    for i, piece in enumerate(pieces):
        core_at = place[1] if i == 0 else 1 - place[1]
        hi_count, _, rows, _ = piece.shape
        for h in range(hi_count):
            for j in range(2):
                row = pl.multiple_of(((h * 2 + (place[0] ^ j)) * 2 + core_at) * rows, rows)
                copies.append(
                    pltpu.make_async_copy(
                        piece.at[h, j],
                        target.at[pl.ds(row, rows), pl.ds(0, piece.shape[-1])],
                        sems.at[len(copies)],
                    )
                )
    return copies


def head_masks(width):
    lane = lax.broadcasted_iota(jnp.int32, (1, width), 1)
    first = jnp.where(lane < width // 2, 1.0, 0.0)
    return first.astype(BF16), (1.0 - first).astype(BF16)


def fill_bias(place, lengths, row, bias):
    part = bias.shape[0] // 4
    for k in range(4):
        base = (place[2] ^ k) * part
        slot = lax.broadcasted_iota(jnp.int32, (part, bias.shape[1]), 0) + base
        bias[k * part : (k + 1) * part, :] = jnp.where(slot < lengths[row], 0.0, -1e30)


def qkv_body(place, x0, x1, x2, x3, p0, p1, p2, p3, vec, h_out, qkv_out, w_qkv, sems):
    row = pl.program_id(0)
    width = vec.shape[1]
    copies = placements((p0, p1, p2, p3), [(0, 3 * width, w_qkv, 0)], place, sems)

    @pl.when(row == 0)
    def _():
        for copy in copies:
            copy.start()

    x = load_slots((x0, x1, x2, x3)).astype(F32)
    unit, _ = centered(x)
    h = (unit * vec[0:1] + vec[1:2]).astype(BF16)
    h_out[...] = h

    @pl.when(row == 0)
    def _():
        for copy in copies:
            copy.wait()

    q = nn_dot(h, w_qkv[:, :width]).astype(BF16)
    qkv_out[:, :width] = q * jnp.asarray(1.0 / math.sqrt(width // HEADS), BF16)
    qkv_out[:, width:] = nn_dot(h, w_qkv[:, width:]).astype(BF16)


def attend_body(place, lengths, qkv, *refs):
    attn_out, lse_out, bias = refs[-3:]
    row = pl.program_id(0) + place[4]
    width = attn_out.shape[1]
    pair = 2 * (width // HEADS)
    half = pair // 2
    fill_bias(place, lengths, row, bias)
    masks = head_masks(pair)

    def score(h):
        at = (h // 2) * pair
        return nt_dot(qkv[:, width + at : width + at + pair], qkv[:, at : at + pair] * masks[h % 2])

    def soft(h, scores):
        scores = scores + bias[...]
        top = jnp.max(scores, axis=0, keepdims=True)
        grown = jnp.exp(scores - top)
        total = jnp.sum(grown, axis=0, keepdims=True)
        lse_out[0, h : h + 1, :] = top + jnp.log(total)
        return (grown * (1.0 / total)).astype(BF16)

    def value(h, turned, probs):
        return nn_dot(turned[(h % 2) * half : (h % 2 + 1) * half], probs)

    turned = [qkv[:, 2 * width + p * pair : 2 * width + (p + 1) * pair].T for p in range(HEADS // 2)]
    scores = [score(h) for h in range(HEADS)]
    probs = [soft(h, scores[h]) for h in range(HEADS)]
    outs = [value(h, turned[h // 2], probs[h]) for h in range(HEADS)]
    for p in range(HEADS // 2):
        attn_out[:, p * pair : (p + 1) * pair] = jnp.concatenate(outs[2 * p : 2 * p + 2], axis=0).T.astype(BF16)


def write_parts(parts, half, y, column, value, dims):
    hi_count, lo_count, rows = dims
    quarter = value.shape[1]
    value = value.astype(BF16)
    for h in range(hi_count):
        for lo in range(lo_count):
            at = (h * lo_count + lo) * rows
            parts[half, lo, y, h, :, column : column + quarter] = value[at : at + rows]


def send_copies(parts, half, y, keep, send, place, sems):
    mine = half == place[3]
    copies = []
    for i in range(parts.shape[1]):
        for target, wanted in ((keep, mine), (send, jnp.logical_not(mine))):
            lo_count = parts.shape[1]
            copy = pltpu.make_async_copy(
                parts.at[half, i, y],
                target.at[(place[5] ^ i) if lo_count > 1 else 0, place[6] ^ y],
                sems.at[half, i, y],
            )
            copies.append((wanted, copy))
    return copies


def start_all(copies):
    for wanted, copy in copies:
        pl.when(wanted)(copy.start)


def wait_all(copies):
    for wanted, copy in copies:
        pl.when(wanted)(copy.wait)


def mlp_body(
    dims, place, x0, x1, x2, x3, attn, d0, d1, d2, d3, b0, b1, b2, b3, c0, c1, vec,
    o0, o1, o2, o3, dx_out, dattn_out, vec_out, up_keep, up_send, down_keep, down_send,
    w_out, w_up, w_down, h_turned, attn_turned, dy_turned, act_all, dup_all, dao_all,
    up_parts, down_parts, out_sems, up_sems, down_sems, part_sems, more_sems,
):
    row = pl.program_id(0)
    width = vec.shape[1]
    hidden = w_up.shape[1]
    slots = attn.shape[0]
    out_copies = placements((b0, b1, b2, b3), [(0, width, w_out, 0)], place, out_sems)
    split = c0.shape[-1]
    jobs = [(width, hidden, w_up, 0), (width + hidden, hidden - split, w_down, split)]
    up_copies = placements((b0, b1, b2, b3), jobs, place, up_sems)
    down_copies = pair_placements((c0, c1), w_down, place, down_sems)

    def arrived(copies):
        @pl.when(row == 0)
        def _():
            for copy in copies:
                copy.wait()

    @pl.when(row == 0)
    def _():
        vec_out[...] = jnp.zeros_like(vec_out)
        for copy in out_copies + up_copies + down_copies:
            copy.start()

    here = pl.ds(pl.multiple_of(row * slots, slots), slots)
    x = load_slots((x0, x1, x2, x3)).astype(F32)
    dy = load_slots((d0, d1, d2, d3))
    dy_turned[:, here] = dy.T
    attn_turned[:, here] = attn[...].T
    arrived(out_copies)
    x_one = x + (nn_dot(attn[...], w_out[...]) + vec[4:5])
    unit, scale = centered(x_one)
    h = (unit * vec[2:3] + vec[3:4]).astype(BF16)
    h_turned[:, here] = h.T
    arrived(up_copies)
    arrived(down_copies)
    for j in range(hidden // width):
        columns = slice(j * width, (j + 1) * width)
        up = nn_dot(h, w_up[:, columns]) + vec[6 + j : 7 + j]
        act, slope = gelu_and_slope(up)
        act_all[here, columns] = act.astype(BF16)
        dup = (slope * nn_dot(dy, w_down[:, columns])).astype(BF16)
        dup_all[here, columns] = dup
        vec_out[6 + j : 7 + j] += jnp.sum(dup.astype(F32), axis=0, keepdims=True)
    result = x_one + (nt_dot(act_all[here, :], w_down[...]) + vec[5:6])
    store_slots((o0, o1, o2, o3), result.astype(BF16))
    dh = nt_dot(dup_all[here, :], w_up[...])
    vec_out[2:3] += jnp.sum(dh * unit, axis=0, keepdims=True)
    vec_out[3:4] += jnp.sum(dh, axis=0, keepdims=True)
    dy_float = dy.astype(F32)
    dx = dy_float + norm_back(unit, scale, dh * vec[2:3])
    dx_out[...] = dx
    dao = dx.astype(BF16)
    dao_all[here, :] = dao
    vec_out[4:5] += jnp.sum(dao.astype(F32), axis=0, keepdims=True)
    vec_out[5:6] += jnp.sum(dy_float, axis=0, keepdims=True)
    dattn_out[...] = nt_dot(dao, w_out[...]).astype(BF16)

    @pl.when(row == pl.num_programs(0) - 1)
    def _():
        quarter = hidden // 4
        small = width // 4
        copies = []
        for half in range(2):
            for y in range(2):
                at = (half * 2 + y) * quarter
                value = nn_dot(h_turned[...], dup_all[:, at : at + quarter])
                write_parts(up_parts, half, y, 0, value, dims)
                value = nn_dot(dy_turned[...], act_all[:, at : at + quarter])
                write_parts(down_parts, half, y, 0, value, dims)
                at = (half * 2 + y) * small
                value = nn_dot(attn_turned[...], dao_all[:, at : at + small])
                write_parts(up_parts, half, y, quarter, value, dims)
                these = send_copies(up_parts, half, y, up_keep, up_send, place, part_sems)
                these += send_copies(down_parts, half, y, down_keep, down_send, place, more_sems)
                start_all(these)
                copies += these
        wait_all(copies)


def back_rows(
    place, lengths, qkv, lse, dattn, xs, dx, pieces, vec, sums, outs, dqkv, vec_out, w_qkv, bias, sems
):
    step = pl.program_id(0)
    width = vec.shape[1]
    slots = qkv.shape[0]
    pair = 2 * (width // HEADS)
    score_scale = 1.0 / math.sqrt(width // HEADS)
    copies = placements(pieces, [(0, 3 * width, w_qkv, 0)], place, sems)

    @pl.when(step == 0)
    def _():
        vec_out[...] = sums[...]
        for copy in copies:
            copy.start()

    fill_bias(place, lengths, step + place[4], bias)
    masks = head_masks(pair)
    half = pair // 2
    pairs = range(HEADS // 2)

    def part(base, p):
        return qkv[:, base + p * pair : base + (p + 1) * pair]

    grads = [dattn[:, p * pair : (p + 1) * pair] for p in pairs]
    qs = [part(0, h // 2) * masks[h % 2] for h in range(HEADS)]
    gs = [grads[h // 2] * masks[h % 2] for h in range(HEADS)]
    k_turned = [part(width, p).T for p in pairs]
    scores = [nt_dot(part(width, h // 2), qs[h]) for h in range(HEADS)]
    dprobs = [nt_dot(part(2 * width, h // 2), gs[h]) for h in range(HEADS)]
    probs_low, ds = [], []
    for h in range(HEADS):
        probs = jnp.exp(scores[h] + bias[...] - lse[0, h : h + 1, :])
        inner = jnp.sum(probs * dprobs[h], axis=0, keepdims=True)
        ds.append((probs * (dprobs[h] - inner)).astype(BF16))
        probs_low.append(probs.astype(BF16))
    dqs = [nn_dot(k_turned[h // 2][(h % 2) * half : (h % 2 + 1) * half], ds[h]) for h in range(HEADS)]
    for p in pairs:
        two = slice(2 * p, 2 * p + 2)
        queries, given = jnp.concatenate(qs[two], axis=0), jnp.concatenate(gs[two], axis=0)
        dk = nn_dot(jnp.concatenate(ds[two], axis=1), queries)
        dv = nn_dot(jnp.concatenate(probs_low[two], axis=1), given)
        dq = jnp.concatenate(dqs[two], axis=0).T * score_scale
        dqkv[:, p * pair : (p + 1) * pair] = dq.astype(BF16)
        dqkv[:, width + p * pair : width + (p + 1) * pair] = dk.astype(BF16)
        dqkv[:, 2 * width + p * pair : 2 * width + (p + 1) * pair] = dv.astype(BF16)

    @pl.when(step == 0)
    def _():
        for copy in copies:
            copy.wait()

    dh = nt_dot(dqkv[...], w_qkv[...])
    x = load_slots(xs).astype(F32)
    unit, scale = centered(x)
    vec_out[0:1] += jnp.sum(dh * unit, axis=0, keepdims=True)
    vec_out[1:2] += jnp.sum(dh, axis=0, keepdims=True)
    grad = (dx[...] + norm_back(unit, scale, dh * vec[0:1])).astype(BF16)
    store_slots(outs, grad)


def back_first_body(
    place, lengths, qkv, lse, dattn, x0, x1, x2, x3, dx, p0, p1, p2, p3, vec, sums,
    o0, o1, o2, o3, dqkv_out, vec_out, w_qkv, bias, sems,
):
    back_rows(
        place, lengths, qkv, lse, dattn, (x0, x1, x2, x3), dx, (p0, p1, p2, p3), vec, sums,
        (o0, o1, o2, o3), dqkv_out, vec_out, w_qkv, bias, sems,
    )


def back_last_body(
    dims, place, lengths, qkv, lse, dattn, x0, x1, x2, x3, dx, p0, p1, p2, p3, vec, sums,
    h_one, before,
    o0, o1, o2, o3, vec_out, keep, send, dqkv, w_qkv, bias, h_turned, parts, sems, out_sems,
):
    step = pl.program_id(0)
    slots = qkv.shape[0]
    here = pl.ds(pl.multiple_of(step * slots, slots), slots)
    back_rows(
        place, lengths, qkv, lse, dattn, (x0, x1, x2, x3), dx, (p0, p1, p2, p3), vec, sums,
        (o0, o1, o2, o3), dqkv.at[here], vec_out, w_qkv, bias, sems,
    )

    @pl.when(step == pl.num_programs(0) - 1)
    def _():
        count = before.shape[0]
        h_turned[...] = h_one[...].T
        quarter = before.shape[1] // 4
        copies = []
        for half in range(2):
            for y in range(2):
                at = (half * 2 + y) * quarter
                value = nn_dot(h_turned[:, :count], before[:, at : at + quarter])
                value = value + nn_dot(h_turned[:, count:], dqkv[:, at : at + quarter])
                write_parts(parts, half, y, 0, value, dims)
                these = send_copies(parts, half, y, keep, send, place, out_sems)
                start_all(these)
                copies += these
        wait_all(copies)


def add_mlp_body(keep, got, down_keep, down_got, *outs):
    for k in range(4):
        outs[k][...] = (keep[k].astype(F32) + got[k].astype(F32)).astype(BF16)
        outs[4][:, k] = (down_keep[k].astype(F32) + down_got[k].astype(F32)).astype(BF16)


def add_qkv_body(keep, got, vec, *outs):
    rows = keep.shape[2]
    sums = vec[...]
    for k, out in enumerate(outs):
        out[:, :rows, :] = (keep[k].astype(F32) + got[k].astype(F32)).astype(BF16)
        out[:, rows:, :] = jnp.zeros((out.shape[0], 16, out.shape[2]), BF16)
        lanes = sums.shape[1] // out.shape[0]
        for h in range(out.shape[0]):
            out[h, rows:, :lanes] = sums[:, h * lanes : (h + 1) * lanes].astype(BF16)


def collect_body(place, *refs):
    out = refs[-1]
    at = 0
    for i in range(0, len(refs) - 1, 4):
        count = refs[i].shape[0]
        for k in range(4):
            out[place[2] ^ k, at : at + count] = refs[i + k][...]
        at += count


def in_order(values, place):
    core, y = place[3], place[7]
    near = (jnp.where(y == 0, values[0], values[1]), jnp.where(y == 0, values[1], values[0]))
    far = (jnp.where(y == 0, values[2], values[3]), jnp.where(y == 0, values[3], values[2]))
    first = (jnp.where(core == 0, near[0], far[0]), jnp.where(core == 0, near[1], far[1]))
    second = (jnp.where(core == 0, far[0], near[0]), jnp.where(core == 0, far[1], near[1]))
    return (*first, *second)


def vec_sums(a0, a2, place, shard):
    lanes = 128
    own = a0[shard:, :lanes].astype(F32)
    far = a2[shard:, :lanes].astype(F32)
    both = own + far
    lane = lax.broadcasted_iota(jnp.int32, both.shape, 1) // (lanes // 2)
    return jnp.where(lane == place[8], both, 0.0)


def square_mlp_body(place, m0, m1, m2, m3, out):
    values = []
    for mlp in (m0, m1, m2, m3):
        value = mlp[...].astype(F32)
        values.append(jnp.sum(value * value))
    first, second, third, fourth = in_order(values, place)
    out[...] = jnp.full(out.shape, (first + second) + (third + fourth), F32)


def square_body(place, before, a0, a1, a2, a3, out):
    shard = a0.shape[0] - 16
    values = []
    for attn in (a0, a1, a2, a3):
        value = attn[:shard].astype(F32)
        values.append(jnp.sum(value * value))
    vec = vec_sums(a0, a2, place, shard)
    first, second, third, fourth = in_order(values, place)
    value = ((first + second) + (third + fourth)) + jnp.sum(vec * vec)
    total_value = before[...] + value
    for d in range(out.shape[0]):
        out[d] = total_value


def adam_parts(weight, moment, second, grad, decay, rate):
    moment_new = BETA_ONE * moment + (1.0 - BETA_ONE) * grad
    second_new = BETA_TWO * second + (1.0 - BETA_TWO) * grad * grad
    first_hat = moment_new * (1.0 / (1.0 - BETA_ONE**ADAM_STEP))
    second_hat = second_new * (1.0 / (1.0 - BETA_TWO**ADAM_STEP))
    step = first_hat / (jnp.sqrt(second_hat) + ADAM_EPS)
    return weight - rate * (step + decay * weight), moment_new, second_new


def adam_body(
    place, squares, m0, m1, m2, m3, a0, a1, a2, a3,
    attn_w, attn_m, attn_v, mlp_w, mlp_m, mlp_v, vec_w, vec_m, vec_v,
    norm_out, attn_wo, attn_mo, attn_vo, mlp_wo, mlp_mo, mlp_vo, vec_wo, vec_mo, vec_vo,
):
    shard = m0.shape[0]
    hidden = mlp_w.shape[2]
    quarter = hidden // 4
    wide = a0.shape[1]
    small = m0.shape[1] - 2 * quarter
    value = squares[0]
    for d in range(1, squares.shape[0]):
        value = value + squares[d]
    norm = jnp.sqrt(value)
    norm_out[...] = norm[0:1, 0:1]
    factor = (CLIP_NORM / jnp.maximum(norm, CLIP_NORM))[0:1, 0:1]
    rows, cols = vec_w.shape
    vec = vec_sums(a0, a2, place, shard)
    grad = (vec[:rows, :cols] + vec[:rows, cols : 2 * cols]) * factor
    parts = adam_parts(vec_w[...], vec_m[...], vec_v[...], grad, 0.0, VEC_RATE)
    for new, new_value in zip((vec_wo, vec_mo, vec_vo), parts):
        new[...] = new_value
    core, y = place[3], place[7]
    olds = (attn_w, attn_m, attn_v)
    news = (attn_wo, attn_mo, attn_vo)
    mlp_olds = (mlp_w, mlp_m, mlp_v)
    mlp_news = (mlp_wo, mlp_mo, mlp_vo)
    for i, (mlp, attn) in enumerate(((m0, a0), (m1, a1), (m2, a2), (m3, a3))):
        side = (core if i < 2 else 1 - core) * 2 + (y if i % 2 == 0 else 1 - y)

        def columns(base, size, side=side):
            return pl.ds(pl.multiple_of(base + side * size, 128), size)

        at = columns(0, wide)
        grad = attn[:shard].astype(F32) * factor
        for new, new_value in zip(news, adam_parts(*[o[:, at] for o in olds], grad, WEIGHT_DECAY, LEARN_RATE)):
            new[:, at] = new_value
        at = columns(4 * wide, small)
        grad = mlp[:, quarter : quarter + small].astype(F32) * factor
        for new, new_value in zip(news, adam_parts(*[o[:, at] for o in olds], grad, WEIGHT_DECAY, LEARN_RATE)):
            new[:, at] = new_value
        at = columns(0, quarter)
        for j, start in ((0, 0), (1, quarter + small)):
            grad = mlp[:, start : start + quarter].astype(F32) * factor
            parts = adam_parts(*[o[j, :, at] for o in mlp_olds], grad, WEIGHT_DECAY, LEARN_RATE)
            for new, new_value in zip(mlp_news, parts):
                new[j, :, at] = new_value


def shape_of(dims, dtype):
    return jax.ShapeDtypeStruct(dims, dtype)


def rows_spec(rows, cols):
    return pl.BlockSpec((rows, cols), lambda r: (r, 0))


def whole_spec(shape):
    return pl.BlockSpec(shape, lambda r: (0,) * len(shape))


def call(body, grid, in_specs, out_specs, out_shape, scratch, cost, name, aliases=None):
    return pl.pallas_call(
        body,
        grid=(grid,),
        in_specs=in_specs,
        out_specs=out_specs,
        out_shape=out_shape,
        scratch_shapes=scratch,
        input_output_aliases=aliases or {},
        compiler_params=pltpu.CompilerParams(
            vmem_limit_bytes=LIMITS.get(name, LIMIT) * 2**20,
            dimension_semantics=("arbitrary",),
        ),
        cost_estimate=pl.CostEstimate(
            flops=int(cost * 5e8), bytes_accessed=int(cost * 1e6), transcendentals=0
        ),
        name=name,
    )


def swap(value, axis):
    return lax.ppermute(value, axis, [(0, 1), (1, 0)])


def ordered(own, other, index, axis):
    first = jnp.where(index == 0, own, other)
    second = jnp.where(index == 0, other, own)
    return jnp.stack([first, second], axis)


def from_seq(pieces):
    moved = [pieces[0]]
    for k in range(1, 4):
        moved.append(lax.ppermute(pieces[k], ("y", "core"), [(j, j ^ k) for j in range(4)]))
    return moved


def spread_hi(half):
    hi_count = lax.axis_size("hi")
    spread = jnp.broadcast_to(half[None], (hi_count, *half.shape))
    return lax.all_to_all(spread, "hi", 0, 0)


def share(own):
    other = swap(own, "lo")
    return [own, other, swap(own, "core"), swap(other, "core")]


def settle(pieces, lo, core, groups=4):
    near = ordered(pieces[0], pieces[1], lo, 1)
    far = ordered(pieces[2], pieces[3], lo, 1)
    whole = ordered(near, far, core, 2)
    cols = whole.shape[-1]
    whole = whole.reshape(groups, 2, 2, -1, cols)
    return [whole[:, 0, 0], whole[:, 1, 0], whole[:, 0, 1], whole[:, 1, 1]]


def add_pair(keep, got):
    return (keep.astype(F32) + got.astype(F32)).astype(BF16)


def spread_plane(part):
    part = part.reshape(4, *part.shape[2:])
    return lax.all_to_all(part, ("lo", "y"), 0, 0)


def total(part):
    return jnp.sum(part.astype(F32), axis=0).astype(BF16)


def to_all(mine):
    return [mine] + [
        lax.ppermute(mine, ("y", "core"), [(j, j ^ k) for j in range(4)]) for k in (2, 1, 3)
    ]


def after(value, *others):
    return lax.optimization_barrier((value, *others))[0]


def in_columns(pieces, y, core):
    near = ordered(pieces[0], pieces[1], y, 1)
    far = ordered(pieces[2], pieces[3], y, 1)
    both = ordered(near, far, core, 1)
    return both.reshape(both.shape[0], -1).astype(F32)


def adam_update(weight, moment, second, grad, decay, rate):
    moment_new = BETA_ONE * moment + (1.0 - BETA_ONE) * grad
    second_new = BETA_TWO * second + (1.0 - BETA_TWO) * grad * grad
    first_hat = moment_new / (1.0 - BETA_ONE**ADAM_STEP)
    second_hat = second_new / (1.0 - BETA_TWO**ADAM_STEP)
    weight_new = weight - rate * (first_hat / (jnp.sqrt(second_hat) + ADAM_EPS) + decay * weight)
    return (weight_new, moment_new, second_new)


def on_device(
    tokens, cotangent, lengths, attn_w, attn_m, attn_v, mlp_w, mlp_m, mlp_v, vec_w, vec_m, vec_v
):
    lo = lax.axis_index("lo")
    y = lax.axis_index("y")
    core = lax.axis_index("core")
    hi_count = lax.axis_size("hi")
    me = y * 2 + core
    micro_count, row_count, part, width = tokens.shape
    hidden = mlp_w.shape[2]
    shard = attn_w.shape[0]
    slots = 4 * part
    rows = micro_count * row_count // 4
    count = rows * slots
    vec_rows, vec_cols = vec_w.shape
    half_rows = shard // 2
    fits = half_rows % 16 == 0

    flat_tokens = tokens.reshape(4, rows, part, width)
    flat_cot = cotangent.reshape(4, rows, part, width)

    def pick(stack, k):
        return lax.dynamic_index_in_dim(stack, me ^ k, 0, keepdims=False)

    def half_of(value):
        return lax.dynamic_slice_in_dim(value, core * half_rows, half_rows, 0)

    xs = from_seq([pick(flat_tokens, k) for k in range(4)])
    lanes = 128
    ride = jnp.pad(vec_w.reshape(-1), (0, half_rows * lanes - vec_w.size)).reshape(half_rows, lanes)
    first_half = jnp.concatenate([half_of(attn_w[:, : 3 * width]), ride], axis=1).astype(BF16)
    qkv_own = spread_hi(first_half)
    split = 3 * hidden // 4
    up_half = jnp.concatenate(
        [half_of(attn_w[:, 3 * width :]), half_of(mlp_w[0]), half_of(mlp_w[1, :, split:])], axis=1
    )
    up_own = spread_hi(after(up_half.astype(BF16), qkv_own))
    qkv_own, xs[3] = lax.optimization_barrier((qkv_own, xs[3]))
    qkv_other = swap(qkv_own, "lo")
    qkv_pieces = [qkv_own, qkv_other, swap(qkv_own, "core"), swap(qkv_other, "core")]
    vec_all = ordered(qkv_pieces[0][:, :, 3 * width :], qkv_pieces[1][:, :, 3 * width :], lo, 1)
    vec_all = vec_all.reshape(2 * hi_count, -1)[:, : vec_w.size].reshape(-1, vec_rows, vec_cols)
    vec_all = vec_all.transpose(1, 0, 2).reshape(vec_rows, width)
    vec_float = jnp.pad(vec_all.astype(F32), ((0, 16 - vec_rows), (0, 0)))

    if fits:
        places = [lo, core, me, core, 0 * lo, lo, y, y, lo]
        dims = (hi_count, 2, shard)
    else:
        qkv_pieces = settle(qkv_pieces, lo, core)
        places = [0 * lo, 0 * lo, me, core, 0 * lo, 0 * lo, 0 * lo, y, lo]
        dims = (1, 1, width)
    place = jnp.stack(places).astype(jnp.int32)
    later = place.at[4].set(rows // 2)
    row_lengths = lax.dynamic_slice_in_dim(lengths.reshape(-1), me * rows, rows)

    vec_spec = whole_spec((16, width))
    lse_spec = pl.BlockSpec((1, HEADS, slots), lambda r: (r, 0, 0))
    group = 2 if rows % 2 == 0 else 1
    slot_spec = pl.BlockSpec((group, part, width), lambda r: (r, 0, 0))
    narrow = rows_spec(group * slots, width)
    wide_qkv = rows_spec(group * slots, 3 * width)
    triple = rows_spec(slots, 3 * width)
    n_piece = 4 * qkv_pieces[0].shape[0]
    dma = pltpu.SemaphoreType.DMA
    h_one, qkv = call(
        qkv_body,
        rows // group,
        [SMEM, *[slot_spec] * 4, *[ANY] * 4, vec_spec],
        [narrow, wide_qkv],
        [shape_of((count, width), BF16), shape_of((count, 3 * width), BF16)],
        [pltpu.VMEM((width, 3 * width), BF16), dma((n_piece,))],
        7,
        "qkv",
    )(place, *xs, *qkv_pieces, vec_float)

    down_half = after(half_of(mlp_w[1, :, :split]).astype(BF16), qkv_other)
    down_pair = jnp.stack(lax.optimization_barrier((down_half, swap(down_half, "lo"), h_one))[:2])
    down_own = spread_hi(after(down_pair, up_own))
    cot = after(flat_cot, qkv_other)
    dys = from_seq([pick(cot, k) for k in range(4)])
    qkv, up_own = lax.optimization_barrier((qkv, up_own))
    up_other = swap(up_own, "lo")

    def half_spec(block, base):
        zeros = (0,) * (len(block) - 1)
        return pl.BlockSpec(block, lambda r: (r + base, *zeros))

    def attend(qkv, base, steps, before):
        return call(
            attend_body,
            steps,
            [SMEM, SMEM, half_spec((slots, 3 * width), base), *[ANY] * len(before)],
            [half_spec((slots, width), base), half_spec((1, HEADS, slots), base)],
            [shape_of((count, width), BF16), shape_of((rows, HEADS, slots), F32)],
            [pltpu.VMEM((slots, slots), F32)],
            4 * steps,
            "attend",
            {3: 0, 4: 1} if before else None,
        )(place.at[4].set(base), row_lengths, qkv, *before)

    up_far = swap(up_own, "core")
    attn, lse = attend(qkv, 0, rows - 1, [])
    up_other, up_far, attn, lse, *dys = lax.optimization_barrier(
        (up_other, up_far, attn, lse, *dys)
    )
    attn, lse = attend(qkv, rows - 1, 1, [attn, lse])
    up_pieces = [up_own, up_other, up_far, swap(up_other, "core")]
    down_own = after(down_own, attn)
    down_far = swap(down_own, "core")
    down_pieces = [down_own, down_far]
    if not fits:
        up_pieces = settle(up_pieces, lo, core)
        split = settle([p[:, j] for p in down_pieces for j in range(2)], lo, core)
        down_pieces = [jnp.stack(split[:2], axis=1), jnp.stack(split[2:], axis=1)]
    n_down = 4 * down_pieces[0].shape[0]

    def parts_shape(quarter):
        return (dims[1], 2, dims[0], dims[2], quarter)

    def in_dp_order(value):
        if fits:
            return value
        value = value.reshape(2, hi_count, 2, shard, value.shape[-1])
        return value.transpose(2, 0, 1, 3, 4)

    turned = pltpu.VMEM((width, count), BF16)
    shape = parts_shape(hidden // 4 + width // 4)
    down_shape = parts_shape(hidden // 4)
    outs = call(
        functools.partial(mlp_body, dims),
        rows // group,
        [SMEM, *[slot_spec] * 4, narrow, *[slot_spec] * 4, *[ANY] * 6, vec_spec],
        [*[slot_spec] * 4, narrow, narrow, vec_spec, *[ANY] * 4],
        [
            *[shape_of((rows, part, width), BF16)] * 4,
            shape_of((count, width), F32),
            shape_of((count, width), BF16),
            shape_of((16, width), F32),
            *[shape_of(shape, BF16)] * 2,
            *[shape_of(down_shape, BF16)] * 2,
        ],
        [
            pltpu.VMEM((width, width), BF16),
            pltpu.VMEM((width, hidden), BF16),
            pltpu.VMEM((width, hidden), BF16),
            turned,
            turned,
            turned,
            pltpu.VMEM((count, hidden), BF16),
            pltpu.VMEM((count, hidden), BF16),
            pltpu.VMEM((count, width), BF16),
            pltpu.VMEM((2, *shape), BF16),
            pltpu.VMEM((2, *down_shape), BF16),
            dma((n_piece,)),
            dma((2 * n_piece,)),
            dma((n_down,)),
            dma((2, dims[1], 2)),
            dma((2, dims[1], 2)),
        ],
        24,
        "mlp",
    )(place, *xs, attn, *dys, *up_pieces, *down_pieces, vec_float)
    results, (dx, dattn, vec_mlp, up_keep, up_send, down_keep, down_send) = outs[:4], outs[4:]
    up_got = swap(up_send, "core")
    down_got = swap(down_send, "core")

    def collect(parts):
        out = (4, rows, part, width)
        return call(
            collect_body,
            1,
            [SMEM, *[whole_spec(p.shape) for p in parts]],
            whole_spec(out),
            shape_of(out, BF16),
            [],
            2,
            "collect",
        )(place, *parts).reshape(tokens.shape)

    results = from_seq(results)
    lead = 2
    lead_count = lead * slots
    back_args = [lse, dattn, *xs, dx]
    weights = [*qkv_pieces, vec_float]

    def back_specs(base):
        return [
            SMEM,
            SMEM,
            half_spec((slots, 3 * width), base),
            half_spec((1, HEADS, slots), base),
            half_spec((slots, width), base),
            *[half_spec((1, part, width), base)] * 4,
            half_spec((slots, width), base),
            *[ANY] * 4,
            vec_spec,
            vec_spec,
        ]

    first_shapes = [shape_of((lead, part, width), BF16)] * 4
    last_shapes = [shape_of((rows - lead, part, width), BF16)] * 4
    back_scratch = [pltpu.VMEM((width, 3 * width), BF16), pltpu.VMEM((slots, slots), F32)]
    outs = call(
        back_first_body,
        lead,
        back_specs(0),
        [*[half_spec((1, part, width), 0)] * 4, triple, vec_spec],
        [*first_shapes, shape_of((lead_count, 3 * width), BF16), shape_of((16, width), F32)],
        [*back_scratch, dma((n_piece,))],
        11,
        "back_first",
    )(place, row_lengths, after(qkv, up_send, down_send), *back_args, *weights, vec_mlp)
    input_first, (grad_first, vec_first) = outs[:4], outs[4:]

    def add_call(body, args, outs):
        args = [a.reshape(4, *a.shape[2:]) if a.ndim > 2 else a for a in args]
        return call(
            body,
            1,
            [whole_spec(a.shape) for a in args],
            [whole_spec(o.shape) for o in outs],
            outs,
            [],
            3,
            "add",
        )(*args)

    def plane_sum(parts):
        moved = [parts[0]]
        for k in (2, 1, 3):
            perm = [(j, j ^ k) for j in range(4)]
            moved.append(lax.ppermute(parts[k], ("lo", "y"), perm))
        return moved

    def add_moved(moved):
        value = (moved[0].astype(F32) + moved[1].astype(F32)) + moved[2].astype(F32)
        return (value + moved[3].astype(F32)).astype(BF16)

    def plane_total(keep, got, extra):
        part = in_dp_order(add_pair(keep, got))
        if extra is not None:
            part = jnp.concatenate([part, extra], axis=3)
        return total(spread_plane(part))

    input_first = from_seq(input_first)
    qkv_last = qkv
    output = collect(results)
    if fits:
        args = [up_keep, up_got, down_keep, down_got]
        args = lax.optimization_barrier((*args, grad_first, *results[:3]))[:4]
        piece = shape_of(up_keep.shape[2:], BF16)
        by_hi = shape_of((hi_count, 4, *down_keep.shape[3:]), BF16)
        *parts, down_part = add_call(add_mlp_body, args, [*[piece] * 4, by_hi])
        qkv_last = after(qkv, *parts, down_part)
        up_moved = plane_sum(parts)
        down_part = total(lax.all_to_all(down_part, "hi", 0, 0))
    quarter = 3 * width // 4
    shape = parts_shape(quarter)
    outs = call(
        functools.partial(back_last_body, dims),
        rows - lead,
        [
            *back_specs(lead),
            whole_spec((count, width)),
            whole_spec((lead_count, 3 * width)),
        ],
        [*[half_spec((1, part, width), 0)] * 4, vec_spec, ANY, ANY],
        [*last_shapes, shape_of((16, width), F32), shape_of(shape, BF16), shape_of(shape, BF16)],
        [
            pltpu.VMEM((count - lead_count, 3 * width), BF16),
            *back_scratch,
            turned,
            pltpu.VMEM((2, *shape), BF16),
            dma((n_piece,)),
            dma((2, dims[1], 2)),
        ],
        13,
        "back_last",
    )(place.at[4].set(lead), row_lengths, qkv_last, *back_args, *weights, vec_first, h_one, grad_first)
    input_last, (vec_last, qkv_keep, qkv_send) = outs[:4], outs[4:]
    if fits:
        qkv_send = after(qkv_send, *up_moved, *input_first)
    qkv_got = swap(qkv_send, "core")

    input_last = from_seq(input_last)
    if fits:
        _, _, _, more_rows, more_cols = qkv_keep.shape
        piece = shape_of((hi_count, more_rows + 16, more_cols), BF16)
        parts = add_call(add_qkv_body, [qkv_keep, qkv_got, vec_last], [piece] * 4)
        qkv_moved = plane_sum(parts)
        down_moved = plane_sum([down_part[k] for k in range(4)])
        up_plane = after(add_moved(up_moved), *parts)
        up_mine = total(lax.all_to_all(up_plane, "hi", 0, 0))
        down_mine = add_moved(down_moved)
        qkv_moved = lax.optimization_barrier((*qkv_moved, *input_last))[:4]
        qkv_plane = after(add_moved(qkv_moved), up_mine)
        qkv_mine = total(lax.all_to_all(qkv_plane, "hi", 0, 0))
    else:
        vec_total = vec_last.reshape(16, hi_count, 2, vec_cols)
        vec_total = vec_total.transpose(1, 0, 2, 3).reshape(1, 1, hi_count, 16, 2 * vec_cols)
        vec_total = jnp.pad(vec_total.astype(BF16), ((0, 0),) * 4 + ((0, quarter - 2 * vec_cols),))
        vec_total = jnp.broadcast_to(vec_total, (2, 2, *vec_total.shape[2:]))
        up_mine = total(lax.all_to_all(plane_total(up_keep, up_got, None), "hi", 0, 0))
        down_mine = total(lax.all_to_all(plane_total(down_keep, down_got, None), "hi", 0, 0))
        qkv_mine = plane_total(qkv_keep, qkv_got, vec_total)
        qkv_mine = total(lax.all_to_all(qkv_mine, "hi", 0, 0))
    mlp_mine = jnp.concatenate([up_mine, down_mine], axis=1)
    mlp_pieces = to_all(mlp_mine)
    attn_pieces = to_all(after(qkv_mine, *mlp_pieces))
    input_grad = collect([*input_first, *input_last])

    dp_count = 2 * hi_count
    if fits:
        pieces = [*mlp_pieces, *attn_pieces]
        piece_specs = [whole_spec(p.shape) for p in pieces]
        squares_shape = (dp_count, 8, 128)
        mlp_square = call(
            square_mlp_body,
            1,
            [SMEM, *piece_specs[:4]],
            whole_spec((8, 128)),
            shape_of((8, 128), F32),
            [],
            2,
            "mlp_squares",
        )(place, *mlp_pieces)
        squares = call(
            square_body,
            1,
            [SMEM, whole_spec((8, 128)), *piece_specs[4:]],
            whole_spec(squares_shape),
            shape_of(squares_shape, F32),
            [],
            1,
            "squares",
        )(place, mlp_square, *attn_pieces)
        squares = lax.all_to_all(squares, ("hi", "lo"), 0, 0)
        states = [attn_w, attn_m, attn_v, mlp_w, mlp_m, mlp_v, vec_w, vec_m, vec_v]
        state_specs = [whole_spec(v.shape) for v in states]
        norm, *new = call(
            adam_body,
            1,
            [SMEM, whole_spec(squares_shape), *piece_specs, *state_specs],
            [whole_spec((1, 1)), *state_specs],
            [shape_of((1, 1), F32), *[shape_of(v.shape, F32) for v in states]],
            [],
            6,
            "adam",
        )(place, squares, *pieces, *states)
        return (output, input_grad, *new, norm.reshape(()))

    vec_sum = attn_pieces[0][shard:].astype(F32) + attn_pieces[2][shard:].astype(F32)
    vec_sum = jnp.where(lo == 0, vec_sum[:, :vec_cols], vec_sum[:, vec_cols : 2 * vec_cols])
    vec_sum = vec_sum[:vec_rows]
    up_at = hidden // 4
    out_at = up_at + width // 4
    up_sum = in_columns([p[:, :up_at] for p in mlp_pieces], y, core)
    out_sum = in_columns([p[:, up_at:out_at] for p in mlp_pieces], y, core)
    down_sum = in_columns([p[:, out_at:] for p in mlp_pieces], y, core)
    qkv_sum = in_columns([p[:shard] for p in attn_pieces], y, core)
    attn_sum = jnp.concatenate([qkv_sum, out_sum], axis=1)
    mlp_sum = jnp.stack([up_sum, down_sum])
    square = jnp.sum(attn_sum * attn_sum) + jnp.sum(mlp_sum * mlp_sum) + jnp.sum(vec_sum * vec_sum)
    squares = lax.all_to_all(jnp.full((dp_count, 8, 128), square), ("hi", "lo"), 0, 0)
    grad_norm = jnp.sqrt(jnp.sum(squares[:, 0, 0]))
    clip_factor = CLIP_NORM / jnp.maximum(grad_norm, CLIP_NORM)
    attn_new = adam_update(
        attn_w, attn_m, attn_v, attn_sum * clip_factor, WEIGHT_DECAY, LEARN_RATE
    )
    mlp_new = adam_update(mlp_w, mlp_m, mlp_v, mlp_sum * clip_factor, WEIGHT_DECAY, LEARN_RATE)
    vec_new = adam_update(vec_w, vec_m, vec_v, vec_sum * clip_factor, 0.0, VEC_RATE)
    return (output, input_grad, *attn_new, *mlp_new, *vec_new, grad_norm)


def solution(mesh):
    dp_count = mesh.shape["dp"]
    seq_count = mesh.shape["seq"]
    fine = jax.sharding.Mesh(
        mesh.devices.reshape(dp_count // 2, 2, seq_count // 2, 2), ("hi", "lo", "y", "core")
    )
    dp = ("hi", "lo")
    seq = ("y", "core")
    acts = P(None, dp, seq, None)
    attn = P(dp, None)
    mlp = P(None, dp, None)
    vec = P(None, dp)
    return jax.shard_map(
        on_device,
        mesh=fine,
        in_specs=(acts, acts, P(None, dp), attn, attn, attn, mlp, mlp, mlp, vec, vec, vec),
        out_specs=(acts, acts, attn, attn, attn, mlp, mlp, mlp, vec, vec, vec, P()),
        check_vma=False,
    )
```

```python
import functools
import math

import jax
import jax.numpy as jnp
from jax import lax
from jax.experimental import pallas as pl
from jax.experimental.pallas import tpu as pltpu
from jax.sharding import PartitionSpec as P

HEADS = 8
ADAM_STEP = 10
CLIP_NORM = 1.0
BETA_ONE = 0.9
BETA_TWO = 0.999
LEARN_RATE = 0.08
VEC_RATE = 0.4
WEIGHT_DECAY = 0.01
ADAM_EPS = 1e-08
NORM_EPS = 1e-05

LIMITS = {"squares": 4, "mlp_squares": 4, "collect": 6, "attend": 8}
LIMIT = 63
F32 = jnp.float32
BF16 = jnp.bfloat16
ANY = pl.BlockSpec(memory_space=pl.ANY)
SMEM = pl.BlockSpec(memory_space=pltpu.SMEM)


def nt_dot(left, right):
    return lax.dot_general(left, right, (((1,), (1,)), ((), ())), preferred_element_type=F32)


def nn_dot(left, right):
    return jnp.dot(left, right, preferred_element_type=F32)


def centered(values):
    center = values - jnp.mean(values, axis=-1, keepdims=True)
    spread = jnp.mean(center * center, axis=-1, keepdims=True)
    scale = lax.rsqrt(spread + NORM_EPS)
    return center * scale, scale


def norm_back(unit, scale, grad):
    mean_grad = jnp.mean(grad, axis=-1, keepdims=True)
    mean_both = jnp.mean(grad * unit, axis=-1, keepdims=True)
    return scale * (grad - mean_grad - unit * mean_both)


def gelu_and_slope(up):
    share = 0.5 + 0.5 * lax.erf(up * (1.0 / math.sqrt(2.0)))
    bell = jnp.exp2(up * up * (-0.5 * math.log2(math.e)))
    return up * share, share + up * (bell * (1.0 / math.sqrt(2.0 * math.pi)))


def load_slots(refs):
    return jnp.concatenate([ref[i] for i in range(refs[0].shape[0]) for ref in refs], axis=0)


def store_slots(refs, value):
    rows, part, _ = refs[0].shape
    for i in range(rows):
        for k, ref in enumerate(refs):
            at = (i * 4 + k) * part
            ref[i] = value[at : at + part]


def placements(pieces, jobs, place, sems):
    lo = place[0]
    core = place[1]
    copies = []
    for i, piece in enumerate(pieces):
        lo_at = lo if i % 2 == 0 else 1 - lo
        core_at = core if i < 2 else 1 - core
        hi_count, rows, _ = piece.shape
        for h in range(hi_count):
            row = pl.multiple_of(((h * 2 + lo_at) * 2 + core_at) * rows, rows)
            for column, width, target, at in jobs:
                copies.append(
                    pltpu.make_async_copy(
                        piece.at[h, :, pl.ds(column, width)],
                        target.at[pl.ds(row, rows), pl.ds(at, width)],
                        sems.at[len(copies)],
                    )
                )
    return copies


def pair_placements(pieces, target, place, sems):
    copies = []
    for i, piece in enumerate(pieces):
        core_at = place[1] if i == 0 else 1 - place[1]
        hi_count, _, rows, _ = piece.shape
        for h in range(hi_count):
            for j in range(2):
                row = pl.multiple_of(((h * 2 + (place[0] ^ j)) * 2 + core_at) * rows, rows)
                copies.append(
                    pltpu.make_async_copy(
                        piece.at[h, j],
                        target.at[pl.ds(row, rows), pl.ds(0, piece.shape[-1])],
                        sems.at[len(copies)],
                    )
                )
    return copies


def head_masks(width):
    lane = lax.broadcasted_iota(jnp.int32, (1, width), 1)
    first = jnp.where(lane < width // 2, 1.0, 0.0)
    return first.astype(BF16), (1.0 - first).astype(BF16)


def fill_bias(place, lengths, row, bias):
    part = bias.shape[0] // 4
    for k in range(4):
        base = (place[2] ^ k) * part
        slot = lax.broadcasted_iota(jnp.int32, (part, bias.shape[1]), 0) + base
        bias[k * part : (k + 1) * part, :] = jnp.where(slot < lengths[row], 0.0, -1e30)


def qkv_body(place, x0, x1, x2, x3, p0, p1, p2, p3, vec, h_out, qkv_out, w_qkv, sems):
    row = pl.program_id(0)
    width = vec.shape[1]
    copies = placements((p0, p1, p2, p3), [(0, 3 * width, w_qkv, 0)], place, sems)

    @pl.when(row == 0)
    def _():
        for copy in copies:
            copy.start()

    x = load_slots((x0, x1, x2, x3)).astype(F32)
    unit, _ = centered(x)
    h = (unit * vec[0:1] + vec[1:2]).astype(BF16)
    h_out[...] = h

    @pl.when(row == 0)
    def _():
        for copy in copies:
            copy.wait()

    q = nn_dot(h, w_qkv[:, :width]).astype(BF16)
    qkv_out[:, :width] = q * jnp.asarray(1.0 / math.sqrt(width // HEADS), BF16)
    qkv_out[:, width:] = nn_dot(h, w_qkv[:, width:]).astype(BF16)


def attend_body(place, lengths, qkv, *refs):
    attn_out, lse_out, bias = refs[-3:]
    row = pl.program_id(0) + place[4]
    width = attn_out.shape[1]
    pair = 2 * (width // HEADS)
    half = pair // 2
    fill_bias(place, lengths, row, bias)
    masks = head_masks(pair)

    def score(h):
        at = (h // 2) * pair
        return nt_dot(qkv[:, width + at : width + at + pair], qkv[:, at : at + pair] * masks[h % 2])

    def soft(h, scores):
        scores = scores + bias[...]
        top = jnp.max(scores, axis=0, keepdims=True)
        grown = jnp.exp(scores - top)
        total = jnp.sum(grown, axis=0, keepdims=True)
        lse_out[0, h : h + 1, :] = top + jnp.log(total)
        return (grown * (1.0 / total)).astype(BF16)

    def value(h, turned, probs):
        return nn_dot(turned[(h % 2) * half : (h % 2 + 1) * half], probs)

    turned = [qkv[:, 2 * width + p * pair : 2 * width + (p + 1) * pair].T for p in range(HEADS // 2)]
    scores = [score(h) for h in range(HEADS)]
    probs = [soft(h, scores[h]) for h in range(HEADS)]
    outs = [value(h, turned[h // 2], probs[h]) for h in range(HEADS)]
    for p in range(HEADS // 2):
        attn_out[:, p * pair : (p + 1) * pair] = jnp.concatenate(outs[2 * p : 2 * p + 2], axis=0).T.astype(BF16)


def write_parts(parts, half, y, column, value, dims):
    hi_count, lo_count, rows = dims
    quarter = value.shape[1]
    value = value.astype(BF16)
    for h in range(hi_count):
        for lo in range(lo_count):
            at = (h * lo_count + lo) * rows
            parts[half, lo, y, h, :, column : column + quarter] = value[at : at + rows]


def send_copies(parts, half, y, keep, send, place, sems):
    mine = half == place[3]
    copies = []
    for i in range(parts.shape[1]):
        for target, wanted in ((keep, mine), (send, jnp.logical_not(mine))):
            lo_count = parts.shape[1]
            copy = pltpu.make_async_copy(
                parts.at[half, i, y],
                target.at[(place[5] ^ i) if lo_count > 1 else 0, place[6] ^ y],
                sems.at[half, i, y],
            )
            copies.append((wanted, copy))
    return copies


def start_all(copies):
    for wanted, copy in copies:
        pl.when(wanted)(copy.start)


def wait_all(copies):
    for wanted, copy in copies:
        pl.when(wanted)(copy.wait)


def mlp_body(
    dims, place, x0, x1, x2, x3, attn, d0, d1, d2, d3, b0, b1, b2, b3, c0, c1, vec,
    o0, o1, o2, o3, dx_out, dattn_out, vec_out, up_keep, up_send, down_keep, down_send,
    w_out, w_up, w_down, h_turned, attn_turned, dy_turned, act_all, dup_all, dao_all,
    up_parts, down_parts, out_sems, up_sems, down_sems, part_sems, more_sems,
):
    row = pl.program_id(0)
    width = vec.shape[1]
    hidden = w_up.shape[1]
    slots = attn.shape[0]
    out_copies = placements((b0, b1, b2, b3), [(0, width, w_out, 0)], place, out_sems)
    split = c0.shape[-1]
    jobs = [(width, hidden, w_up, 0), (width + hidden, hidden - split, w_down, split)]
    up_copies = placements((b0, b1, b2, b3), jobs, place, up_sems)
    down_copies = pair_placements((c0, c1), w_down, place, down_sems)

    def arrived(copies):
        @pl.when(row == 0)
        def _():
            for copy in copies:
                copy.wait()

    @pl.when(row == 0)
    def _():
        vec_out[...] = jnp.zeros_like(vec_out)
        for copy in out_copies + up_copies + down_copies:
            copy.start()

    here = pl.ds(pl.multiple_of(row * slots, slots), slots)
    x = load_slots((x0, x1, x2, x3)).astype(F32)
    dy = load_slots((d0, d1, d2, d3))
    dy_turned[:, here] = dy.T
    attn_turned[:, here] = attn[...].T
    arrived(out_copies)
    x_one = x + (nn_dot(attn[...], w_out[...]) + vec[4:5])
    unit, scale = centered(x_one)
    h = (unit * vec[2:3] + vec[3:4]).astype(BF16)
    h_turned[:, here] = h.T
    arrived(up_copies)
    arrived(down_copies)
    spans = [slice(j * width, (j + 1) * width) for j in range(hidden // width)]
    result = x_one + vec[5:6]
    dh = None
    for j, span in enumerate(spans):
        act, slope = gelu_and_slope(nn_dot(h, w_up[:, span]) + vec[6 + j : 7 + j])
        act = act.astype(BF16)
        act_all[here, span] = act
        dup = (slope * nn_dot(dy, w_down[:, span])).astype(BF16)
        dup_all[here, span] = dup
        vec_out[6 + j : 7 + j] += jnp.sum(dup.astype(F32), axis=0, keepdims=True)
        result = result + nt_dot(act, w_down[:, span])
        part = nt_dot(dup, w_up[:, span])
        dh = part if dh is None else dh + part
    store_slots((o0, o1, o2, o3), result.astype(BF16))
    vec_out[2:3] += jnp.sum(dh * unit, axis=0, keepdims=True)
    vec_out[3:4] += jnp.sum(dh, axis=0, keepdims=True)
    dy_float = dy.astype(F32)
    dx = dy_float + norm_back(unit, scale, dh * vec[2:3])
    dx_out[...] = dx
    dao = dx.astype(BF16)
    dao_all[here, :] = dao
    vec_out[4:5] += jnp.sum(dao.astype(F32), axis=0, keepdims=True)
    vec_out[5:6] += jnp.sum(dy_float, axis=0, keepdims=True)
    dattn_out[...] = nt_dot(dao, w_out[...]).astype(BF16)

    @pl.when(row == pl.num_programs(0) - 1)
    def _():
        quarter = hidden // 4
        small = width // 4
        copies = []
        for half in range(2):
            for y in range(2):
                at = (half * 2 + y) * quarter
                value = nn_dot(h_turned[...], dup_all[:, at : at + quarter])
                write_parts(up_parts, half, y, 0, value, dims)
                value = nn_dot(dy_turned[...], act_all[:, at : at + quarter])
                write_parts(down_parts, half, y, 0, value, dims)
                at = (half * 2 + y) * small
                value = nn_dot(attn_turned[...], dao_all[:, at : at + small])
                write_parts(up_parts, half, y, quarter, value, dims)
                these = send_copies(up_parts, half, y, up_keep, up_send, place, part_sems)
                these += send_copies(down_parts, half, y, down_keep, down_send, place, more_sems)
                start_all(these)
                copies += these
        wait_all(copies)


def back_rows(
    place, lengths, qkv, lse, dattn, xs, dx, pieces, vec, sums, outs, dqkv, vec_out, w_qkv, bias, sems
):
    step = pl.program_id(0)
    width = vec.shape[1]
    slots = qkv.shape[0]
    pair = 2 * (width // HEADS)
    score_scale = 1.0 / math.sqrt(width // HEADS)
    copies = placements(pieces, [(0, 3 * width, w_qkv, 0)], place, sems)

    @pl.when(step == 0)
    def _():
        vec_out[...] = sums[...]
        for copy in copies:
            copy.start()

    fill_bias(place, lengths, step + place[4], bias)
    masks = head_masks(pair)
    half = pair // 2
    pairs = range(HEADS // 2)

    def part(base, p):
        return qkv[:, base + p * pair : base + (p + 1) * pair]

    grads = [dattn[:, p * pair : (p + 1) * pair] for p in pairs]
    qs = [part(0, h // 2) * masks[h % 2] for h in range(HEADS)]
    gs = [grads[h // 2] * masks[h % 2] for h in range(HEADS)]
    k_turned = [part(width, p).T for p in pairs]
    scores = [nt_dot(part(width, h // 2), qs[h]) for h in range(HEADS)]
    dprobs = [nt_dot(part(2 * width, h // 2), gs[h]) for h in range(HEADS)]
    probs_low, ds = [], []
    for h in range(HEADS):
        probs = jnp.exp(scores[h] + bias[...] - lse[0, h : h + 1, :])
        inner = jnp.sum(probs * dprobs[h], axis=0, keepdims=True)
        ds.append((probs * (dprobs[h] - inner)).astype(BF16))
        probs_low.append(probs.astype(BF16))
    dqs = [nn_dot(k_turned[h // 2][(h % 2) * half : (h % 2 + 1) * half], ds[h]) for h in range(HEADS)]
    for p in pairs:
        two = slice(2 * p, 2 * p + 2)
        queries, given = jnp.concatenate(qs[two], axis=0), jnp.concatenate(gs[two], axis=0)
        dk = nn_dot(jnp.concatenate(ds[two], axis=1), queries)
        dv = nn_dot(jnp.concatenate(probs_low[two], axis=1), given)
        dq = jnp.concatenate(dqs[two], axis=0).T * score_scale
        dqkv[:, p * pair : (p + 1) * pair] = dq.astype(BF16)
        dqkv[:, width + p * pair : width + (p + 1) * pair] = dk.astype(BF16)
        dqkv[:, 2 * width + p * pair : 2 * width + (p + 1) * pair] = dv.astype(BF16)

    @pl.when(step == 0)
    def _():
        for copy in copies:
            copy.wait()

    dh = nt_dot(dqkv[...], w_qkv[...])
    x = load_slots(xs).astype(F32)
    unit, scale = centered(x)
    vec_out[0:1] += jnp.sum(dh * unit, axis=0, keepdims=True)
    vec_out[1:2] += jnp.sum(dh, axis=0, keepdims=True)
    grad = (dx[...] + norm_back(unit, scale, dh * vec[0:1])).astype(BF16)
    store_slots(outs, grad)


def back_first_body(
    place, lengths, qkv, lse, dattn, x0, x1, x2, x3, dx, p0, p1, p2, p3, vec, sums,
    o0, o1, o2, o3, dqkv_out, vec_out, w_qkv, bias, sems,
):
    back_rows(
        place, lengths, qkv, lse, dattn, (x0, x1, x2, x3), dx, (p0, p1, p2, p3), vec, sums,
        (o0, o1, o2, o3), dqkv_out, vec_out, w_qkv, bias, sems,
    )


def back_last_body(
    dims, place, lengths, qkv, lse, dattn, x0, x1, x2, x3, dx, p0, p1, p2, p3, vec, sums,
    h_one, before,
    o0, o1, o2, o3, vec_out, keep, send, dqkv, w_qkv, bias, h_turned, parts, sems, out_sems,
):
    step = pl.program_id(0)
    slots = qkv.shape[0]
    here = pl.ds(pl.multiple_of(step * slots, slots), slots)
    back_rows(
        place, lengths, qkv, lse, dattn, (x0, x1, x2, x3), dx, (p0, p1, p2, p3), vec, sums,
        (o0, o1, o2, o3), dqkv.at[here], vec_out, w_qkv, bias, sems,
    )

    @pl.when(step == pl.num_programs(0) - 1)
    def _():
        count = before.shape[0]
        h_turned[...] = h_one[...].T
        quarter = before.shape[1] // 4
        copies = []
        for half in range(2):
            for y in range(2):
                at = (half * 2 + y) * quarter
                value = nn_dot(h_turned[:, :count], before[:, at : at + quarter])
                value = value + nn_dot(h_turned[:, count:], dqkv[:, at : at + quarter])
                write_parts(parts, half, y, 0, value, dims)
                these = send_copies(parts, half, y, keep, send, place, out_sems)
                start_all(these)
                copies += these
        wait_all(copies)


def add_mlp_body(keep, got, down_keep, down_got, *outs):
    for k in range(4):
        outs[k][...] = (keep[k].astype(F32) + got[k].astype(F32)).astype(BF16)
        outs[4][:, k] = (down_keep[k].astype(F32) + down_got[k].astype(F32)).astype(BF16)


def add_qkv_body(keep, got, vec, *outs):
    rows = keep.shape[2]
    sums = vec[...]
    for k, out in enumerate(outs):
        out[:, :rows, :] = (keep[k].astype(F32) + got[k].astype(F32)).astype(BF16)
        out[:, rows:, :] = jnp.zeros((out.shape[0], 16, out.shape[2]), BF16)
        lanes = sums.shape[1] // out.shape[0]
        for h in range(out.shape[0]):
            out[h, rows:, :lanes] = sums[:, h * lanes : (h + 1) * lanes].astype(BF16)


def collect_body(place, *refs):
    out = refs[-1]
    at = 0
    for i in range(0, len(refs) - 1, 4):
        count = refs[i].shape[0]
        for k in range(4):
            out[place[2] ^ k, at : at + count] = refs[i + k][...]
        at += count


def in_order(values, place):
    core, y = place[3], place[7]
    near = (jnp.where(y == 0, values[0], values[1]), jnp.where(y == 0, values[1], values[0]))
    far = (jnp.where(y == 0, values[2], values[3]), jnp.where(y == 0, values[3], values[2]))
    first = (jnp.where(core == 0, near[0], far[0]), jnp.where(core == 0, near[1], far[1]))
    second = (jnp.where(core == 0, far[0], near[0]), jnp.where(core == 0, far[1], near[1]))
    return (*first, *second)


def vec_sums(a0, a2, place, shard):
    lanes = 128
    own = a0[shard:, :lanes].astype(F32)
    far = a2[shard:, :lanes].astype(F32)
    both = own + far
    lane = lax.broadcasted_iota(jnp.int32, both.shape, 1) // (lanes // 2)
    return jnp.where(lane == place[8], both, 0.0)


def square_mlp_body(place, m0, m1, m2, m3, out):
    values = []
    for mlp in (m0, m1, m2, m3):
        value = mlp[...].astype(F32)
        values.append(jnp.sum(value * value))
    first, second, third, fourth = in_order(values, place)
    out[...] = jnp.full(out.shape, (first + second) + (third + fourth), F32)


def square_body(place, before, a0, a1, a2, a3, out):
    shard = a0.shape[0] - 16
    values = []
    for attn in (a0, a1, a2, a3):
        value = attn[:shard].astype(F32)
        values.append(jnp.sum(value * value))
    vec = vec_sums(a0, a2, place, shard)
    first, second, third, fourth = in_order(values, place)
    value = ((first + second) + (third + fourth)) + jnp.sum(vec * vec)
    total_value = before[...] + value
    for d in range(out.shape[0]):
        out[d] = total_value


def adam_parts(weight, moment, second, grad, decay, rate):
    moment_new = BETA_ONE * moment + (1.0 - BETA_ONE) * grad
    second_new = BETA_TWO * second + (1.0 - BETA_TWO) * grad * grad
    first_hat = moment_new * (1.0 / (1.0 - BETA_ONE**ADAM_STEP))
    second_hat = second_new * (1.0 / (1.0 - BETA_TWO**ADAM_STEP))
    step = first_hat / (jnp.sqrt(second_hat) + ADAM_EPS)
    return weight - rate * (step + decay * weight), moment_new, second_new


def adam_body(
    place, squares, m0, m1, m2, m3, a0, a1, a2, a3,
    attn_w, attn_m, attn_v, mlp_w, mlp_m, mlp_v, vec_w, vec_m, vec_v,
    norm_out, attn_wo, attn_mo, attn_vo, mlp_wo, mlp_mo, mlp_vo, vec_wo, vec_mo, vec_vo,
):
    shard = m0.shape[0]
    hidden = mlp_w.shape[2]
    quarter = hidden // 4
    wide = a0.shape[1]
    small = m0.shape[1] - 2 * quarter
    value = squares[0]
    for d in range(1, squares.shape[0]):
        value = value + squares[d]
    norm = jnp.sqrt(value)
    norm_out[...] = norm[0:1, 0:1]
    factor = (CLIP_NORM / jnp.maximum(norm, CLIP_NORM))[0:1, 0:1]
    rows, cols = vec_w.shape
    vec = vec_sums(a0, a2, place, shard)
    grad = (vec[:rows, :cols] + vec[:rows, cols : 2 * cols]) * factor
    parts = adam_parts(vec_w[...], vec_m[...], vec_v[...], grad, 0.0, VEC_RATE)
    for new, new_value in zip((vec_wo, vec_mo, vec_vo), parts):
        new[...] = new_value
    core, y = place[3], place[7]
    olds = (attn_w, attn_m, attn_v)
    news = (attn_wo, attn_mo, attn_vo)
    mlp_olds = (mlp_w, mlp_m, mlp_v)
    mlp_news = (mlp_wo, mlp_mo, mlp_vo)
    for i, (mlp, attn) in enumerate(((m0, a0), (m1, a1), (m2, a2), (m3, a3))):
        side = (core if i < 2 else 1 - core) * 2 + (y if i % 2 == 0 else 1 - y)

        def columns(base, size, side=side):
            return pl.ds(pl.multiple_of(base + side * size, 128), size)

        at = columns(0, wide)
        grad = attn[:shard].astype(F32) * factor
        for new, new_value in zip(news, adam_parts(*[o[:, at] for o in olds], grad, WEIGHT_DECAY, LEARN_RATE)):
            new[:, at] = new_value
        at = columns(4 * wide, small)
        grad = mlp[:, quarter : quarter + small].astype(F32) * factor
        for new, new_value in zip(news, adam_parts(*[o[:, at] for o in olds], grad, WEIGHT_DECAY, LEARN_RATE)):
            new[:, at] = new_value
        at = columns(0, quarter)
        for j, start in ((0, 0), (1, quarter + small)):
            grad = mlp[:, start : start + quarter].astype(F32) * factor
            parts = adam_parts(*[o[j, :, at] for o in mlp_olds], grad, WEIGHT_DECAY, LEARN_RATE)
            for new, new_value in zip(mlp_news, parts):
                new[j, :, at] = new_value


def shape_of(dims, dtype):
    return jax.ShapeDtypeStruct(dims, dtype)


def rows_spec(rows, cols):
    return pl.BlockSpec((rows, cols), lambda r: (r, 0))


def whole_spec(shape):
    return pl.BlockSpec(shape, lambda r: (0,) * len(shape))


def call(body, grid, in_specs, out_specs, out_shape, scratch, cost, name, aliases=None):
    return pl.pallas_call(
        body,
        grid=(grid,),
        in_specs=in_specs,
        out_specs=out_specs,
        out_shape=out_shape,
        scratch_shapes=scratch,
        input_output_aliases=aliases or {},
        compiler_params=pltpu.CompilerParams(
            vmem_limit_bytes=LIMITS.get(name, LIMIT) * 2**20,
            dimension_semantics=("arbitrary",),
        ),
        cost_estimate=pl.CostEstimate(
            flops=int(cost * 5e8), bytes_accessed=int(cost * 1e6), transcendentals=0
        ),
        name=name,
    )


def swap(value, axis):
    return lax.ppermute(value, axis, [(0, 1), (1, 0)])


def ordered(own, other, index, axis):
    first = jnp.where(index == 0, own, other)
    second = jnp.where(index == 0, other, own)
    return jnp.stack([first, second], axis)


def from_seq(pieces):
    moved = [pieces[0]]
    for k in range(1, 4):
        moved.append(lax.ppermute(pieces[k], ("y", "core"), [(j, j ^ k) for j in range(4)]))
    return moved


def spread_hi(half):
    hi_count = lax.axis_size("hi")
    spread = jnp.broadcast_to(half[None], (hi_count, *half.shape))
    return lax.all_to_all(spread, "hi", 0, 0)


def share(own):
    other = swap(own, "lo")
    return [own, other, swap(own, "core"), swap(other, "core")]


def settle(pieces, lo, core, groups=4):
    near = ordered(pieces[0], pieces[1], lo, 1)
    far = ordered(pieces[2], pieces[3], lo, 1)
    whole = ordered(near, far, core, 2)
    cols = whole.shape[-1]
    whole = whole.reshape(groups, 2, 2, -1, cols)
    return [whole[:, 0, 0], whole[:, 1, 0], whole[:, 0, 1], whole[:, 1, 1]]


def add_pair(keep, got):
    return (keep.astype(F32) + got.astype(F32)).astype(BF16)


def spread_plane(part):
    part = part.reshape(4, *part.shape[2:])
    return lax.all_to_all(part, ("lo", "y"), 0, 0)


def total(part):
    return jnp.sum(part.astype(F32), axis=0).astype(BF16)


def to_all(mine):
    return [mine] + [
        lax.ppermute(mine, ("y", "core"), [(j, j ^ k) for j in range(4)]) for k in (2, 1, 3)
    ]


def after(value, *others):
    return lax.optimization_barrier((value, *others))[0]


def in_columns(pieces, y, core):
    near = ordered(pieces[0], pieces[1], y, 1)
    far = ordered(pieces[2], pieces[3], y, 1)
    both = ordered(near, far, core, 1)
    return both.reshape(both.shape[0], -1).astype(F32)


def adam_update(weight, moment, second, grad, decay, rate):
    moment_new = BETA_ONE * moment + (1.0 - BETA_ONE) * grad
    second_new = BETA_TWO * second + (1.0 - BETA_TWO) * grad * grad
    first_hat = moment_new / (1.0 - BETA_ONE**ADAM_STEP)
    second_hat = second_new / (1.0 - BETA_TWO**ADAM_STEP)
    weight_new = weight - rate * (first_hat / (jnp.sqrt(second_hat) + ADAM_EPS) + decay * weight)
    return (weight_new, moment_new, second_new)


def on_device(
    tokens, cotangent, lengths, attn_w, attn_m, attn_v, mlp_w, mlp_m, mlp_v, vec_w, vec_m, vec_v
):
    lo = lax.axis_index("lo")
    y = lax.axis_index("y")
    core = lax.axis_index("core")
    hi_count = lax.axis_size("hi")
    me = y * 2 + core
    micro_count, row_count, part, width = tokens.shape
    hidden = mlp_w.shape[2]
    shard = attn_w.shape[0]
    slots = 4 * part
    rows = micro_count * row_count // 4
    count = rows * slots
    vec_rows, vec_cols = vec_w.shape
    half_rows = shard // 2
    fits = half_rows % 16 == 0

    flat_tokens = tokens.reshape(4, rows, part, width)
    flat_cot = cotangent.reshape(4, rows, part, width)

    def pick(stack, k):
        return lax.dynamic_index_in_dim(stack, me ^ k, 0, keepdims=False)

    def half_of(value):
        return lax.dynamic_slice_in_dim(value, core * half_rows, half_rows, 0)

    xs = from_seq([pick(flat_tokens, k) for k in range(4)])
    lanes = 128
    ride = jnp.pad(vec_w.reshape(-1), (0, half_rows * lanes - vec_w.size)).reshape(half_rows, lanes)
    first_half = jnp.concatenate([half_of(attn_w[:, : 3 * width]), ride], axis=1).astype(BF16)
    qkv_own = spread_hi(first_half)
    split = 3 * hidden // 4
    up_half = jnp.concatenate(
        [half_of(attn_w[:, 3 * width :]), half_of(mlp_w[0]), half_of(mlp_w[1, :, split:])], axis=1
    )
    up_own = spread_hi(after(up_half.astype(BF16), qkv_own))
    qkv_own, xs[3] = lax.optimization_barrier((qkv_own, xs[3]))
    qkv_other = swap(qkv_own, "lo")
    qkv_pieces = [qkv_own, qkv_other, swap(qkv_own, "core"), swap(qkv_other, "core")]
    vec_all = ordered(qkv_pieces[0][:, :, 3 * width :], qkv_pieces[1][:, :, 3 * width :], lo, 1)
    vec_all = vec_all.reshape(2 * hi_count, -1)[:, : vec_w.size].reshape(-1, vec_rows, vec_cols)
    vec_all = vec_all.transpose(1, 0, 2).reshape(vec_rows, width)
    vec_float = jnp.pad(vec_all.astype(F32), ((0, 16 - vec_rows), (0, 0)))

    if fits:
        places = [lo, core, me, core, 0 * lo, lo, y, y, lo]
        dims = (hi_count, 2, shard)
    else:
        qkv_pieces = settle(qkv_pieces, lo, core)
        places = [0 * lo, 0 * lo, me, core, 0 * lo, 0 * lo, 0 * lo, y, lo]
        dims = (1, 1, width)
    place = jnp.stack(places).astype(jnp.int32)
    later = place.at[4].set(rows // 2)
    row_lengths = lax.dynamic_slice_in_dim(lengths.reshape(-1), me * rows, rows)

    vec_spec = whole_spec((16, width))
    lse_spec = pl.BlockSpec((1, HEADS, slots), lambda r: (r, 0, 0))
    group = 2 if rows % 2 == 0 else 1
    slot_spec = pl.BlockSpec((group, part, width), lambda r: (r, 0, 0))
    narrow = rows_spec(group * slots, width)
    wide_qkv = rows_spec(group * slots, 3 * width)
    triple = rows_spec(slots, 3 * width)
    n_piece = 4 * qkv_pieces[0].shape[0]
    dma = pltpu.SemaphoreType.DMA
    h_one, qkv = call(
        qkv_body,
        rows // group,
        [SMEM, *[slot_spec] * 4, *[ANY] * 4, vec_spec],
        [narrow, wide_qkv],
        [shape_of((count, width), BF16), shape_of((count, 3 * width), BF16)],
        [pltpu.VMEM((width, 3 * width), BF16), dma((n_piece,))],
        7,
        "qkv",
    )(place, *xs, *qkv_pieces, vec_float)

    down_half = after(half_of(mlp_w[1, :, :split]).astype(BF16), qkv_other)
    down_pair = jnp.stack(lax.optimization_barrier((down_half, swap(down_half, "lo"), h_one))[:2])
    down_own = spread_hi(after(down_pair, up_own))
    cot = after(flat_cot, qkv_other)
    dys = from_seq([pick(cot, k) for k in range(4)])
    qkv, up_own = lax.optimization_barrier((qkv, up_own))
    up_other = swap(up_own, "lo")

    def half_spec(block, base):
        zeros = (0,) * (len(block) - 1)
        return pl.BlockSpec(block, lambda r: (r + base, *zeros))

    def attend(qkv, base, steps, before):
        return call(
            attend_body,
            steps,
            [SMEM, SMEM, half_spec((slots, 3 * width), base), *[ANY] * len(before)],
            [half_spec((slots, width), base), half_spec((1, HEADS, slots), base)],
            [shape_of((count, width), BF16), shape_of((rows, HEADS, slots), F32)],
            [pltpu.VMEM((slots, slots), F32)],
            4 * steps,
            "attend",
            {3: 0, 4: 1} if before else None,
        )(place.at[4].set(base), row_lengths, qkv, *before)

    up_far = swap(up_own, "core")
    attn, lse = attend(qkv, 0, rows - 1, [])
    up_other, attn, lse, *dys = lax.optimization_barrier(
        (up_other, attn, lse, *dys)
    )
    attn, lse = attend(qkv, rows - 1, 1, [attn, lse])
    up_pieces = [up_own, up_other, up_far, swap(up_other, "core")]
    down_own = after(down_own, attn)
    down_far = swap(down_own, "core")
    down_pieces = [down_own, down_far]
    if not fits:
        up_pieces = settle(up_pieces, lo, core)
        split = settle([p[:, j] for p in down_pieces for j in range(2)], lo, core)
        down_pieces = [jnp.stack(split[:2], axis=1), jnp.stack(split[2:], axis=1)]
    n_down = 4 * down_pieces[0].shape[0]

    def parts_shape(quarter):
        return (dims[1], 2, dims[0], dims[2], quarter)

    def in_dp_order(value):
        if fits:
            return value
        value = value.reshape(2, hi_count, 2, shard, value.shape[-1])
        return value.transpose(2, 0, 1, 3, 4)

    turned = pltpu.VMEM((width, count), BF16)
    shape = parts_shape(hidden // 4 + width // 4)
    down_shape = parts_shape(hidden // 4)
    outs = call(
        functools.partial(mlp_body, dims),
        rows // group,
        [SMEM, *[slot_spec] * 4, narrow, *[slot_spec] * 4, *[ANY] * 6, vec_spec],
        [*[slot_spec] * 4, narrow, narrow, vec_spec, *[ANY] * 4],
        [
            *[shape_of((rows, part, width), BF16)] * 4,
            shape_of((count, width), F32),
            shape_of((count, width), BF16),
            shape_of((16, width), F32),
            *[shape_of(shape, BF16)] * 2,
            *[shape_of(down_shape, BF16)] * 2,
        ],
        [
            pltpu.VMEM((width, width), BF16),
            pltpu.VMEM((width, hidden), BF16),
            pltpu.VMEM((width, hidden), BF16),
            turned,
            turned,
            turned,
            pltpu.VMEM((count, hidden), BF16),
            pltpu.VMEM((count, hidden), BF16),
            pltpu.VMEM((count, width), BF16),
            pltpu.VMEM((2, *shape), BF16),
            pltpu.VMEM((2, *down_shape), BF16),
            dma((n_piece,)),
            dma((2 * n_piece,)),
            dma((n_down,)),
            dma((2, dims[1], 2)),
            dma((2, dims[1], 2)),
        ],
        24,
        "mlp",
    )(place, *xs, attn, *dys, *up_pieces, *down_pieces, vec_float)
    results, (dx, dattn, vec_mlp, up_keep, up_send, down_keep, down_send) = outs[:4], outs[4:]
    up_got = swap(up_send, "core")
    down_got = swap(down_send, "core")

    def collect(parts):
        out = (4, rows, part, width)
        return call(
            collect_body,
            1,
            [SMEM, *[whole_spec(p.shape) for p in parts]],
            whole_spec(out),
            shape_of(out, BF16),
            [],
            2,
            "collect",
        )(place, *parts).reshape(tokens.shape)

    results = from_seq(results)
    lead = 2
    lead_count = lead * slots
    back_args = [lse, dattn, *xs, dx]
    weights = [*qkv_pieces, vec_float]

    def back_specs(base):
        return [
            SMEM,
            SMEM,
            half_spec((slots, 3 * width), base),
            half_spec((1, HEADS, slots), base),
            half_spec((slots, width), base),
            *[half_spec((1, part, width), base)] * 4,
            half_spec((slots, width), base),
            *[ANY] * 4,
            vec_spec,
            vec_spec,
        ]

    first_shapes = [shape_of((lead, part, width), BF16)] * 4
    last_shapes = [shape_of((rows - lead, part, width), BF16)] * 4
    back_scratch = [pltpu.VMEM((width, 3 * width), BF16), pltpu.VMEM((slots, slots), F32)]
    outs = call(
        back_first_body,
        lead,
        back_specs(0),
        [*[half_spec((1, part, width), 0)] * 4, triple, vec_spec],
        [*first_shapes, shape_of((lead_count, 3 * width), BF16), shape_of((16, width), F32)],
        [*back_scratch, dma((n_piece,))],
        11,
        "back_first",
    )(place, row_lengths, after(qkv, up_send, down_send), *back_args, *weights, vec_mlp)
    input_first, (grad_first, vec_first) = outs[:4], outs[4:]

    def add_call(body, args, outs):
        args = [a.reshape(4, *a.shape[2:]) if a.ndim > 2 else a for a in args]
        return call(
            body,
            1,
            [whole_spec(a.shape) for a in args],
            [whole_spec(o.shape) for o in outs],
            outs,
            [],
            3,
            "add",
        )(*args)

    def plane_sum(parts):
        moved = [parts[0]]
        for k in (2, 1, 3):
            perm = [(j, j ^ k) for j in range(4)]
            moved.append(lax.ppermute(parts[k], ("lo", "y"), perm))
        return moved

    def add_moved(moved):
        value = (moved[0].astype(F32) + moved[1].astype(F32)) + moved[2].astype(F32)
        return (value + moved[3].astype(F32)).astype(BF16)

    def plane_total(keep, got, extra):
        part = in_dp_order(add_pair(keep, got))
        if extra is not None:
            part = jnp.concatenate([part, extra], axis=3)
        return total(spread_plane(part))

    input_first = from_seq(input_first)
    qkv_last = qkv
    output = collect(results)
    if fits:
        args = [up_keep, up_got, down_keep, down_got]
        args = lax.optimization_barrier((*args, grad_first, *results[:3]))[:4]
        piece = shape_of(up_keep.shape[2:], BF16)
        by_hi = shape_of((hi_count, 4, *down_keep.shape[3:]), BF16)
        *parts, down_part = add_call(add_mlp_body, args, [*[piece] * 4, by_hi])
        qkv_last = after(qkv, *parts, down_part)
        up_moved = plane_sum(parts)
        down_part = total(lax.all_to_all(down_part, "hi", 0, 0))
    quarter = 3 * width // 4
    shape = parts_shape(quarter)
    outs = call(
        functools.partial(back_last_body, dims),
        rows - lead,
        [
            *back_specs(lead),
            whole_spec((count, width)),
            whole_spec((lead_count, 3 * width)),
        ],
        [*[half_spec((1, part, width), 0)] * 4, vec_spec, ANY, ANY],
        [*last_shapes, shape_of((16, width), F32), shape_of(shape, BF16), shape_of(shape, BF16)],
        [
            pltpu.VMEM((count - lead_count, 3 * width), BF16),
            *back_scratch,
            turned,
            pltpu.VMEM((2, *shape), BF16),
            dma((n_piece,)),
            dma((2, dims[1], 2)),
        ],
        13,
        "back_last",
    )(place.at[4].set(lead), row_lengths, qkv_last, *back_args, *weights, vec_first, h_one, grad_first)
    input_last, (vec_last, qkv_keep, qkv_send) = outs[:4], outs[4:]
    if fits:
        qkv_send = after(qkv_send, *up_moved, *input_first)
    qkv_got = swap(qkv_send, "core")

    input_last = from_seq(input_last)
    if fits:
        _, _, _, more_rows, more_cols = qkv_keep.shape
        piece = shape_of((hi_count, more_rows + 16, more_cols), BF16)
        parts = add_call(add_qkv_body, [qkv_keep, qkv_got, vec_last], [piece] * 4)
        qkv_moved = plane_sum(parts)
        down_moved = plane_sum([down_part[k] for k in range(4)])
        up_plane = after(add_moved(up_moved), *parts)
        up_mine = total(lax.all_to_all(up_plane, "hi", 0, 0))
        down_mine = add_moved(down_moved)
        qkv_moved = lax.optimization_barrier((*qkv_moved, *input_last))[:4]
        qkv_plane = after(add_moved(qkv_moved), up_mine)
        qkv_mine = total(lax.all_to_all(qkv_plane, "hi", 0, 0))
    else:
        vec_total = vec_last.reshape(16, hi_count, 2, vec_cols)
        vec_total = vec_total.transpose(1, 0, 2, 3).reshape(1, 1, hi_count, 16, 2 * vec_cols)
        vec_total = jnp.pad(vec_total.astype(BF16), ((0, 0),) * 4 + ((0, quarter - 2 * vec_cols),))
        vec_total = jnp.broadcast_to(vec_total, (2, 2, *vec_total.shape[2:]))
        up_mine = total(lax.all_to_all(plane_total(up_keep, up_got, None), "hi", 0, 0))
        down_mine = total(lax.all_to_all(plane_total(down_keep, down_got, None), "hi", 0, 0))
        qkv_mine = plane_total(qkv_keep, qkv_got, vec_total)
        qkv_mine = total(lax.all_to_all(qkv_mine, "hi", 0, 0))
    mlp_mine = jnp.concatenate([up_mine, down_mine], axis=1)
    mlp_side = swap(mlp_mine, "y")
    mlp_pieces = [mlp_mine, mlp_side, swap(mlp_mine, "core"), swap(mlp_side, "core")]
    attn_pieces = to_all(after(qkv_mine, *mlp_pieces))
    input_grad = collect([*input_first, *input_last])

    dp_count = 2 * hi_count
    if fits:
        pieces = [*mlp_pieces, *attn_pieces]
        piece_specs = [whole_spec(p.shape) for p in pieces]
        squares_shape = (dp_count, 8, 128)
        mlp_square = call(
            square_mlp_body,
            1,
            [SMEM, *piece_specs[:4]],
            whole_spec((8, 128)),
            shape_of((8, 128), F32),
            [],
            2,
            "mlp_squares",
        )(place, *mlp_pieces)
        squares = call(
            square_body,
            1,
            [SMEM, whole_spec((8, 128)), *piece_specs[4:]],
            whole_spec(squares_shape),
            shape_of(squares_shape, F32),
            [],
            1,
            "squares",
        )(place, mlp_square, *attn_pieces)
        squares = lax.all_to_all(squares, ("hi", "lo"), 0, 0)
        states = [attn_w, attn_m, attn_v, mlp_w, mlp_m, mlp_v, vec_w, vec_m, vec_v]
        state_specs = [whole_spec(v.shape) for v in states]
        norm, *new = call(
            adam_body,
            1,
            [SMEM, whole_spec(squares_shape), *piece_specs, *state_specs],
            [whole_spec((1, 1)), *state_specs],
            [shape_of((1, 1), F32), *[shape_of(v.shape, F32) for v in states]],
            [],
            6,
            "adam",
        )(place, squares, *pieces, *states)
        return (output, input_grad, *new, norm.reshape(()))

    vec_sum = attn_pieces[0][shard:].astype(F32) + attn_pieces[2][shard:].astype(F32)
    vec_sum = jnp.where(lo == 0, vec_sum[:, :vec_cols], vec_sum[:, vec_cols : 2 * vec_cols])
    vec_sum = vec_sum[:vec_rows]
    up_at = hidden // 4
    out_at = up_at + width // 4
    up_sum = in_columns([p[:, :up_at] for p in mlp_pieces], y, core)
    out_sum = in_columns([p[:, up_at:out_at] for p in mlp_pieces], y, core)
    down_sum = in_columns([p[:, out_at:] for p in mlp_pieces], y, core)
    qkv_sum = in_columns([p[:shard] for p in attn_pieces], y, core)
    attn_sum = jnp.concatenate([qkv_sum, out_sum], axis=1)
    mlp_sum = jnp.stack([up_sum, down_sum])
    square = jnp.sum(attn_sum * attn_sum) + jnp.sum(mlp_sum * mlp_sum) + jnp.sum(vec_sum * vec_sum)
    squares = lax.all_to_all(jnp.full((dp_count, 8, 128), square), ("hi", "lo"), 0, 0)
    grad_norm = jnp.sqrt(jnp.sum(squares[:, 0, 0]))
    clip_factor = CLIP_NORM / jnp.maximum(grad_norm, CLIP_NORM)
    attn_new = adam_update(
        attn_w, attn_m, attn_v, attn_sum * clip_factor, WEIGHT_DECAY, LEARN_RATE
    )
    mlp_new = adam_update(mlp_w, mlp_m, mlp_v, mlp_sum * clip_factor, WEIGHT_DECAY, LEARN_RATE)
    vec_new = adam_update(vec_w, vec_m, vec_v, vec_sum * clip_factor, 0.0, VEC_RATE)
    return (output, input_grad, *attn_new, *mlp_new, *vec_new, grad_norm)


def solution(mesh):
    dp_count = mesh.shape["dp"]
    seq_count = mesh.shape["seq"]
    fine = jax.sharding.Mesh(
        mesh.devices.reshape(dp_count // 2, 2, seq_count // 2, 2), ("hi", "lo", "y", "core")
    )
    dp = ("hi", "lo")
    seq = ("y", "core")
    acts = P(None, dp, seq, None)
    attn = P(dp, None)
    mlp = P(None, dp, None)
    vec = P(None, dp)
    return jax.shard_map(
        on_device,
        mesh=fine,
        in_specs=(acts, acts, P(None, dp), attn, attn, attn, mlp, mlp, mlp, vec, vec, vec),
        out_specs=(acts, acts, attn, attn, attn, mlp, mlp, mlp, vec, vec, vec, P()),
        check_vma=False,
    )
```
